32 devices in a mesh: tm: 8 (over z, x), chan: 4 (over y, core).
Axes of the slice: x: 2, y: 2, z: 4, core: 2. Of those that a mesh axis runs over, the one named last changes fastest.
Arguments:
- data: bfloat16 [384, 16384], P('chan', 'tm'), may hold values from 0.049804688 to 2
- motifs: bfloat16 [384, 2048], P('chan', 'tm'), may hold values from 9.727478e-05 to 0.001953125
- loadings: float32 [64, 16384], P(None, 'tm'), as said below
Outputs:
- factors_now: float32 [64, 16384], P(None, 'tm')
The draws below stay inside these ranges and needn't reach their ends.
Inputs may be any that keep to these rules, and one draw needn't show every extreme that they name: `loadings`: every entry is positive.
All inputs are finite; a program needn't handle non-finite values.
Results may differ from the reference program's by a relative error of at most 0.0003.
Values may be sent and summed in bfloat16 or wider, within the bound.
No kernel may reach another device: no remote copies, remote signals or barrier semaphores. Data moves between devices by JAX's collectives and lax.ppermute only.
A program may use at most 128 MiB of HBM per device.

```python
import math
import jax
import jax.numpy as jnp
from jax import lax

CHANNELS = 384
FACTORS = 64
LAGS = 32
ITERS = 3
TOTAL = 16384


def draw_loadings(key, part):
    first_key, second_key = jax.random.split(jax.random.fold_in(key, 7))
    ramp = 1.0 + 2.0 * jnp.arange(TOTAL, dtype=jnp.float32) / (TOTAL - 1)
    base = jax.random.uniform(first_key, (FACTORS, TOTAL), jnp.float32, 0.2, 1.0)
    scales = jnp.exp(jax.random.uniform(second_key, (FACTORS, 1), jnp.float32) * jnp.log(4.0))
    return (base * scales * ramp[None, :]).astype(jnp.float32)


def levels(stream_key, extent, cuts, least, top_value):
    def one(position, shards_of):
        heights = jax.random.uniform(jax.random.fold_in(jax.random.fold_in(stream_key, 6), position), (shards_of,), jnp.float32, least / len(cuts), top_value / len(cuts))
        return jnp.repeat(jnp.exp(heights), extent[position] // shards_of).reshape((-1,) + (1,) * (len(extent) - position - 1))

    level = one(*cuts[0])
    for cut in cuts[1:]:
        level = level * one(*cut)
    return level


def setup_inputs(seed: int = 0) -> dict:
    key_of = jax.random.split(jax.random.key(seed), 4)
    return {
        "data": jnp.clip(jnp.exp(math.log(2.0) - 3.6927934 * jax.random.uniform(key_of[0], (CHANNELS, TOTAL), jnp.float32) ** levels(key_of[0], (CHANNELS, TOTAL), ((0, 4), (1, 8)), -0.2, 0.2)), 0.049804688, 2.0).astype(jnp.bfloat16),
        "motifs": jnp.clip(jnp.exp(math.log(0.001953125) - 2.9996462 * jax.random.uniform(key_of[1], (CHANNELS, FACTORS * LAGS), jnp.float32) ** levels(key_of[1], (CHANNELS, FACTORS * LAGS), ((0, 4), (1, 8)), -0.2, 0.2)), 9.72747802734375e-05, 0.001953125).astype(jnp.bfloat16),
        "loadings": draw_loadings(jax.random.fold_in(key_of[3], 71), 0),
    }


penalty_weight = 0.2


def shift_back(field, offset):
    if offset == 0:
        return field
    return jnp.concatenate([field[:, offset:], jnp.zeros((field.shape[0], offset), field.dtype)], 1)


def shift_fore(field, offset):
    if offset == 0:
        return field
    cols = field.shape[1]
    return jnp.concatenate([jnp.zeros((field.shape[0], offset), field.dtype), field[:, :cols - offset]], 1)


def reference(data, motifs, loadings):
    signal = data.astype(jnp.float32)
    motif_all = motifs.astype(jnp.float32).reshape(CHANNELS, FACTORS, LAGS)
    length_all = signal.shape[1]
    hp = lax.Precision.HIGHEST

    def correlate(field):
        result = jnp.zeros((FACTORS, length_all), jnp.float32)
        for offset in range(LAGS):
            result = result + jnp.dot(motif_all[:, :, offset].T, shift_back(field, offset), precision=hp, preferred_element_type=jnp.float32)
        return result

    numerator = correlate(signal)
    factors_now = loadings
    off_mask = 1.0 - jnp.eye(FACTORS, dtype=jnp.float32)
    for sweep in range(ITERS):
        gram_mat = jnp.dot(factors_now, factors_now.T, precision=hp, preferred_element_type=jnp.float32) / length_all
        rounded = lax.optimization_barrier(factors_now.astype(jnp.bfloat16)).astype(jnp.float32)
        recon = jnp.zeros((CHANNELS, length_all), jnp.float32)
        for offset in range(LAGS):
            recon = recon + jnp.dot(motif_all[:, :, offset], shift_fore(rounded, offset), precision=hp, preferred_element_type=jnp.float32)
        recon = lax.optimization_barrier(recon.astype(jnp.bfloat16)).astype(jnp.float32)
        denominator = correlate(recon)
        penalty = penalty_weight * jnp.dot(gram_mat * off_mask, factors_now, precision=hp, preferred_element_type=jnp.float32)
        factors_now = factors_now * numerator / (denominator + penalty)
    return factors_now
```

```python
import functools

import jax
import jax.numpy as jnp
from jax import lax
from jax.experimental import pallas as pl
from jax.experimental.pallas import tpu as pltpu
from jax.sharding import PartitionSpec as P

LAGS = 32
ITERS = 3
PENALTY = 0.2

PHASES = 4
CHUNKS = 16
REACH = LAGS // PHASES
LANES = 128
GROUP = 8

NT = (((1,), (1,)), ((), ()))
NN = (((1,), (0,)), ((), ()))
TN = (((0,), (0,)), ((), ()))
F32 = jnp.float32
BF16 = jnp.bfloat16


def dot(a, b, dims=NN):
    return lax.dot_general(a, b, dims, preferred_element_type=F32)


def split(a):
    high = a.astype(BF16)
    return high, (a - high.astype(F32)).astype(BF16)


def vmem(n=1):
    return [pl.BlockSpec(memory_space=pltpu.VMEM)] * n


def smem(n=1):
    return [pl.BlockSpec(memory_space=pltpu.SMEM)] * n


def call(body, out_shape, in_specs, scratch=(), flops=0, moved=0, limit=40):
    return pl.pallas_call(
        body,
        out_shape=out_shape,
        in_specs=in_specs,
        out_specs=jax.tree.map(lambda _: pl.BlockSpec(memory_space=pltpu.VMEM), out_shape),
        scratch_shapes=list(scratch),
        compiler_params=pltpu.CompilerParams(vmem_limit_bytes=limit * 2**20),
        cost_estimate=pl.CostEstimate(flops=flops, bytes_accessed=moved, transcendentals=0),
    )


class Plan:
    def __init__(self, steps, factors):
        self.steps = steps
        self.factors = factors
        self.width = PHASES * factors
        self.edge = 2 * REACH
        self.rows = steps // PHASES + 2 * self.edge
        self.per = self.rows // CHUNKS
        self.ext = self.per + 2 * REACH
        self.stride = PHASES * self.per
        self.halo = PHASES * (self.edge + REACH)
        self.front = PHASES * self.edge
        self.back = PHASES * (self.edge + REACH)
        wide = steps + 2 * self.halo
        self.wide = -(-wide // LANES) * LANES
        self.tiles = LAGS + PHASES


def lay_loadings(plan, pair_ref, out_ref, buf):
    for i in range(plan.wide // LANES):
        buf[i * LANES : (i + 1) * LANES, :] = pair_ref[:, i * LANES : (i + 1) * LANES].T
    for m in range(plan.ext):
        row = slice(m * CHUNKS, (m + 1) * CHUNKS)
        for h in range(PHASES // 2):
            out_ref[row, h * LANES : (h + 1) * LANES] = buf[
                pl.ds(PHASES * m + 2 * h, CHUNKS, stride=plan.stride), :
            ]


def lay_data(plan, data_ref, out_ref, buf):
    channels = data_ref.shape[0]
    fill = jnp.zeros((LANES - channels, LANES), F32)
    for i in range(plan.wide // LANES):
        tile = data_ref[:, i * LANES : (i + 1) * LANES].astype(F32)
        buf[i * LANES : (i + 1) * LANES, :] = jnp.concatenate([tile, fill], 0).T
    for m in range(plan.per + REACH):
        row = slice(m * CHUNKS, (m + 1) * CHUNKS)
        for p in range(PHASES):
            out_ref[row, p * LANES : (p + 1) * LANES] = buf[
                pl.ds(PHASES * m + p, CHUNKS, stride=plan.stride), :
            ].astype(BF16)


def sum_block(plan, slot_ref, motif_ref, data_ref, stk_ref, auto_ref, numer_ref, padded):
    factors = plan.factors
    channels = motif_ref.shape[1]
    span = GROUP * LAGS
    padded[channels:, :] = jnp.zeros((LANES - channels, span), BF16)
    row = lax.broadcasted_iota(jnp.int32, (span, span), 0)
    col = lax.broadcasted_iota(jnp.int32, (span, span), 1)
    pick = jnp.where(col == (row % GROUP) * LAGS + row // GROUP, 1.0, 0.0).astype(BF16)
    for q in range(PHASES):
        rows = slice(q * factors, (q + 1) * factors)
        if q:
            stk_ref[rows, : q * LANES] = jnp.zeros((factors, q * LANES), BF16)
        stk_ref[rows, (LAGS + q) * LANES :] = jnp.zeros((factors, (PHASES - q) * LANES), BF16)
    for pair in range(factors // (2 * GROUP)):
        halves = []
        for half in range(2):
            padded[:channels, :] = motif_ref[slot_ref[2 * pair + half]]
            halves.append(dot(pick, padded[...], NT))
        for lag in range(LAGS):
            at = slice(lag * GROUP, (lag + 1) * GROUP)
            tile = jnp.concatenate([halves[0][at], halves[1][at]], 0).astype(BF16)
            for q in range(PHASES):
                first = q * factors + pair * 2 * GROUP
                stk_ref[first : first + 2 * GROUP, (lag + q) * LANES : (lag + q + 1) * LANES] = tile

    last = (PHASES - 1) * factors
    chunk = 2 * LANES
    shift = PHASES * LANES // chunk
    auto_ref[...] = jnp.zeros_like(auto_ref)
    for u in range(plan.tiles * LANES // chunk):
        taps = min(u // shift + 1, REACH)
        left = jnp.concatenate(
            [
                stk_ref[last : last + factors, (u - shift * a) * chunk : (u - shift * a + 1) * chunk]
                for a in range(taps)
            ],
            0,
        )
        auto_ref[: taps * factors, :] += dot(left, stk_ref[:, u * chunk : (u + 1) * chunk], NT)

    deep = PHASES * LANES
    for s in range(REACH + 1):
        part = dot(
            data_ref[s * CHUNKS : s * CHUNKS + plan.rows, :], stk_ref[:, s * deep : (s + 1) * deep], NT
        )
        if s == 0:
            numer_ref[...] = part
        else:
            numer_ref[...] += part


def tail_part(plan, stk_ref, x_ref, out_ref):
    width = plan.width
    deep = PHASES * LANES
    start = (plan.steps // PHASES + plan.edge) - (CHUNKS - 1) * plan.per + REACH
    inside = [x_ref[(start - REACH + i) * CHUNKS + CHUNKS - 1, :][None, :] for i in range(REACH)]
    known = jnp.concatenate(inside + [jnp.zeros((REACH, width), F32)], 0).astype(BF16).astype(F32)
    ahead = jnp.zeros((REACH, deep), F32)
    for s in range(1, REACH + 1):
        rows = known[REACH - s : 2 * REACH - s].astype(BF16)
        ahead += dot(rows, stk_ref[:, s * deep : (s + 1) * deep])
    ahead = jnp.concatenate([jnp.zeros((REACH, deep), F32), ahead], 0)
    out = jnp.zeros((REACH, width), F32)
    for s in range(1, REACH + 1):
        high, low = split(ahead[s : s + REACH])
        part = stk_ref[:, s * deep : (s + 1) * deep]
        out += dot(high, part, NT) + dot(low, part, NT)
    out_ref[...] = out


def tail_body(plan, blocks, flag_ref, x_ref, *refs):
    stks, out_ref, part = refs[:blocks], refs[blocks], refs[blocks + 1]
    out_ref[...] = jnp.zeros_like(out_ref)

    @pl.when(flag_ref[1] == 1)
    def _():
        for stk_ref in stks:
            tail_part(plan, stk_ref, x_ref, part)
            out_ref[...] += part[...]


def taps_body(plan, auto_a, auto_b, high_ref, low_ref, line):
    factors, width = plan.factors, plan.width
    line[:, :width] = jnp.zeros((factors, width), F32)
    for a in range(REACH):
        rows = slice(a * factors, (a + 1) * factors)
        line[:, (REACH - a) * width : (REACH - a + 1) * width] = auto_a[rows, :] + auto_b[rows, :]
    zero = (REACH * PHASES + PHASES - 1) * factors
    back = [
        line[:, zero - d * factors : zero - (d - 1) * factors].T for d in range(1, PHASES)
    ]
    back.append(jnp.zeros((factors, factors), F32))
    line[:, (REACH + 1) * width :] = jnp.concatenate(back, 1)
    for s in range(REACH + 1):
        for p in range(PHASES):
            first = zero - (PHASES * s + p) * factors
            high, low = split(line[:, first : first + width])
            rows = slice(s * width + p * factors, s * width + (p + 1) * factors)
            high_ref[rows, :] = high
            low_ref[rows, :] = low


def conv_body(plan, x_ref, high_ref, low_ref, out_ref, xb):
    width, rows = plan.width, plan.rows
    xb[...] = x_ref[...].astype(BF16)
    first = True
    for s in range(-REACH, REACH + 1):
        at = (REACH + s) * CHUNKS
        mat = slice(abs(s) * width, (abs(s) + 1) * width)
        dims = NN if s >= 0 else NT
        part = dot(xb[at : at + rows, :], high_ref[mat, :], dims)
        part += dot(xb[at : at + rows, :], low_ref[mat, :], dims)
        if first:
            out_ref[...] = part
        else:
            out_ref[...] += part
        first = False


def first_conv_body(plan, auto_a, auto_b, x_ref, high_ref, low_ref, out_ref, line, xb):
    taps_body(plan, auto_a, auto_b, high_ref, low_ref, line)
    conv_body(plan, x_ref, high_ref, low_ref, out_ref, xb)


def gram_of(plan, kept):
    factors = plan.factors
    high, low = split(kept)
    cross = dot(high, low, TN)
    full = dot(high, high, TN) + cross + cross.T
    total = full[:factors, :factors]
    for p in range(1, PHASES):
        at = slice(p * factors, (p + 1) * factors)
        total += full[at, at]
    return total


def own_rows(plan):
    row = lax.broadcasted_iota(jnp.int32, (plan.rows, plan.width), 0)
    m, j = row // CHUNKS, row % CHUNKS
    n = plan.per * j + m - plan.edge
    return n < 0, n >= plan.steps // PHASES


def gram_body(plan, x_ref, out_ref):
    before, after = own_rows(plan)
    x = x_ref[REACH * CHUNKS : REACH * CHUNKS + plan.rows, :]
    out_ref[...] = gram_of(plan, jnp.where(before | after, 0.0, x))


def updated(plan, flag_ref, x_ref, den_ref, numer_a, numer_b, tail_a, tail_b, gram_ref, scale, den):
    factors, width, rows = plan.factors, plan.width, plan.rows
    r = lax.broadcasted_iota(jnp.int32, (factors, factors), 0)
    c = lax.broadcasted_iota(jnp.int32, (factors, factors), 1)
    off = jnp.where(r == c, 0.0, gram_ref[...]) * scale
    blank = jnp.zeros((factors, factors), F32)
    mix = jnp.concatenate(
        [
            jnp.concatenate([off if p == q else blank for q in range(PHASES)], 1)
            for p in range(PHASES)
        ],
        0,
    )
    x = x_ref[REACH * CHUNKS : REACH * CHUNKS + rows, :]
    xh, xl = split(x)
    mh, ml = split(mix)
    den[...] = den_ref[...] + (dot(xh, mh) + dot(xh, ml) + dot(xl, mh))

    @pl.when(flag_ref[1] == 1)
    def _():
        start = (plan.steps // PHASES + plan.edge) - (CHUNKS - 1) * plan.per
        for i in range(REACH):
            at = slice((start - REACH + i) * CHUNKS, (start - REACH + i + 1) * CHUNKS)
            j = lax.broadcasted_iota(jnp.int32, (CHUNKS, width), 0)
            over = tail_a[i : i + 1, :] + tail_b[i : i + 1, :]
            den[at, :] -= jnp.where(j == CHUNKS - 1, over, 0.0)

    before, after = own_rows(plan)
    out_of = (before & (flag_ref[0] == 1)) | (after & (flag_ref[1] == 1))
    new = x * (numer_a[...] + numer_b[...]) / den[...]
    return jnp.where(out_of, 0.0, new), before | after


def update_body(plan, scale, flag_ref, x_ref, den_ref, na, nb, ta, tb, gram_ref, out_ref, own_ref, den):
    new, foreign = updated(plan, flag_ref, x_ref, den_ref, na, nb, ta, tb, gram_ref, scale, den)
    rows, width = plan.rows, plan.width
    edge = REACH * CHUNKS
    out_ref[edge : edge + rows, :] = new
    j = lax.broadcasted_iota(jnp.int32, (edge, width), 0) % CHUNKS
    low = pltpu.roll(new[rows - edge :], 1, 0)
    out_ref[:edge, :] = jnp.where(j == 0, 0.0, low)
    high = pltpu.roll(new[:edge], edge - 1, 0)
    out_ref[edge + rows :, :] = jnp.where(j == CHUNKS - 1, 0.0, high)
    own_ref[...] = gram_of(plan, jnp.where(foreign, 0.0, new))


def last_body(plan, scale, flag_ref, x_ref, den_ref, na, nb, ta, tb, gram_ref, out_ref, den, buf):
    new, _ = updated(plan, flag_ref, x_ref, den_ref, na, nb, ta, tb, gram_ref, scale, den)
    den[...] = new
    for m in range(plan.per):
        for h in range(PHASES // 2):
            both = den[m * CHUNKS : (m + 1) * CHUNKS, h * LANES : (h + 1) * LANES]
            at = PHASES * m + 2 * h
            buf[pl.ds(at, CHUNKS, stride=plan.stride), :] = both
            buf[pl.ds(at + 1, CHUNKS, stride=plan.stride), :] = pltpu.roll(both, LANES // 2, 1)
    for i in range(plan.steps // LANES):
        at = plan.front + i * LANES
        out_ref[:, i * LANES : (i + 1) * LANES] = buf[at : at + LANES, :].T[: plan.factors, :]


def swap(x, axis, bit):
    count = lax.axis_size(axis)
    return lax.ppermute(x, axis, [(i, i ^ bit) for i in range(count)])


def shifted(x, axis, by):
    count = lax.axis_size(axis)
    return lax.ppermute(x, axis, [(i, i + by) for i in range(count) if 0 <= i + by < count])


def doubling(axis):
    count = lax.axis_size(axis)
    bits = [1 << b for b in range(count.bit_length() - 1)]
    return bits[1:] + bits[:1]


def total(x, axis):
    for bit in doubling(axis):
        x = x + swap(x, axis, bit)
    return x


def on_device(data, motifs, loadings):
    channels, steps = data.shape
    factors = loadings.shape[0]
    plan = Plan(steps, factors)
    shards = lax.axis_size("tm")
    me = lax.axis_index("tm")
    width, rows = plan.width, plan.rows
    ext_rows = plan.ext * CHUNKS
    sds = jax.ShapeDtypeStruct

    flags = jnp.stack([me == 0, me == shards - 1]).astype(jnp.int32)

    slots = motifs[None]
    order = [0]
    for bit in doubling("tm"):
        slots = jnp.concatenate([slots, swap(slots, "tm", bit)], 0)
        order = order + [o ^ bit for o in order]
    place = [order.index(b) for b in range(shards)]
    slot_of = jnp.take(jnp.array(place, jnp.int32), jnp.arange(shards, dtype=jnp.int32) ^ me)
    if motifs.shape[1] != GROUP * LAGS:
        whole = jnp.moveaxis(jnp.take(slots, slot_of, axis=0), 0, 1).reshape(channels, -1)
        slots = jnp.moveaxis(whole.reshape(channels, -1, GROUP * LAGS), 1, 0)
        slot_of = jnp.arange(slots.shape[0], dtype=jnp.int32)

    motif_blocks, data_blocks = [slots], [data]
    for bit in doubling("chan")[:-1]:
        motif_blocks += [swap(b, "chan", bit) for b in motif_blocks]
        data_blocks += [swap(b, "chan", bit) for b in data_blocks]
    blocks = len(motif_blocks)

    halo = plan.halo
    def rim(cut):
        return jnp.concatenate([cut(loadings)] + [cut(b).astype(F32) for b in data_blocks], 0)

    left = shifted(rim(lambda a: a[:, steps - halo :]), "tm", 1)
    right = shifted(rim(lambda a: a[:, :halo]), "tm", -1)

    fill = plan.wide - steps - 2 * halo
    x_wide = jnp.concatenate(
        [left[:factors], loadings, right[:factors], jnp.zeros((factors, fill), F32)], 1
    )
    x_pair = jnp.concatenate([x_wide, jnp.concatenate([x_wide[:, 1:], x_wide[:, :1]], 1)], 0)
    x = call(
        functools.partial(lay_loadings, plan),
        sds((ext_rows, width), F32),
        vmem(),
        [pltpu.VMEM((plan.wide, LANES), F32)],
    )(x_pair)

    lay = call(
        functools.partial(lay_data, plan),
        sds(((plan.per + REACH) * CHUNKS, PHASES * LANES), BF16),
        vmem(),
        [pltpu.VMEM((plan.wide, LANES), F32)],
    )
    summed = call(
        functools.partial(sum_block, plan),
        (
            sds((width, plan.tiles * LANES), BF16),
            sds((REACH * factors, width), F32),
            sds((rows, width), F32),
        ),
        smem() + vmem(2),
        [pltpu.VMEM((LANES, GROUP * LAGS), BF16)],
    )
    stks, auto, numer = [], 0.0, 0.0
    for b in range(blocks):
        at = slice(factors + b * channels, factors + (b + 1) * channels)
        wide = jnp.concatenate(
            [
                left[at, halo - plan.front :].astype(BF16),
                data_blocks[b],
                right[at, : plan.back].astype(BF16),
                jnp.zeros((channels, plan.wide - steps - plan.front - plan.back), BF16),
            ],
            1,
        )
        stk, auto_part, numer_part = summed(slot_of, motif_blocks[b], lay(wide))
        stks.append(stk)
        auto = auto + auto_part
        numer = numer + numer_part

    tail_of = call(
        functools.partial(tail_body, plan, blocks),
        sds((REACH, width), F32),
        smem() + vmem(1 + blocks),
        [pltpu.VMEM((REACH, width), F32)],
    )
    gram_local = call(functools.partial(gram_body, plan), sds((factors, factors), F32), vmem())(x)

    auto_far = swap(auto, "chan", 1)
    numer_far = swap(numer, "chan", 1)

    mats = sds(((REACH + 1) * width, width), BF16)
    high, low, den = call(
        functools.partial(first_conv_body, plan),
        (mats, mats, sds((rows, width), F32)),
        vmem(3),
        [pltpu.VMEM((factors, (REACH + 2) * width), F32), pltpu.VMEM((ext_rows, width), BF16)],
    )(auto, auto_far, x)
    conv = call(
        functools.partial(conv_body, plan),
        sds((rows, width), F32),
        vmem(3),
        [pltpu.VMEM((ext_rows, width), BF16)],
    )
    scale = PENALTY / (steps * shards)
    update = call(
        functools.partial(update_body, plan, scale),
        (sds((ext_rows, width), F32), sds((factors, factors), F32)),
        smem() + vmem(7),
        [pltpu.VMEM((rows, width), F32)],
    )
    finish = call(
        functools.partial(last_body, plan, scale),
        sds((factors, steps), F32),
        smem() + vmem(7),
        [pltpu.VMEM((rows, width), F32), pltpu.VMEM((plan.wide, LANES), F32)],
    )
    for sweep in range(ITERS):
        gram = total(gram_local, "tm")
        tail = tail_of(flags, x, *stks)
        tail_far = swap(tail, "chan", 1)
        if sweep:
            den = conv(x, high, low)
        operands = (flags, x, den, numer, numer_far, tail, tail_far, gram)
        if sweep < ITERS - 1:
            x, gram_local = update(*operands)
        else:
            return finish(*operands)


def solution(mesh):
    in_specs = (P("chan", "tm"), P("chan", "tm"), P(None, "tm"))
    out_specs = P(None, "tm")
    return jax.shard_map(
        on_device, mesh=mesh, in_specs=in_specs, out_specs=out_specs, check_vma=False
    )
```

```python
import functools

import jax
import jax.numpy as jnp
from jax import lax
from jax.experimental import pallas as pl
from jax.experimental.pallas import tpu as pltpu
from jax.sharding import PartitionSpec as P

LAGS = 32
ITERS = 3
PENALTY = 0.2

PHASES = 4
CHUNKS = 16
REACH = LAGS // PHASES
LANES = 128
GROUP = 8

NT = (((1,), (1,)), ((), ()))
NN = (((1,), (0,)), ((), ()))
TN = (((0,), (0,)), ((), ()))
F32 = jnp.float32
BF16 = jnp.bfloat16


def dot(a, b, dims=NN):
    return lax.dot_general(a, b, dims, preferred_element_type=F32)


def split(a):
    high = a.astype(BF16)
    return high, (a - high.astype(F32)).astype(BF16)


def vmem(n=1):
    return [pl.BlockSpec(memory_space=pltpu.VMEM)] * n


def smem(n=1):
    return [pl.BlockSpec(memory_space=pltpu.SMEM)] * n


def call(body, out_shape, in_specs, scratch=(), flops=0, moved=0, limit=16):
    return pl.pallas_call(
        body,
        out_shape=out_shape,
        in_specs=in_specs,
        out_specs=jax.tree.map(lambda _: pl.BlockSpec(memory_space=pltpu.VMEM), out_shape),
        scratch_shapes=list(scratch),
        compiler_params=pltpu.CompilerParams(vmem_limit_bytes=limit * 2**20),
        cost_estimate=pl.CostEstimate(flops=flops, bytes_accessed=moved, transcendentals=0),
    )


class Plan:
    def __init__(self, steps, factors):
        self.steps = steps
        self.factors = factors
        self.width = PHASES * factors
        self.edge = 2 * REACH
        self.rows = steps // PHASES + 2 * self.edge
        self.per = self.rows // CHUNKS
        self.ext = self.per + 2 * REACH
        self.stride = PHASES * self.per
        self.halo = PHASES * (self.edge + REACH)
        self.front = PHASES * self.edge
        self.back = PHASES * (self.edge + REACH)
        wide = steps + 2 * self.halo
        self.wide = -(-wide // LANES) * LANES
        self.tiles = LAGS + PHASES


def lane_tiles(count):
    return [slice(i * LANES, (i + 1) * LANES) for i in range(count)]


def row_tile(m):
    return slice(m * CHUNKS, (m + 1) * CHUNKS)


def turned(buf, left, middle, right, tiles):
    parts = [left] + [middle[:, at] for at in lane_tiles(tiles)] + [right]
    for i, part in enumerate(parts):
        part = part.astype(F32)
        spare = LANES - part.shape[0]
        low = part if spare == part.shape[0] else jnp.zeros((spare, LANES), F32)
        buf[i * LANES : (i + 1) * LANES, :] = jnp.concatenate([part, low], 0).T


def spread(plan, tile, m, bits_ref):
    j = lax.broadcasted_iota(jnp.int32, tile.shape, 0)
    bits_ref[row_tile(m + REACH), :] = tile.astype(BF16)
    if m >= plan.per - REACH:
        low = jnp.where(j == 0, 0.0, pltpu.roll(tile, 1, 0))
        bits_ref[row_tile(m - plan.per + REACH), :] = low.astype(BF16)
    if m < REACH:
        high = jnp.where(j == CHUNKS - 1, 0.0, pltpu.roll(tile, CHUNKS - 1, 0))
        bits_ref[row_tile(m + plan.per + REACH), :] = high.astype(BF16)


def lay_loadings(plan, load_ref, left_ref, right_ref, x_ref, bits_ref, low_ref, buf):
    factors = plan.factors
    turned(buf, left_ref[:factors, :], load_ref, right_ref[:factors, :], plan.steps // LANES)
    lane = lax.broadcasted_iota(jnp.int32, (CHUNKS, LANES), 1)
    skip = LANES - plan.halo
    for m in range(plan.ext):
        halves = []
        for h in range(PHASES // 2):
            at = skip + PHASES * m + 2 * h
            even = buf[pl.ds(at, CHUNKS, stride=plan.stride), :]
            odd = buf[pl.ds(at + 1, CHUNKS, stride=plan.stride), :]
            halves.append(jnp.where(lane < factors, even, odd))
        tile = jnp.concatenate(halves, 1)
        bits = tile.astype(BF16)
        bits_ref[row_tile(m), :] = bits
        if REACH <= m < REACH + plan.per:
            x_ref[row_tile(m - REACH), :] = tile
            low_ref[row_tile(m - REACH), :] = (tile - bits.astype(F32)).astype(BF16)


def lay_data(plan, data_ref, rims_ref, out_ref, buf):
    turned(buf, rims_ref[:, :LANES], data_ref, rims_ref[:, LANES:], plan.steps // LANES)
    skip = LANES - plan.front
    for m in range(plan.per + REACH):
        for p, at in enumerate(lane_tiles(PHASES)):
            rows = pl.ds(skip + PHASES * m + p, CHUNKS, stride=plan.stride)
            out_ref[row_tile(m), at] = buf[rows, :].astype(BF16)


def first_gram(load_ref, out_ref):
    high, low = split(load_ref[...])
    cross = dot(high, low, NT)
    out_ref[...] = dot(high, high, NT) + cross + cross.T


def rim_body(plan, load_ref, data_ref, even_ref, tail_ref, head_ref):
    factors = plan.factors
    ends = ((tail_ref, slice(plan.steps - LANES, plan.steps)), (head_ref, slice(0, LANES)))
    for rim_ref, at in ends:
        rim_ref[:factors, :] = load_ref[:, at]
        rim_ref[factors:, :] = data_ref[:, at].astype(F32)


def lay_motifs(plan, me_ref, even_ref, odd_ref, stk_ref, padded):
    factors = plan.factors
    channels = even_ref.shape[1]
    span = GROUP * LAGS
    me = me_ref[0]
    padded[channels:, :] = jnp.zeros((LANES - channels, 2 * span), BF16)
    row = lax.broadcasted_iota(jnp.int32, (span, span), 0)
    col = lax.broadcasted_iota(jnp.int32, (span, span), 1)
    pick = jnp.where(col == (row % GROUP) * LAGS + row // GROUP, 1.0, 0.0).astype(BF16)
    for q in range(PHASES):
        rows = slice(q * factors, (q + 1) * factors)
        if q:
            stk_ref[rows, : q * LANES] = jnp.zeros((factors, q * LANES), BF16)
        stk_ref[rows, (LAGS + q) * LANES :] = jnp.zeros((factors, (PHASES - q) * LANES), BF16)
    swapped = me % 2
    for pair in range(factors // (2 * GROUP)):
        at = (me // 2) ^ pair
        one, two = even_ref[at].astype(F32), odd_ref[at].astype(F32)
        padded[:channels, :span] = jnp.where(swapped == 1, two, one).astype(BF16)
        padded[:channels, span:] = jnp.where(swapped == 1, one, two).astype(BF16)
        halves = [dot(pick, padded[:, h * span : (h + 1) * span], NT) for h in range(2)]
        for lag in range(LAGS):
            cut = slice(lag * GROUP, (lag + 1) * GROUP)
            tile = jnp.concatenate([halves[0][cut], halves[1][cut]], 0).astype(BF16)
            for q in range(PHASES):
                first = q * factors + pair * 2 * GROUP
                stk_ref[first : first + 2 * GROUP, (lag + q) * LANES : (lag + q + 1) * LANES] = tile


def auto_body(plan, me_ref, even_ref, odd_ref, *refs):
    before, (stk_ref, auto_ref, padded) = refs[:-3], refs[-3:]
    factors = plan.factors
    lay_motifs(plan, me_ref, even_ref, odd_ref, stk_ref, padded)
    last = (PHASES - 1) * factors
    chunk = 2 * LANES
    shift = PHASES * LANES // chunk
    auto_ref[...] = before[0][...] if before else jnp.zeros_like(auto_ref)
    for u in range(plan.tiles * LANES // chunk):
        taps = min(u // shift + 1, REACH)
        cuts = [u - shift * a for a in range(taps)]
        left = [stk_ref[last : last + factors, c * chunk : (c + 1) * chunk] for c in cuts]
        auto_ref[: taps * factors, :] += dot(
            jnp.concatenate(left, 0), stk_ref[:, u * chunk : (u + 1) * chunk], NT
        )


def numer_body(plan, stk_ref, data_ref, *refs):
    before, numer_ref = refs[:-1], refs[-1]
    deep = PHASES * LANES
    for s in range(REACH + 1):
        rows = slice(s * CHUNKS, s * CHUNKS + plan.rows)
        part = dot(data_ref[rows, :], stk_ref[:, s * deep : (s + 1) * deep], NT)
        if s:
            numer_ref[...] += part
        else:
            numer_ref[...] = part + before[0][...] if before else part


def tail_part(plan, stk_ref, bits_ref):
    width = plan.width
    deep = PHASES * LANES
    start = (plan.steps // PHASES + plan.edge) - (CHUNKS - 1) * plan.per + REACH
    inside = [
        bits_ref[row_tile(start - REACH + i), :].astype(F32)[CHUNKS - 1 :] for i in range(REACH)
    ]
    known = jnp.concatenate(inside + [jnp.zeros((REACH, width), F32)], 0)
    ahead = jnp.zeros((REACH, deep), F32)
    for s in range(1, REACH + 1):
        rows = known[REACH - s : 2 * REACH - s].astype(BF16)
        ahead += dot(rows, stk_ref[:, s * deep : (s + 1) * deep])
    blank = jnp.zeros((REACH, deep), F32)
    high = ahead.astype(BF16).astype(F32)
    high, low = jnp.concatenate([blank, high], 0), jnp.concatenate([blank, ahead - high], 0)
    out = jnp.zeros((2 * REACH, width), F32)
    for s in range(1, REACH + 1):
        both = jnp.concatenate([high[s : s + REACH], low[s : s + REACH]], 0).astype(BF16)
        out += dot(both, stk_ref[:, s * deep : (s + 1) * deep], NT)
    return out[:REACH] + out[REACH:]


def tail_body(plan, shards, me_ref, bits_ref, *refs):
    stks, out_ref = refs[:-1], refs[-1]
    out_ref[...] = jnp.zeros_like(out_ref)

    @pl.when(me_ref[0] == shards - 1)
    def _():
        for stk_ref in stks:
            out_ref[...] += tail_part(plan, stk_ref, bits_ref)


def taps_body(plan, auto_a, auto_b, high_ref, low_ref, line):
    factors, width = plan.factors, plan.width
    line[:, :width] = jnp.zeros((factors, width), F32)
    for a in range(REACH):
        rows = slice(a * factors, (a + 1) * factors)
        line[:, (REACH - a) * width : (REACH - a + 1) * width] = auto_a[rows, :] + auto_b[rows, :]
    zero = (REACH * PHASES + PHASES - 1) * factors
    back = [
        line[:, zero - d * factors : zero - (d - 1) * factors].T for d in range(1, PHASES)
    ]
    back.append(jnp.zeros((factors, factors), F32))
    line[:, (REACH + 1) * width :] = jnp.concatenate(back, 1)
    for s in range(REACH + 1):
        for p in range(PHASES):
            first = zero - (PHASES * s + p) * factors
            high, low = split(line[:, first : first + width])
            rows = slice(s * width + p * factors, s * width + (p + 1) * factors)
            high_ref[rows, :] = high
            low_ref[rows, :] = low


def conv_body(plan, offsets, bits_ref, high_ref, low_ref, *refs):
    before, out_ref = refs[:-1], refs[-1]
    width, rows = plan.width, plan.rows
    for i, s in enumerate(offsets):
        at = (REACH + s) * CHUNKS
        mat = slice(abs(s) * width, (abs(s) + 1) * width)
        dims = NN if s >= 0 else NT
        part = dot(bits_ref[at : at + rows, :], high_ref[mat, :], dims)
        part += dot(bits_ref[at : at + rows, :], low_ref[mat, :], dims)
        if i:
            out_ref[...] += part
        else:
            out_ref[...] = part + before[0][...] if before else part


def first_conv_body(plan, offsets, auto_a, auto_b, bits_ref, high_ref, low_ref, out_ref, line):
    taps_body(plan, auto_a, auto_b, high_ref, low_ref, line)
    conv_body(plan, offsets, bits_ref, high_ref, low_ref, out_ref)


def penalties(plan, scale, me_ref, grams, bits_ref, low_ref):
    factors, rows = plan.factors, plan.rows
    total = grams[0][...]
    if len(grams) > 1:
        here, far, both = (g[...] for g in grams[1:])
        odd = me_ref[1] == 1
        near = jnp.where(odd, far, here)
        next_one = jnp.where(odd, here, far)
        total = (total + near) + (next_one + both)
    r = lax.broadcasted_iota(jnp.int32, (factors, factors), 0)
    c = lax.broadcasted_iota(jnp.int32, (factors, factors), 1)
    off = jnp.where(r == c, 0.0, total) * scale
    blank = jnp.zeros((factors, factors), F32)
    high, low = split(
        jnp.concatenate(
            [
                jnp.concatenate([off if p == q else blank for q in range(PHASES)], 1)
                for p in range(PHASES)
            ],
            0,
        )
    )
    bits = bits_ref[REACH * CHUNKS : REACH * CHUNKS + rows, :]
    return dot(bits, high) + dot(bits, low) + dot(low_ref[...], high)


def new_tile(plan, shards, me_ref, m, x_ref, den_ref, numer, pen, tails):
    at = row_tile(m)
    den = den_ref[at, :] + pen[at, :]
    j = lax.broadcasted_iota(jnp.int32, den.shape, 0)
    end = (plan.steps // PHASES + plan.edge) - (CHUNKS - 1) * plan.per
    if end - REACH <= m < end:
        i = m - end + REACH
        over = tails[0][i : i + 1, :] + tails[1][i : i + 1, :]
        den -= jnp.where((j == CHUNKS - 1) & (me_ref[0] == shards - 1), over, 0.0)
    new = x_ref[at, :] * numer / den
    if m < plan.edge:
        new = jnp.where((j == 0) & (me_ref[0] == 0), 0.0, new)
    if m >= end:
        new = jnp.where((j == CHUNKS - 1) & (me_ref[0] == shards - 1), 0.0, new)
    return new


def update_body(plan, scale, shards, counts, me_ref, x_ref, bits_ref, low_ref, den_ref, *refs):
    numers, tails, grams = refs[: counts[0]], refs[counts[0] :][:2], refs[counts[0] + 2 :][: counts[1]]
    refs = refs[counts[0] + 2 + counts[1] :]
    if counts[0] > 1:
        numer_ref, refs = refs[0], refs[1:]
    out_ref, out_bits, out_low, gram_ref, pen, both = refs
    factors, width = plan.factors, plan.width
    pen[...] = penalties(plan, scale, me_ref, grams, bits_ref, low_ref)
    end = (plan.steps // PHASES + plan.edge) - (CHUNKS - 1) * plan.per
    for m in range(plan.per):
        at = row_tile(m)
        numer = numers[0][at, :]
        if counts[0] > 1:
            numer = numer + numers[1][at, :]
            numer_ref[at, :] = numer
        new = new_tile(plan, shards, me_ref, m, x_ref, den_ref, numer, pen, tails)
        out_ref[at, :] = new
        spread(plan, new, m, out_bits)
        high, low = split(new)
        out_low[at, :] = low
        j = lax.broadcasted_iota(jnp.int32, new.shape, 0)
        kept = new
        if m < plan.edge:
            kept = jnp.where(j == 0, 0.0, kept)
        if m >= end:
            kept = jnp.where(j == CHUNKS - 1, 0.0, kept)
        high, low = split(kept)
        both[at, :width] = high
        both[at, width:] = low
    full = dot(both[:, :width], both[...], TN)
    cross = full[:, width:]
    full = full[:, :width] + cross + cross.T
    gram_ref[...] = sum(
        full[p * factors : (p + 1) * factors, p * factors : (p + 1) * factors] for p in range(PHASES)
    )


def last_body(plan, scale, shards, counts, me_ref, x_ref, bits_ref, low_ref, den_ref, *refs):
    numers, tails, grams = refs[: counts[0]], refs[counts[0] :][:2], refs[counts[0] + 2 :][: counts[1]]
    out_ref, pen, buf = refs[counts[0] + 2 + counts[1] :]
    pen[...] = penalties(plan, scale, me_ref, grams, bits_ref, low_ref)
    for m in range(plan.per):
        numer = sum(n[row_tile(m), :] for n in numers)
        new = new_tile(plan, shards, me_ref, m, x_ref, den_ref, numer, pen, tails)
        for h, lanes in enumerate(lane_tiles(PHASES // 2)):
            at = PHASES * m + 2 * h
            buf[pl.ds(at, CHUNKS, stride=plan.stride), :] = new[:, lanes]
            turn = pltpu.roll(new[:, lanes], LANES // 2, 1)
            buf[pl.ds(at + 1, CHUNKS, stride=plan.stride), :] = turn
    for i, lanes in enumerate(lane_tiles(plan.steps // LANES)):
        at = plan.front + i * LANES
        out_ref[:, lanes] = buf[at : at + LANES, :].T[: plan.factors, :]


def swap(x, axis, bit):
    count = lax.axis_size(axis)
    return lax.ppermute(x, axis, [(i, i ^ bit) for i in range(count)])


def mixed(x, bit_even, bit_odd):
    wide = lax.axis_size("chan")
    pairs = []
    for t in range(lax.axis_size("tm")):
        for c in range(wide):
            far = t ^ (bit_odd if c % 2 else bit_even)
            pairs.append((t * wide + c, far * wide + c))
    return lax.ppermute(x, ("tm", "chan"), pairs)


def shifted(x, axis, by):
    count = lax.axis_size(axis)
    return lax.ppermute(x, axis, [(i, i + by) for i in range(count) if 0 <= i + by < count])


def doubling(axis):
    count = lax.axis_size(axis)
    bits = [1 << b for b in range(count.bit_length() - 1)]
    return bits[1:] + bits[:1]


def after(x, *others):
    return lax.optimization_barrier((x, *others))[0]


def gram_rounds(x, odd, meanwhile):
    bits = doubling("tm")
    singles, pairs = bits[-1:], bits[:-1]
    if len(pairs) % 2:
        singles, pairs = singles + pairs[-1:], pairs[:-1]
    gaps = list(meanwhile)

    def gap(y):
        return after(y, *gaps.pop(0)()) if gaps else y

    for bit in singles:
        x = x + gap(swap(x, "tm", bit))
    terms = [x]
    while pairs:
        one, two, pairs = pairs[0], pairs[1], pairs[2:]
        here, both = mixed(x, one, two), swap(x, "tm", one ^ two)
        here = gap(here)
        far = swap(here, "chan", 1)
        terms = [x, here, far, both]
        if pairs:
            near, other = jnp.where(odd, far, here), jnp.where(odd, here, far)
            x = (x + near) + (other + both)
    return terms


def on_device(data, motifs, loadings):
    channels, steps = data.shape
    factors = loadings.shape[0]
    plan = Plan(steps, factors)
    shards = lax.axis_size("tm")
    width, rows = plan.width, plan.rows
    ext_rows = plan.ext * CHUNKS
    sds = jax.ShapeDtypeStruct
    place = jnp.stack([lax.axis_index("tm"), lax.axis_index("chan") % 2]).astype(jnp.int32)
    odd = place[1] == 1

    rim = sds((factors + channels, LANES), F32)
    gram = call(first_gram, sds((factors, factors), F32), vmem())(loadings)

    start = place
    bits = doubling("tm")
    even = motifs[None]
    for i, bit in enumerate(bits[:-1]):
        near, gram_near = swap(even, "tm", bit), swap(gram, "tm", bit)
        if i == 1:
            near, gram_near, right = lax.optimization_barrier((near, gram_near, right))
        else:
            near, gram_near = lax.optimization_barrier((near, gram_near))
        even, gram = jnp.concatenate([even, near], 0), gram + gram_near
        if i == 0:
            tail_rim, head_rim = call(functools.partial(rim_body, plan), (rim, rim), vmem(3))(
                loadings, data, even
            )
            left, right = shifted(tail_rim, "tm", 1), shifted(head_rim, "tm", -1)
            far_data = swap(after(data, even), "chan", 2)
    odds = swap(even, "tm", bits[-1])
    far_even = swap(even, "chan", 2)
    gram_near = swap(gram, "tm", bits[-1])
    odds, far_even, gram_near, left, far_data = lax.optimization_barrier(
        (odds, far_even, gram_near, left, far_data)
    )
    gram = gram + gram_near
    if motifs.shape[1] != GROUP * LAGS:
        order = [0]
        for bit in bits:
            order = order + [o ^ bit for o in order]
        slots = jnp.concatenate([even, odds], 0)
        index = jnp.array([order.index(b) for b in range(shards)], jnp.int32)
        slots = jnp.take(slots, jnp.take(index, jnp.arange(shards) ^ place[0]), axis=0)
        slots = jnp.moveaxis(slots, 0, 1).reshape(channels, -1, GROUP * LAGS)
        slots = jnp.moveaxis(slots, 1, 0)
        even, odds = slots[0::2], slots[1::2]
        start = place * 0
        far_even = swap(even, "chan", 2)

    rims = jnp.concatenate([left[factors:], right[factors:]], 1).astype(BF16)
    far_odds = swap(jnp.concatenate([odds, rims[None]], 0), "chan", 2)
    far_rims = far_odds[-1]

    x, bits_x, low_x = call(
        functools.partial(lay_loadings, plan),
        (sds((rows, width), F32), sds((ext_rows, width), BF16), sds((rows, width), BF16)),
        vmem(3),
        [pltpu.VMEM((steps + 2 * LANES, LANES), F32)],
    )(loadings, left, right)
    lay = call(
        functools.partial(lay_data, plan),
        sds(((plan.per + REACH) * CHUNKS, PHASES * LANES), BF16),
        vmem(2),
        [pltpu.VMEM((steps + 2 * LANES, LANES), F32)],
    )

    def autos(evens, odd_ones, *before):
        return call(
            functools.partial(auto_body, plan),
            (sds((width, plan.tiles * LANES), BF16), sds((REACH * factors, width), F32)),
            smem() + vmem(2 + len(before)),
            [pltpu.VMEM((LANES, 2 * GROUP * LAGS), BF16)],
        )(start, evens, odd_ones, *before)

    def numers(stk, laid, *before):
        return call(
            functools.partial(numer_body, plan), sds((rows, width), F32), vmem(2 + len(before))
        )(stk, laid, *before)

    stk, auto = autos(even, odds)
    numer = numers(stk, lay(data, rims))
    far_laid = lay(far_data, far_rims)
    far_stk, auto = autos(far_even, far_odds, auto)
    auto_far = swap(auto, "chan", 1)
    numer = numers(far_stk, far_laid, numer)
    numer_far = swap(numer, "chan", 1)

    grams = [gram]

    def tail_of(bits_now):
        tail = call(
            functools.partial(tail_body, plan, shards),
            sds((REACH, width), F32),
            smem() + vmem(3),
        )(place, bits_now, stk, far_stk)
        return tail, swap(tail, "chan", 1)

    mats = sds(((REACH + 1) * width, width), BF16)
    every = list(range(-REACH, REACH + 1))
    high, low, den = call(
        functools.partial(first_conv_body, plan, every),
        (mats, mats, sds((rows, width), F32)),
        vmem(3),
        [pltpu.VMEM((factors, (REACH + 2) * width), F32)],
    )(auto, auto_far, bits_x)

    def conv(offsets, bits_now, *before):
        return call(
            functools.partial(conv_body, plan, offsets), sds((rows, width), F32), vmem(3 + len(before))
        )(bits_now, high, low, *before)

    scale = PENALTY / (steps * shards)
    field, window = sds((rows, width), F32), sds((ext_rows, width), BF16)
    low_field = sds((rows, width), BF16)
    numers_now = (numer, numer_far)
    for sweep in range(ITERS):
        if sweep == 0:
            tails = tail_of(bits_x)
        else:
            tails = tail_of(bits_x)
            part = conv(every[:REACH], bits_x)
            den = conv(every[REACH:], bits_x, part)
            grams = gram_rounds(gram, odd, [lambda: (part,), lambda: (den,)])
        operands = (place, x, bits_x, low_x, den, *numers_now, *tails, *grams)
        counts = (len(numers_now), len(grams))
        if sweep == ITERS - 1:
            return call(
                functools.partial(last_body, plan, scale, shards, counts),
                sds((factors, steps), F32),
                smem() + vmem(len(operands) - 1),
                [pltpu.VMEM((rows, width), F32), pltpu.VMEM((steps + 2 * LANES, LANES), F32)],
            )(*operands)
        outs = (field, window, low_field, sds((factors, factors), F32))
        if counts[0] > 1:
            outs = (field,) + outs
        got = call(
            functools.partial(update_body, plan, scale, shards, counts),
            outs,
            smem() + vmem(len(operands) - 1),
            [pltpu.VMEM((rows, width), F32), pltpu.VMEM((rows, 2 * width), BF16)],
        )(*operands)
        if counts[0] > 1:
            numers_now, got = got[:1], got[1:]
        x, bits_x, low_x, gram = got


def solution(mesh):
    in_specs = (P("chan", "tm"), P("chan", "tm"), P(None, "tm"))
    out_specs = P(None, "tm")
    return jax.shard_map(
        on_device, mesh=mesh, in_specs=in_specs, out_specs=out_specs, check_vma=False
    )
```

```python
import functools

import jax
import jax.numpy as jnp
from jax import lax
from jax.experimental import pallas as pl
from jax.experimental.pallas import tpu as pltpu
from jax.sharding import PartitionSpec as P

LAGS = 32
ITERS = 3
PENALTY = 0.2

PHASES = 4
CHUNKS = 16
REACH = LAGS // PHASES
LANES = 128
GROUP = 8

NT = (((1,), (1,)), ((), ()))
NN = (((1,), (0,)), ((), ()))
TN = (((0,), (0,)), ((), ()))
F32 = jnp.float32
BF16 = jnp.bfloat16


def dot(a, b, dims=NN):
    return lax.dot_general(a, b, dims, preferred_element_type=F32)


def split(a):
    high = a.astype(BF16)
    return high, (a - high.astype(F32)).astype(BF16)


def vmem(n=1):
    return [pl.BlockSpec(memory_space=pltpu.VMEM)] * n


def smem(n=1):
    return [pl.BlockSpec(memory_space=pltpu.SMEM)] * n


def call(body, out_shape, in_specs, scratch=(), flops=0, moved=0, limit=16):
    return pl.pallas_call(
        body,
        out_shape=out_shape,
        in_specs=in_specs,
        out_specs=jax.tree.map(lambda _: pl.BlockSpec(memory_space=pltpu.VMEM), out_shape),
        scratch_shapes=list(scratch),
        compiler_params=pltpu.CompilerParams(vmem_limit_bytes=limit * 2**20),
        cost_estimate=pl.CostEstimate(flops=flops, bytes_accessed=moved, transcendentals=0),
    )


class Plan:
    def __init__(self, steps, factors):
        self.steps = steps
        self.factors = factors
        self.width = PHASES * factors
        self.edge = 2 * REACH
        self.rows = steps // PHASES + 2 * self.edge
        self.per = self.rows // CHUNKS
        self.ext = self.per + 2 * REACH
        self.stride = PHASES * self.per
        self.halo = PHASES * (self.edge + REACH)
        self.front = PHASES * self.edge
        self.back = PHASES * (self.edge + REACH)
        wide = steps + 2 * self.halo
        self.wide = -(-wide // LANES) * LANES
        self.tiles = LAGS + PHASES


def lane_tiles(count):
    return [slice(i * LANES, (i + 1) * LANES) for i in range(count)]


def row_tile(m):
    return slice(m * CHUNKS, (m + 1) * CHUNKS)


def turned(buf, left, middle, right, tiles):
    parts = [left] + [middle[:, at] for at in lane_tiles(tiles)] + [right]
    for i, part in enumerate(parts):
        part = part.astype(F32)
        spare = LANES - part.shape[0]
        low = part if spare == part.shape[0] else jnp.zeros((spare, LANES), F32)
        buf[i * LANES : (i + 1) * LANES, :] = jnp.concatenate([part, low], 0).T


def spread(plan, tile, m, bits_ref):
    j = lax.broadcasted_iota(jnp.int32, tile.shape, 0)
    bits_ref[row_tile(m + REACH), :] = tile.astype(BF16)
    if m >= plan.per - REACH:
        low = jnp.where(j == 0, 0.0, pltpu.roll(tile, 1, 0))
        bits_ref[row_tile(m - plan.per + REACH), :] = low.astype(BF16)
    if m < REACH:
        high = jnp.where(j == CHUNKS - 1, 0.0, pltpu.roll(tile, CHUNKS - 1, 0))
        bits_ref[row_tile(m + plan.per + REACH), :] = high.astype(BF16)


def lay_loadings(plan, shards, me_ref, load_ref, left_ref, right_ref, stk_a, stk_b, *refs):
    x_ref, bits_ref, low_ref, tail_ref, buf, past, ahead = refs
    factors = plan.factors
    turned(buf, left_ref[:factors, :], load_ref, right_ref[:factors, :], plan.steps // LANES)
    lane = lax.broadcasted_iota(jnp.int32, (CHUNKS, LANES), 1)
    skip = LANES - plan.halo
    for m in range(plan.ext):
        halves = []
        for h in range(PHASES // 2):
            at = skip + PHASES * m + 2 * h
            even = buf[pl.ds(at, CHUNKS, stride=plan.stride), :]
            odd = buf[pl.ds(at + 1, CHUNKS, stride=plan.stride), :]
            halves.append(jnp.where(lane < factors, even, odd))
        tile = jnp.concatenate(halves, 1)
        bits = tile.astype(BF16)
        bits_ref[row_tile(m), :] = bits
        if REACH <= m < REACH + plan.per:
            x_ref[row_tile(m - REACH), :] = tile
            low_ref[row_tile(m - REACH), :] = (tile - bits.astype(F32)).astype(BF16)
    tail_body(plan, shards, me_ref, bits_ref, (stk_a, stk_b), tail_ref, past, ahead)


def lay_data(plan, data_ref, rims_ref, out_ref, buf):
    turned(buf, rims_ref[:, :LANES], data_ref, rims_ref[:, LANES:], plan.steps // LANES)
    skip = LANES - plan.front
    for m in range(plan.per + REACH):
        for p, at in enumerate(lane_tiles(PHASES)):
            rows = pl.ds(skip + PHASES * m + p, CHUNKS, stride=plan.stride)
            out_ref[row_tile(m), at] = buf[rows, :].astype(BF16)


def first_body(plan, me_ref, load_any, data_any, motif_any, *refs):
    motif_ref, gram_ref, near_ref, wide_ref, load_ref, data_ref, sems = refs
    factors = plan.factors
    moves = [
        pltpu.make_async_copy(source, target, sems.at[i])
        for i, (source, target) in enumerate(
            ((load_any, load_ref), (data_any, data_ref), (motif_any, motif_ref.at[0]))
        )
    ]
    for move in moves:
        move.start()
    for move in moves:
        move.wait()
    odd = me_ref[0] % 2 == 1
    head, tail = slice(0, LANES), slice(plan.steps - LANES, plan.steps)
    for rim_ref, even_at, odd_at in ((near_ref, tail, head), (wide_ref, head, tail)):
        rim_ref[:factors, :] = jnp.where(odd, load_ref[:, odd_at], load_ref[:, even_at])
        rim_ref[factors:, :] = jnp.where(
            odd, data_ref[:, odd_at].astype(F32), data_ref[:, even_at].astype(F32)
        )
    high, low = split(load_ref[...])
    cross = dot(high, low, NT)
    gram_ref[...] = dot(high, high, NT) + cross + cross.T


def lay_motifs(plan, me_ref, even_ref, odd_ref, stk_ref, padded):
    factors = plan.factors
    channels = even_ref.shape[1]
    span = GROUP * LAGS
    me = me_ref[0]
    padded[channels:, :] = jnp.zeros((LANES - channels, 2 * span), BF16)
    row = lax.broadcasted_iota(jnp.int32, (span, span), 0)
    col = lax.broadcasted_iota(jnp.int32, (span, span), 1)
    pick = jnp.where(col == (row % GROUP) * LAGS + row // GROUP, 1.0, 0.0).astype(BF16)
    for q in range(PHASES):
        rows = slice(q * factors, (q + 1) * factors)
        if q:
            stk_ref[rows, : q * LANES] = jnp.zeros((factors, q * LANES), BF16)
        stk_ref[rows, (LAGS + q) * LANES :] = jnp.zeros((factors, (PHASES - q) * LANES), BF16)
    swapped = me % 2
    for pair in range(factors // (2 * GROUP)):
        at = (me // 2) ^ pair
        one, two = even_ref[at].astype(F32), odd_ref[at].astype(F32)
        padded[:channels, :span] = jnp.where(swapped == 1, two, one).astype(BF16)
        padded[:channels, span:] = jnp.where(swapped == 1, one, two).astype(BF16)
        halves = [dot(pick, padded[:, h * span : (h + 1) * span], NT) for h in range(2)]
        for lag in range(LAGS):
            cut = slice(lag * GROUP, (lag + 1) * GROUP)
            tile = jnp.concatenate([halves[0][cut], halves[1][cut]], 0).astype(BF16)
            for q in range(PHASES):
                first = q * factors + pair * 2 * GROUP
                stk_ref[first : first + 2 * GROUP, (lag + q) * LANES : (lag + q + 1) * LANES] = tile


def auto_body(plan, me_ref, even_ref, odd_ref, *refs):
    before, (stk_ref, auto_ref, padded) = refs[:-3], refs[-3:]
    factors = plan.factors
    lay_motifs(plan, me_ref, even_ref, odd_ref, stk_ref, padded)
    last = (PHASES - 1) * factors
    chunk = 2 * LANES
    shift = PHASES * LANES // chunk
    auto_ref[...] = before[0][...] if before else jnp.zeros_like(auto_ref)
    for u in range(plan.tiles * LANES // chunk):
        taps = min(u // shift + 1, REACH)
        cuts = [u - shift * a for a in range(taps)]
        left = [stk_ref[last : last + factors, c * chunk : (c + 1) * chunk] for c in cuts]
        auto_ref[: taps * factors, :] += dot(
            jnp.concatenate(left, 0), stk_ref[:, u * chunk : (u + 1) * chunk], NT
        )


def numer_body(plan, stk_ref, data_ref, *refs):
    before, numer_ref = refs[:-1], refs[-1]
    deep = PHASES * LANES
    for s in range(REACH + 1):
        rows = slice(s * CHUNKS, s * CHUNKS + plan.rows)
        part = dot(data_ref[rows, :], stk_ref[:, s * deep : (s + 1) * deep], NT)
        if s:
            numer_ref[...] += part
        else:
            numer_ref[...] = part + before[0][...] if before else part


def tail_part(plan, stk_ref, past, ahead):
    factors = plan.factors
    group = 2 * LANES // factors
    known = past[...]
    total = jnp.zeros((LAGS, LANES), F32)
    for first in range(0, LAGS, group):
        lags = range(first, first + group)
        rows = jnp.concatenate([known[LAGS - l : 2 * LAGS - l, :factors] for l in lags], 1)
        mat = jnp.concatenate([stk_ref[:factors, l * LANES : (l + 1) * LANES] for l in lags], 0)
        total += dot(rows.astype(BF16), mat)
    ahead[LAGS:, :] = total
    beyond = ahead[...]
    high = beyond.astype(BF16).astype(F32)
    low = beyond - high
    out = jnp.zeros((2 * LAGS, factors), F32)
    for first in range(0, LAGS, 2):
        lags = range(first, first + 2)
        rows = jnp.concatenate(
            [jnp.concatenate([part[l : l + LAGS] for l in lags], 1) for part in (high, low)], 0
        )
        mat = stk_ref[:factors, first * LANES : (first + 2) * LANES]
        out += dot(rows.astype(BF16), mat, NT)
    return out[:LAGS] + out[LAGS:]


def tail_body(plan, shards, me_ref, bits_ref, stks, out_ref, past, ahead):
    out_ref[...] = jnp.zeros_like(out_ref)

    @pl.when(me_ref[0] == shards - 1)
    def _():
        factors = plan.factors
        start = (plan.steps // PHASES + plan.edge) - (CHUNKS - 1) * plan.per
        ends = [
            bits_ref[row_tile(start + i), :].astype(F32)[CHUNKS - 1 :] for i in range(REACH)
        ]
        known = jnp.concatenate(ends, 0)
        past[...] = jnp.zeros_like(past)
        ahead[...] = jnp.zeros_like(ahead)
        for p in range(PHASES):
            part = known[:, p * factors : (p + 1) * factors]
            part = jnp.concatenate([part, jnp.zeros((REACH, LANES - factors), F32)], 1)
            past[pl.ds(p, REACH, stride=PHASES), :] = part
        over = sum(tail_part(plan, stk_ref, past, ahead) for stk_ref in stks)
        past[:LAGS, :] = jnp.concatenate([over, jnp.zeros((LAGS, LANES - factors), F32)], 1)
        out_ref[...] = jnp.concatenate(
            [past[pl.ds(p, REACH, stride=PHASES), :][:, :factors] for p in range(PHASES)], 1
        )


def taps_body(plan, auto_a, auto_b, high_ref, low_ref, line):
    factors, width = plan.factors, plan.width
    line[:, :width] = jnp.zeros((factors, width), F32)
    for a in range(REACH):
        rows = slice(a * factors, (a + 1) * factors)
        line[:, (REACH - a) * width : (REACH - a + 1) * width] = auto_a[rows, :] + auto_b[rows, :]
    zero = (REACH * PHASES + PHASES - 1) * factors
    back = [
        line[:, zero - d * factors : zero - (d - 1) * factors].T for d in range(1, PHASES)
    ]
    back.append(jnp.zeros((factors, factors), F32))
    line[:, (REACH + 1) * width :] = jnp.concatenate(back, 1)
    for s in range(REACH + 1):
        for p in range(PHASES):
            first = zero - (PHASES * s + p) * factors
            high, low = split(line[:, first : first + width])
            rows = slice(s * width + p * factors, s * width + (p + 1) * factors)
            high_ref[rows, :] = high
            low_ref[rows, :] = low


def conv_body(plan, offsets, bits_ref, high_ref, low_ref, *refs):
    before, out_ref = refs[:-1], refs[-1]
    width, rows = plan.width, plan.rows
    for i, s in enumerate(offsets):
        at = (REACH + s) * CHUNKS
        mat = slice(abs(s) * width, (abs(s) + 1) * width)
        dims = NN if s >= 0 else NT
        part = dot(bits_ref[at : at + rows, :], high_ref[mat, :], dims)
        part += dot(bits_ref[at : at + rows, :], low_ref[mat, :], dims)
        if i:
            out_ref[...] += part
        else:
            out_ref[...] = part + before[0][...] if before else part


def conv_tail_body(plan, shards, offsets, me_ref, bits_ref, high_ref, low_ref, stk_a, stk_b, *refs):
    out_ref, tail_ref, past, ahead = refs
    tail_body(plan, shards, me_ref, bits_ref, (stk_a, stk_b), tail_ref, past, ahead)
    conv_body(plan, offsets, bits_ref, high_ref, low_ref, out_ref)


def first_conv_body(plan, offsets, auto_a, auto_b, bits_ref, high_ref, low_ref, out_ref, line):
    taps_body(plan, auto_a, auto_b, high_ref, low_ref, line)
    conv_body(plan, offsets, bits_ref, high_ref, low_ref, out_ref)


def penalties(plan, scale, me_ref, grams, bits_ref, low_ref):
    factors, rows = plan.factors, plan.rows
    total = grams[0][...]
    if len(grams) > 1:
        here, far, both = (g[...] for g in grams[1:])
        odd = me_ref[1] == 1
        near = jnp.where(odd, far, here)
        next_one = jnp.where(odd, here, far)
        total = (total + near) + (next_one + both)
    r = lax.broadcasted_iota(jnp.int32, (factors, factors), 0)
    c = lax.broadcasted_iota(jnp.int32, (factors, factors), 1)
    off = jnp.where(r == c, 0.0, total) * scale
    blank = jnp.zeros((factors, factors), F32)
    high, low = split(
        jnp.concatenate(
            [
                jnp.concatenate([off if p == q else blank for q in range(PHASES)], 1)
                for p in range(PHASES)
            ],
            0,
        )
    )
    bits = bits_ref[REACH * CHUNKS : REACH * CHUNKS + rows, :]
    return dot(bits, high) + dot(bits, low) + dot(low_ref[...], high)


def new_tile(plan, shards, me_ref, m, x_ref, den_ref, numer, pen, tails):
    at = row_tile(m)
    den = den_ref[at, :] + pen[at, :]
    j = lax.broadcasted_iota(jnp.int32, den.shape, 0)
    end = (plan.steps // PHASES + plan.edge) - (CHUNKS - 1) * plan.per
    if end - REACH <= m < end:
        i = m - end + REACH
        over = tails[0][i : i + 1, :] + tails[1][i : i + 1, :]
        den -= jnp.where((j == CHUNKS - 1) & (me_ref[0] == shards - 1), over, 0.0)
    new = x_ref[at, :] * numer / den
    if m < plan.edge:
        new = jnp.where((j == 0) & (me_ref[0] == 0), 0.0, new)
    if m >= end:
        new = jnp.where((j == CHUNKS - 1) & (me_ref[0] == shards - 1), 0.0, new)
    return new


def update_body(plan, scale, shards, counts, me_ref, x_ref, bits_ref, low_ref, den_ref, *refs):
    numers, tails, grams = refs[: counts[0]], refs[counts[0] :][:2], refs[counts[0] + 2 :][: counts[1]]
    refs = refs[counts[0] + 2 + counts[1] :]
    if counts[0] > 1:
        numer_ref, refs = refs[0], refs[1:]
    out_ref, out_bits, out_low, gram_ref, pen, both = refs
    factors, width = plan.factors, plan.width
    pen[...] = penalties(plan, scale, me_ref, grams, bits_ref, low_ref)
    end = (plan.steps // PHASES + plan.edge) - (CHUNKS - 1) * plan.per
    for m in range(plan.per):
        at = row_tile(m)
        numer = numers[0][at, :]
        if counts[0] > 1:
            numer = numer + numers[1][at, :]
            numer_ref[at, :] = numer
        new = new_tile(plan, shards, me_ref, m, x_ref, den_ref, numer, pen, tails)
        out_ref[at, :] = new
        spread(plan, new, m, out_bits)
        high, low = split(new)
        out_low[at, :] = low
        j = lax.broadcasted_iota(jnp.int32, new.shape, 0)
        kept = new
        if m < plan.edge:
            kept = jnp.where(j == 0, 0.0, kept)
        if m >= end:
            kept = jnp.where(j == CHUNKS - 1, 0.0, kept)
        high, low = split(kept)
        both[at, :width] = high
        both[at, width:] = low
    full = dot(both[:, :width], both[...], TN)
    cross = full[:, width:]
    full = full[:, :width] + cross + cross.T
    gram_ref[...] = sum(
        full[p * factors : (p + 1) * factors, p * factors : (p + 1) * factors] for p in range(PHASES)
    )


def last_body(plan, scale, shards, counts, me_ref, x_ref, bits_ref, low_ref, den_ref, *refs):
    numers, tails, grams = refs[: counts[0]], refs[counts[0] :][:2], refs[counts[0] + 2 :][: counts[1]]
    out_ref, pen, buf = refs[counts[0] + 2 + counts[1] :]
    pen[...] = penalties(plan, scale, me_ref, grams, bits_ref, low_ref)
    for m in range(plan.per):
        numer = sum(n[row_tile(m), :] for n in numers)
        new = new_tile(plan, shards, me_ref, m, x_ref, den_ref, numer, pen, tails)
        for h, lanes in enumerate(lane_tiles(PHASES // 2)):
            at = PHASES * m + 2 * h
            buf[pl.ds(at, CHUNKS, stride=plan.stride), :] = new[:, lanes]
            turn = pltpu.roll(new[:, lanes], LANES // 2, 1)
            buf[pl.ds(at + 1, CHUNKS, stride=plan.stride), :] = turn
    for i, lanes in enumerate(lane_tiles(plan.steps // LANES)):
        at = plan.front + i * LANES
        out_ref[:, lanes] = buf[at : at + LANES, :].T[: plan.factors, :]


def swap(x, axis, bit):
    count = lax.axis_size(axis)
    return lax.ppermute(x, axis, [(i, i ^ bit) for i in range(count)])


def mixed(x, bit_even, bit_odd):
    wide = lax.axis_size("chan")
    pairs = []
    for t in range(lax.axis_size("tm")):
        for c in range(wide):
            far = t ^ (bit_odd if c % 2 else bit_even)
            pairs.append((t * wide + c, far * wide + c))
    return lax.ppermute(x, ("tm", "chan"), pairs)


def shifted(x, axis, by):
    count = lax.axis_size(axis)
    return lax.ppermute(x, axis, [(i, i + by) for i in range(count) if 0 <= i + by < count])


def between(x, axis):
    count = lax.axis_size(axis)
    pairs = [(i, i + 1) for i in range(1, count - 1, 2)]
    return lax.ppermute(x, axis, pairs + [(b, a) for a, b in pairs])


def doubling(axis):
    count = lax.axis_size(axis)
    bits = [1 << b for b in range(count.bit_length() - 1)]
    return bits[1:] + bits[:1]


def after(x, *others):
    return lax.optimization_barrier((x, *others))[0]


def gram_rounds(x, odd, *meanwhile):
    bits = doubling("tm")
    singles, pairs = bits[-1:], bits[:-1]
    if len(pairs) % 2:
        singles, pairs = singles + pairs[-1:], pairs[:-1]
    gaps = list(meanwhile)

    def gap(*values):
        others = gaps.pop(0) if gaps else ()
        return lax.optimization_barrier(values + others)[: len(values)]

    for bit in singles:
        x = x + gap(swap(x, "tm", bit))[0]
    terms = [x]
    while pairs:
        one, two, pairs = pairs[0], pairs[1], pairs[2:]
        here, both = gap(mixed(x, one, two), swap(x, "tm", one ^ two))
        far = swap(here, "chan", 1)
        terms = [x, here, far, both]
        if pairs:
            near, other = jnp.where(odd, far, here), jnp.where(odd, here, far)
            x = (x + near) + (other + both)
    return terms


def on_device(data, motifs, loadings):
    channels, steps = data.shape
    factors = loadings.shape[0]
    plan = Plan(steps, factors)
    shards = lax.axis_size("tm")
    width, rows = plan.width, plan.rows
    ext_rows = plan.ext * CHUNKS
    sds = jax.ShapeDtypeStruct
    place = jnp.stack([lax.axis_index("tm"), lax.axis_index("chan") % 2]).astype(jnp.int32)
    odd = place[1] == 1

    rim = sds((factors + channels, LANES), F32)
    even, gram, near_rim, wide_rim = call(
        functools.partial(first_body, plan),
        (
            sds((1,) + motifs.shape, BF16),
            sds((factors, factors), F32),
            rim,
            rim,
        ),
        smem() + [pl.BlockSpec(memory_space=pltpu.HBM)] * 3,
        [
            pltpu.VMEM(loadings.shape, F32),
            pltpu.VMEM(data.shape, BF16),
            pltpu.SemaphoreType.DMA((3,)),
        ],
        limit=53,
    )(place, loadings, data, motifs)

    start = place
    bits = doubling("tm")
    for i, bit in enumerate(bits[:-1]):
        near = swap(even if i else motifs[None], "tm", bit)
        if i:
            gram_near = swap(gram, "tm", bits[i - 1])
            if i == 1:
                wide_rim = between(wide_rim, "tm")
                far_data = swap(after(data, even), "chan", 2)
                near, gram_near, wide_rim = lax.optimization_barrier((near, gram_near, wide_rim))
            else:
                near, gram_near = lax.optimization_barrier((near, gram_near))
            gram = gram + gram_near
        even = jnp.concatenate([even, near], 0)
    odds = swap(even, "tm", bits[-1])
    far_even = swap(even, "chan", 2)
    gram_near = swap(gram, "tm", bits[-2])
    near_rim = swap(after(near_rim, even), "tm", 1)
    odds, far_even, gram_near, near_rim, far_data = lax.optimization_barrier(
        (odds, far_even, gram_near, near_rim, far_data)
    )
    gram = gram + gram_near
    gram_near = swap(gram, "tm", bits[-1])
    right_side = lax.axis_index("tm") % 2 == 1
    left = jnp.where(right_side, near_rim, wide_rim)
    right = jnp.where(right_side, wide_rim, near_rim)
    if motifs.shape[1] != GROUP * LAGS:
        order = [0]
        for bit in bits:
            order = order + [o ^ bit for o in order]
        slots = jnp.concatenate([even, odds], 0)
        index = jnp.array([order.index(b) for b in range(shards)], jnp.int32)
        slots = jnp.take(slots, jnp.take(index, jnp.arange(shards) ^ place[0]), axis=0)
        slots = jnp.moveaxis(slots, 0, 1).reshape(channels, -1, GROUP * LAGS)
        slots = jnp.moveaxis(slots, 1, 0)
        even, odds = slots[0::2], slots[1::2]
        start = place * 0
        far_even = swap(even, "chan", 2)

    rims = jnp.concatenate([left[factors:], right[factors:]], 1).astype(BF16)
    far_odds = swap(jnp.concatenate([odds, rims[None]], 0), "chan", 2)
    far_odds, gram_near = lax.optimization_barrier((far_odds, gram_near))
    gram = gram + gram_near
    far_rims = far_odds[-1]

    lay = call(
        functools.partial(lay_data, plan),
        sds(((plan.per + REACH) * CHUNKS, PHASES * LANES), BF16),
        vmem(2),
        [pltpu.VMEM((steps + 2 * LANES, LANES), F32)],
    )

    def autos(evens, odd_ones, *before):
        return call(
            functools.partial(auto_body, plan),
            (sds((width, plan.tiles * LANES), BF16), sds((REACH * factors, width), F32)),
            smem() + vmem(2 + len(before)),
            [pltpu.VMEM((LANES, 2 * GROUP * LAGS), BF16)],
        )(start, evens, odd_ones, *before)

    def numers(stk, laid, *before):
        return call(
            functools.partial(numer_body, plan), sds((rows, width), F32), vmem(2 + len(before))
        )(stk, laid, *before)

    stk, auto = autos(even, odds)
    numer = numers(stk, lay(data, rims))
    far_odds, numer = lax.optimization_barrier((far_odds, numer))
    far_stk, auto = autos(far_even, far_odds, auto)
    far_data, far_rims, auto = lax.optimization_barrier((far_data, far_rims, auto))
    auto_far = swap(auto, "chan", 1)
    field, window = sds((rows, width), F32), sds((ext_rows, width), BF16)
    low_field, rest = sds((rows, width), BF16), sds((REACH, width), F32)
    tail_room = [pltpu.VMEM((2 * LAGS, LANES), F32)] * 2
    x, bits_x, low_x, tail = call(
        functools.partial(lay_loadings, plan, shards),
        (field, window, low_field, rest),
        smem() + vmem(5),
        [pltpu.VMEM((steps + 2 * LANES, LANES), F32)] + tail_room,
    )(place, loadings, left, right, stk, far_stk)
    far_laid = lay(far_data, far_rims)
    far_laid, auto_far, x = lax.optimization_barrier((far_laid, auto_far, x))
    numer = numers(far_stk, far_laid, numer)
    numer_far = swap(numer, "chan", 1)
    grams = [gram]

    mats = sds(((REACH + 1) * width, width), BF16)
    every = list(range(-REACH, REACH + 1))
    high, low, den = call(
        functools.partial(first_conv_body, plan, every),
        (mats, mats, sds((rows, width), F32)),
        vmem(3),
        [pltpu.VMEM((factors, (REACH + 2) * width), F32)],
    )(auto, auto_far, bits_x)

    def conv(offsets, bits_now, before):
        return call(functools.partial(conv_body, plan, offsets), field, vmem(4))(
            bits_now, high, low, before
        )

    def conv_tail(offsets, bits_now):
        return call(
            functools.partial(conv_tail_body, plan, shards, offsets),
            (field, rest),
            smem() + vmem(5),
            tail_room,
        )(place, bits_now, high, low, stk, far_stk)

    scale = PENALTY / (steps * shards)
    numers_now = (numer, numer_far)
    for sweep in range(ITERS):
        if sweep:
            part, tail = conv_tail(every[:REACH], bits_x)
            tails = (tail, swap(tail, "chan", 1))
            den = conv(every[REACH:], bits_x, part)
            grams = gram_rounds(gram, odd, (part,), (den, tails[1]))
        else:
            tails = (tail, swap(tail, "chan", 1))
        operands = (place, x, bits_x, low_x, den, *numers_now, *tails, *grams)
        counts = (len(numers_now), len(grams))
        if sweep == ITERS - 1:
            return call(
                functools.partial(last_body, plan, scale, shards, counts),
                sds((factors, steps), F32),
                smem() + vmem(len(operands) - 1),
                [pltpu.VMEM((rows, width), F32), pltpu.VMEM((steps + 2 * LANES, LANES), F32)],
            )(*operands)
        outs = (field, window, low_field, sds((factors, factors), F32))
        if counts[0] > 1:
            outs = (field,) + outs
        got = call(
            functools.partial(update_body, plan, scale, shards, counts),
            outs,
            smem() + vmem(len(operands) - 1),
            [pltpu.VMEM((rows, width), F32), pltpu.VMEM((rows, 2 * width), BF16)],
        )(*operands)
        if counts[0] > 1:
            numers_now, got = got[:1], got[1:]
        x, bits_x, low_x, gram = got


def solution(mesh):
    in_specs = (P("chan", "tm"), P("chan", "tm"), P(None, "tm"))
    out_specs = P(None, "tm")
    return jax.shard_map(
        on_device, mesh=mesh, in_specs=in_specs, out_specs=out_specs, check_vma=False
    )
```

```python
import functools

import jax
import jax.numpy as jnp
from jax import lax
from jax.experimental import pallas as pl
from jax.experimental.pallas import tpu as pltpu
from jax.sharding import PartitionSpec as P

LAGS = 32
ITERS = 3
PENALTY = 0.2

PHASES = 4
CHUNKS = 16
REACH = LAGS // PHASES
LANES = 128
GROUP = 8

NT = (((1,), (1,)), ((), ()))
NN = (((1,), (0,)), ((), ()))
TN = (((0,), (0,)), ((), ()))
F32 = jnp.float32
BF16 = jnp.bfloat16


def dot(a, b, dims=NN):
    return lax.dot_general(a, b, dims, preferred_element_type=F32)


def split(a):
    high = a.astype(BF16)
    return high, (a - high.astype(F32)).astype(BF16)


def vmem(n=1):
    return [pl.BlockSpec(memory_space=pltpu.VMEM)] * n


def smem(n=1):
    return [pl.BlockSpec(memory_space=pltpu.SMEM)] * n


def call(body, out_shape, in_specs, scratch=(), flops=0, moved=0, limit=16):
    return pl.pallas_call(
        body,
        out_shape=out_shape,
        in_specs=in_specs,
        out_specs=jax.tree.map(lambda _: pl.BlockSpec(memory_space=pltpu.VMEM), out_shape),
        scratch_shapes=list(scratch),
        compiler_params=pltpu.CompilerParams(vmem_limit_bytes=limit * 2**20),
        cost_estimate=pl.CostEstimate(flops=flops, bytes_accessed=moved, transcendentals=0),
    )


class Plan:
    def __init__(self, steps, factors):
        self.steps = steps
        self.factors = factors
        self.width = PHASES * factors
        self.edge = 2 * REACH
        self.rows = steps // PHASES + 2 * self.edge
        self.per = self.rows // CHUNKS
        self.ext = self.per + 2 * REACH
        self.stride = PHASES * self.per
        self.halo = PHASES * (self.edge + REACH)
        self.front = PHASES * self.edge
        self.back = PHASES * (self.edge + REACH)
        wide = steps + 2 * self.halo
        self.wide = -(-wide // LANES) * LANES
        self.tiles = LAGS + PHASES


def lane_tiles(count):
    return [slice(i * LANES, (i + 1) * LANES) for i in range(count)]


def row_tile(m):
    return slice(m * CHUNKS, (m + 1) * CHUNKS)


def turned(buf, left, middle, right, tiles):
    parts = [left] + [middle[:, at] for at in lane_tiles(tiles)] + [right]
    for i, part in enumerate(parts):
        part = part.astype(F32)
        spare = LANES - part.shape[0]
        low = part if spare == part.shape[0] else jnp.zeros((spare, LANES), F32)
        buf[i * LANES : (i + 1) * LANES, :] = jnp.concatenate([part, low], 0).T


def spread(plan, tile, m, bits_ref):
    j = lax.broadcasted_iota(jnp.int32, tile.shape, 0)
    bits_ref[row_tile(m + REACH), :] = tile.astype(BF16)
    if m >= plan.per - REACH:
        low = jnp.where(j == 0, 0.0, pltpu.roll(tile, 1, 0))
        bits_ref[row_tile(m - plan.per + REACH), :] = low.astype(BF16)
    if m < REACH:
        high = jnp.where(j == CHUNKS - 1, 0.0, pltpu.roll(tile, CHUNKS - 1, 0))
        bits_ref[row_tile(m + plan.per + REACH), :] = high.astype(BF16)


def lay_loadings(plan, load_ref, left_ref, right_ref, x_ref, bits_ref, low_ref, buf):
    factors = plan.factors
    turned(buf, left_ref[:factors, :], load_ref, right_ref[:factors, :], plan.steps // LANES)
    lane = lax.broadcasted_iota(jnp.int32, (CHUNKS, LANES), 1)
    skip = LANES - plan.halo
    for m in range(plan.ext):
        halves = []
        for h in range(PHASES // 2):
            at = skip + PHASES * m + 2 * h
            even = buf[pl.ds(at, CHUNKS, stride=plan.stride), :]
            odd = buf[pl.ds(at + 1, CHUNKS, stride=plan.stride), :]
            halves.append(jnp.where(lane < factors, even, odd))
        tile = jnp.concatenate(halves, 1)
        bits = tile.astype(BF16)
        bits_ref[row_tile(m), :] = bits
        if REACH <= m < REACH + plan.per:
            x_ref[row_tile(m - REACH), :] = tile
            low_ref[row_tile(m - REACH), :] = (tile - bits.astype(F32)).astype(BF16)


def lay_data(plan, data_ref, rims_ref, out_ref, buf):
    turned(buf, rims_ref[:, :LANES], data_ref, rims_ref[:, LANES:], plan.steps // LANES)
    skip = LANES - plan.front
    for m in range(plan.per + REACH):
        for p, at in enumerate(lane_tiles(PHASES)):
            rows = pl.ds(skip + PHASES * m + p, CHUNKS, stride=plan.stride)
            out_ref[row_tile(m), at] = buf[rows, :].astype(BF16)


def first_body(plan, load_any, data_any, motif_any, *refs):
    data_ref, motif_ref, gram_ref, near_ref, wide_ref, load_ref, sems = refs
    factors = plan.factors
    moves = [
        pltpu.make_async_copy(source, target, sems.at[i])
        for i, (source, target) in enumerate(
            ((load_any, load_ref), (data_any, data_ref), (motif_any, motif_ref.at[0]))
        )
    ]
    for move in moves:
        move.start()
    for move in moves:
        move.wait()
    odd = lax.axis_index("tm") % 2 == 1
    head, tail = slice(0, LANES), slice(plan.steps - LANES, plan.steps)
    for rim_ref, even_at, odd_at in ((near_ref, tail, head), (wide_ref, head, tail)):
        rim_ref[:factors, :] = jnp.where(odd, load_ref[:, odd_at], load_ref[:, even_at])
        rim_ref[factors:, :] = jnp.where(
            odd, data_ref[:, odd_at].astype(F32), data_ref[:, even_at].astype(F32)
        )
    high, low = split(load_ref[...])
    cross = dot(high, low, NT)
    gram_ref[...] = dot(high, high, NT) + cross + cross.T


def lay_motifs(plan, me, even_ref, odd_ref, stk_ref, padded):
    factors = plan.factors
    channels = even_ref.shape[1]
    span = GROUP * LAGS
    padded[channels:, :] = jnp.zeros((LANES - channels, padded.shape[1]), BF16)
    row = lax.broadcasted_iota(jnp.int32, (span, span), 0)
    col = lax.broadcasted_iota(jnp.int32, (span, span), 1)
    pick = jnp.where(col == (row % GROUP) * LAGS + row // GROUP, 1.0, 0.0).astype(BF16)
    for q in range(PHASES):
        rows = slice(q * factors, (q + 1) * factors)
        if q:
            stk_ref[rows, : q * LANES] = jnp.zeros((factors, q * LANES), BF16)
        stk_ref[rows, (LAGS + q) * LANES :] = jnp.zeros((factors, (PHASES - q) * LANES), BF16)
    swapped = me % 2
    for pair in range(factors // (2 * GROUP)):
        at = (me // 2) ^ pair
        one, two = even_ref[at].astype(F32), odd_ref[at].astype(F32)
        room = slice(2 * pair * span, (2 * pair + 1) * span), slice((2 * pair + 1) * span, (2 * pair + 2) * span)
        padded[:channels, room[0]] = jnp.where(swapped == 1, two, one).astype(BF16)
        padded[:channels, room[1]] = jnp.where(swapped == 1, one, two).astype(BF16)
        halves = [dot(pick, padded[:, at], NT) for at in room]
        for lag in range(LAGS):
            cut = slice(lag * GROUP, (lag + 1) * GROUP)
            tile = jnp.concatenate([halves[0][cut], halves[1][cut]], 0).astype(BF16)
            for q in range(PHASES):
                first = q * factors + pair * 2 * GROUP
                stk_ref[first : first + 2 * GROUP, (lag + q) * LANES : (lag + q + 1) * LANES] = tile


def auto_body(plan, moved, even_ref, odd_ref, *refs):
    before, (stk_ref, auto_ref, padded) = refs[:-3], refs[-3:]
    factors = plan.factors
    me = lax.axis_index("tm") if moved else 0
    lay_motifs(plan, me, even_ref, odd_ref, stk_ref, padded)
    last = (PHASES - 1) * factors
    deep = PHASES * LANES
    auto_ref[...] = before[0][...] if before else jnp.zeros_like(auto_ref)
    for u in range(REACH + 1):
        taps = min(u + 1, REACH)
        cuts = [slice((u - a) * deep, (u - a + 1) * deep) for a in range(taps)]
        left = jnp.concatenate([stk_ref[last : last + factors, cut] for cut in cuts], 0)
        auto_ref[: taps * factors, :] += dot(left, stk_ref[:, u * deep : (u + 1) * deep], NT)


def numer_body(plan, stk_ref, data_ref, numer_ref, before=None):
    deep = PHASES * LANES
    for s in range(REACH + 1):
        rows = slice(s * CHUNKS, s * CHUNKS + plan.rows)
        part = dot(data_ref[rows, :], stk_ref[:, s * deep : (s + 1) * deep], NT)
        if s:
            numer_ref[...] += part
        else:
            numer_ref[...] = part if before is None else part + before[...]


def numer_tail_body(plan, shards, stk_a, stk_b, data_ref, before, bits_ref, *refs):
    numer_ref, tail_ref, past, ahead = refs
    tail_body(plan, shards, bits_ref, (stk_a, stk_b), tail_ref, past, ahead)
    numer_body(plan, stk_b, data_ref, numer_ref, before)


def tail_part(plan, stk_ref, past, ahead):
    factors = plan.factors
    group = 2 * LANES // factors
    known = past[...]
    total = jnp.zeros((LAGS, LANES), F32)
    for first in range(0, LAGS, group):
        lags = range(first, first + group)
        rows = jnp.concatenate([known[LAGS - l : 2 * LAGS - l, :factors] for l in lags], 1)
        mat = jnp.concatenate([stk_ref[:factors, l * LANES : (l + 1) * LANES] for l in lags], 0)
        total += dot(rows.astype(BF16), mat)
    ahead[LAGS:, :] = total
    beyond = ahead[...]
    high = beyond.astype(BF16).astype(F32)
    low = beyond - high
    out = jnp.zeros((2 * LAGS, factors), F32)
    for first in range(0, LAGS, 2):
        lags = range(first, first + 2)
        rows = jnp.concatenate(
            [jnp.concatenate([part[l : l + LAGS] for l in lags], 1) for part in (high, low)], 0
        )
        mat = stk_ref[:factors, first * LANES : (first + 2) * LANES]
        out += dot(rows.astype(BF16), mat, NT)
    return out[:LAGS] + out[LAGS:]


def tail_body(plan, shards, bits_ref, stks, out_ref, past, ahead):
    out_ref[...] = jnp.zeros_like(out_ref)

    @pl.when(lax.axis_index("tm") == shards - 1)
    def _():
        factors = plan.factors
        start = (plan.steps // PHASES + plan.edge) - (CHUNKS - 1) * plan.per
        ends = [
            bits_ref[row_tile(start + i), :].astype(F32)[CHUNKS - 1 :] for i in range(REACH)
        ]
        known = jnp.concatenate(ends, 0)
        past[...] = jnp.zeros_like(past)
        ahead[...] = jnp.zeros_like(ahead)
        for p in range(PHASES):
            part = known[:, p * factors : (p + 1) * factors]
            part = jnp.concatenate([part, jnp.zeros((REACH, LANES - factors), F32)], 1)
            past[pl.ds(p, REACH, stride=PHASES), :] = part
        over = sum(tail_part(plan, stk_ref, past, ahead) for stk_ref in stks)
        past[:LAGS, :] = jnp.concatenate([over, jnp.zeros((LAGS, LANES - factors), F32)], 1)
        out_ref[...] = jnp.concatenate(
            [past[pl.ds(p, REACH, stride=PHASES), :][:, :factors] for p in range(PHASES)], 1
        )


def taps_body(plan, auto_a, auto_b, high_ref, low_ref, line):
    factors, width = plan.factors, plan.width
    line[:, :width] = jnp.zeros((factors, width), F32)
    for a in range(REACH):
        rows = slice(a * factors, (a + 1) * factors)
        line[:, (REACH - a) * width : (REACH - a + 1) * width] = auto_a[rows, :] + auto_b[rows, :]
    zero = (REACH * PHASES + PHASES - 1) * factors
    back = [
        line[:, zero - d * factors : zero - (d - 1) * factors].T for d in range(1, PHASES)
    ]
    back.append(jnp.zeros((factors, factors), F32))
    line[:, (REACH + 1) * width :] = jnp.concatenate(back, 1)
    for s in range(REACH + 1):
        for p in range(PHASES):
            first = zero - (PHASES * s + p) * factors
            high, low = split(line[:, first : first + width])
            rows = slice(s * width + p * factors, s * width + (p + 1) * factors)
            high_ref[rows, :] = high
            low_ref[rows, :] = low


def conv_body(plan, offsets, bits_ref, high_ref, low_ref, *refs):
    before, out_ref = refs[:-1], refs[-1]
    width, rows = plan.width, plan.rows
    for i, s in enumerate(offsets):
        at = (REACH + s) * CHUNKS
        mat = slice(abs(s) * width, (abs(s) + 1) * width)
        dims = NN if s >= 0 else NT
        part = dot(bits_ref[at : at + rows, :], high_ref[mat, :], dims)
        part += dot(bits_ref[at : at + rows, :], low_ref[mat, :], dims)
        if i:
            out_ref[...] += part
        else:
            out_ref[...] = part + before[0][...] if before else part


def conv_tail_body(plan, shards, offsets, bits_ref, high_ref, low_ref, stk_a, stk_b, *refs):
    out_ref, tail_ref, past, ahead = refs
    tail_body(plan, shards, bits_ref, (stk_a, stk_b), tail_ref, past, ahead)
    conv_body(plan, offsets, bits_ref, high_ref, low_ref, out_ref)


def first_conv_body(plan, offsets, auto_a, auto_b, bits_ref, high_ref, low_ref, out_ref, line):
    taps_body(plan, auto_a, auto_b, high_ref, low_ref, line)
    conv_body(plan, offsets, bits_ref, high_ref, low_ref, out_ref)


def penalties(plan, scale, grams, bits_ref, low_ref):
    factors, rows = plan.factors, plan.rows
    total = grams[0][...]
    if len(grams) > 1:
        here, far, both = (g[...] for g in grams[1:])
        odd = lax.axis_index("chan") % 2 == 1
        near = jnp.where(odd, far, here)
        next_one = jnp.where(odd, here, far)
        total = (total + near) + (next_one + both)
    r = lax.broadcasted_iota(jnp.int32, (factors, factors), 0)
    c = lax.broadcasted_iota(jnp.int32, (factors, factors), 1)
    off = jnp.where(r == c, 0.0, total) * scale
    blank = jnp.zeros((factors, factors), F32)
    high, low = split(
        jnp.concatenate(
            [
                jnp.concatenate([off if p == q else blank for q in range(PHASES)], 1)
                for p in range(PHASES)
            ],
            0,
        )
    )
    bits = bits_ref[REACH * CHUNKS : REACH * CHUNKS + rows, :]
    return dot(bits, high) + dot(bits, low) + dot(low_ref[...], high)


def new_tile(plan, shards, me, m, x_ref, den_ref, numer, pen, tails):
    at = row_tile(m)
    den = den_ref[at, :] + pen[at, :]
    j = lax.broadcasted_iota(jnp.int32, den.shape, 0)
    end = (plan.steps // PHASES + plan.edge) - (CHUNKS - 1) * plan.per
    if end - REACH <= m < end:
        i = m - end + REACH
        over = tails[0][i : i + 1, :] + tails[1][i : i + 1, :]
        den -= jnp.where((j == CHUNKS - 1) & (me == shards - 1), over, 0.0)
    new = x_ref[at, :] * numer / den
    if m < plan.edge:
        new = jnp.where((j == 0) & (me == 0), 0.0, new)
    if m >= end:
        new = jnp.where((j == CHUNKS - 1) & (me == shards - 1), 0.0, new)
    return new


def update_body(plan, scale, shards, counts, x_ref, bits_ref, low_ref, den_ref, *refs):
    numers, tails, grams = refs[: counts[0]], refs[counts[0] :][:2], refs[counts[0] + 2 :][: counts[1]]
    refs = refs[counts[0] + 2 + counts[1] :]
    if counts[0] > 1:
        numer_ref, refs = refs[0], refs[1:]
    out_ref, out_bits, out_low, gram_ref, pen, both = refs
    factors, width = plan.factors, plan.width
    me = lax.axis_index("tm")
    pen[...] = penalties(plan, scale, grams, bits_ref, low_ref)
    end = (plan.steps // PHASES + plan.edge) - (CHUNKS - 1) * plan.per
    for m in range(plan.per):
        at = row_tile(m)
        numer = numers[0][at, :]
        if counts[0] > 1:
            numer = numer + numers[1][at, :]
            numer_ref[at, :] = numer
        new = new_tile(plan, shards, me, m, x_ref, den_ref, numer, pen, tails)
        out_ref[at, :] = new
        spread(plan, new, m, out_bits)
        high, low = split(new)
        out_low[at, :] = low
        j = lax.broadcasted_iota(jnp.int32, new.shape, 0)
        kept = new
        if m < plan.edge:
            kept = jnp.where(j == 0, 0.0, kept)
        if m >= end:
            kept = jnp.where(j == CHUNKS - 1, 0.0, kept)
        high, low = split(kept)
        both[at, :width] = high
        both[at, width:] = low
    same, cross = 0.0, 0.0
    for lanes in lane_tiles(width // LANES):
        ahead = slice(width + lanes.start, width + lanes.stop)
        full = dot(both[:, lanes], jnp.concatenate([both[:, lanes], both[:, ahead]], 1), TN)
        for p in range(LANES // factors):
            at = slice(p * factors, (p + 1) * factors)
            same += full[at, at]
            cross += full[at, LANES + at.start : LANES + at.stop]
    gram_ref[...] = same + cross + cross.T


def last_body(plan, scale, shards, counts, x_ref, bits_ref, low_ref, den_ref, *refs):
    numers, tails, grams = refs[: counts[0]], refs[counts[0] :][:2], refs[counts[0] + 2 :][: counts[1]]
    out_ref, pen, buf = refs[counts[0] + 2 + counts[1] :]
    me = lax.axis_index("tm")
    pen[...] = penalties(plan, scale, grams, bits_ref, low_ref)
    for m in range(plan.per):
        numer = sum(n[row_tile(m), :] for n in numers)
        new = new_tile(plan, shards, me, m, x_ref, den_ref, numer, pen, tails)
        for h, lanes in enumerate(lane_tiles(PHASES // 2)):
            at = PHASES * m + 2 * h
            buf[pl.ds(at, CHUNKS, stride=plan.stride), :] = new[:, lanes]
            turn = pltpu.roll(new[:, lanes], LANES // 2, 1)
            buf[pl.ds(at + 1, CHUNKS, stride=plan.stride), :] = turn
    for i, lanes in enumerate(lane_tiles(plan.steps // LANES)):
        at = plan.front + i * LANES
        out_ref[:, lanes] = buf[at : at + LANES, :].T[: plan.factors, :]


def swap(x, axis, bit):
    count = lax.axis_size(axis)
    return lax.ppermute(x, axis, [(i, i ^ bit) for i in range(count)])


def mixed(x, bit_even, bit_odd):
    wide = lax.axis_size("chan")
    pairs = []
    for t in range(lax.axis_size("tm")):
        for c in range(wide):
            far = t ^ (bit_odd if c % 2 else bit_even)
            pairs.append((t * wide + c, far * wide + c))
    return lax.ppermute(x, ("tm", "chan"), pairs)


def shifted(x, axis, by):
    count = lax.axis_size(axis)
    return lax.ppermute(x, axis, [(i, i + by) for i in range(count) if 0 <= i + by < count])


def between(x, axis):
    count = lax.axis_size(axis)
    pairs = [(i, i + 1) for i in range(1, count - 1, 2)]
    return lax.ppermute(x, axis, pairs + [(b, a) for a, b in pairs])


def doubling(axis):
    count = lax.axis_size(axis)
    bits = [1 << b for b in range(count.bit_length() - 1)]
    return bits[1:] + bits[:1]


def after(x, *others):
    return lax.optimization_barrier((x, *others))[0]


def gram_rounds(x, odd, *meanwhile):
    bits = doubling("tm")
    singles, pairs = bits[-1:], bits[:-1]
    if len(pairs) % 2:
        singles, pairs = singles + pairs[-1:], pairs[:-1]
    gaps = list(meanwhile)

    def gap(*values):
        others = gaps.pop(0) if gaps else ()
        return lax.optimization_barrier(values + others)[: len(values)]

    for bit in singles:
        x = x + gap(swap(x, "tm", bit))[0]
    terms = [x]
    while pairs:
        one, two, pairs = pairs[0], pairs[1], pairs[2:]
        here, both = gap(mixed(x, one, two), swap(x, "tm", one ^ two))
        far = swap(here, "chan", 1)
        terms = [x, here, far, both]
        if pairs:
            near, other = jnp.where(odd, far, here), jnp.where(odd, here, far)
            x = (x + near) + (other + both)
    return terms


def on_device(data, motifs, loadings):
    channels, steps = data.shape
    factors = loadings.shape[0]
    plan = Plan(steps, factors)
    shards = lax.axis_size("tm")
    width, rows = plan.width, plan.rows
    ext_rows = plan.ext * CHUNKS
    sds = jax.ShapeDtypeStruct
    me = lax.axis_index("tm")
    odd = lax.axis_index("chan") % 2 == 1

    rim = sds((factors + channels, LANES), F32)
    data_in, even, gram, near_rim, wide_rim = call(
        functools.partial(first_body, plan),
        (
            sds(data.shape, BF16),
            sds((1,) + motifs.shape, BF16),
            sds((factors, factors), F32),
            rim,
            rim,
        ),
        [pl.BlockSpec(memory_space=pltpu.HBM)] * 3,
        [
            pltpu.VMEM(loadings.shape, F32),
            pltpu.SemaphoreType.DMA((3,)),
        ],
        limit=53,
    )(loadings, data, motifs)

    moved = motifs.shape[1] == GROUP * LAGS
    bits = doubling("tm")
    for i, bit in enumerate(bits[:-1]):
        near = swap(even if i else motifs[None], "tm", bit)
        if i:
            gram_near = swap(gram, "tm", bits[i - 1])
            if i == 1:
                wide_rim = between(wide_rim, "tm")
                far_data = swap(after(data_in, even), "chan", 2)
                near, gram_near, wide_rim, far_data = lax.optimization_barrier(
                (near, gram_near, wide_rim, far_data)
            )
            else:
                near, gram_near = lax.optimization_barrier((near, gram_near))
            gram = gram + gram_near
        even = jnp.concatenate([even, near], 0)
    odds = swap(even, "tm", bits[-1])
    far_even = swap(even, "chan", 2)
    gram_near = swap(gram, "tm", bits[-2])
    near_rim = swap(after(near_rim, even), "tm", 1)
    right_side = me % 2 == 1
    left = jnp.where(right_side, near_rim, wide_rim)
    right = jnp.where(right_side, wide_rim, near_rim)
    if not moved:
        order = [0]
        for bit in bits:
            order = order + [o ^ bit for o in order]
        slots = jnp.concatenate([even, odds], 0)
        index = jnp.array([order.index(b) for b in range(shards)], jnp.int32)
        slots = jnp.take(slots, jnp.take(index, jnp.arange(shards) ^ me), axis=0)
        slots = jnp.moveaxis(slots, 0, 1).reshape(channels, -1, GROUP * LAGS)
        slots = jnp.moveaxis(slots, 1, 0)
        even, odds = slots[0::2], slots[1::2]
        far_even = swap(even, "chan", 2)

    lay = call(
        functools.partial(lay_data, plan),
        sds(((plan.per + REACH) * CHUNKS, PHASES * LANES), BF16),
        vmem(2),
        [pltpu.VMEM((steps + 2 * LANES, LANES), F32)],
    )

    field, window = sds((rows, width), F32), sds((ext_rows, width), BF16)
    low_field, rest = sds((rows, width), BF16), sds((REACH, width), F32)
    tail_room = [pltpu.VMEM((2 * LAGS, LANES), F32)] * 2
    rims = jnp.concatenate([left[factors:], right[factors:]], 1).astype(BF16)
    own_laid = lay(data_in, rims)
    x, bits_x, low_x = call(
        functools.partial(lay_loadings, plan),
        (field, window, low_field),
        vmem(3),
        [pltpu.VMEM((steps + 2 * LANES, LANES), F32)],
    )(loadings, left, right)
    odds, far_even, gram_near, far_data, own_laid, x, bits_x = lax.optimization_barrier(
        (odds, far_even, gram_near, far_data, own_laid, x, bits_x)
    )
    gram = gram + gram_near
    gram_near = swap(gram, "tm", bits[-1])
    far_odds = swap(jnp.concatenate([odds, rims[None]], 0), "chan", 2)
    far_odds, gram_near = lax.optimization_barrier((far_odds, gram_near))
    gram = gram + gram_near
    far_rims = far_odds[-1]

    def autos(evens, odd_ones, *before):
        return call(
            functools.partial(auto_body, plan, moved),
            (sds((width, plan.tiles * LANES), BF16), sds((REACH * factors, width), F32)),
            vmem(2 + len(before)),
            [pltpu.VMEM((LANES, factors * LAGS), BF16)],
        )(evens, odd_ones, *before)

    stk, auto = autos(even, odds)
    numer = call(functools.partial(numer_body, plan), field, vmem(2))(stk, own_laid)
    far_odds, numer = lax.optimization_barrier((far_odds, numer))
    far_stk, auto = autos(far_even, far_odds, auto)
    far_data, far_rims, auto = lax.optimization_barrier((far_data, far_rims, auto))
    auto_far = swap(auto, "chan", 1)
    numer, tail = call(
        functools.partial(numer_tail_body, plan, shards),
        (field, rest),
        vmem(5),
        tail_room,
    )(stk, far_stk, lay(far_data, far_rims), numer, bits_x)
    numer, tail, auto_far = lax.optimization_barrier((numer, tail, auto_far))
    numer_far = swap(numer, "chan", 1)
    grams = [gram]

    mats = sds(((REACH + 1) * width, width), BF16)
    every = list(range(-REACH, REACH + 1))
    high, low, den = call(
        functools.partial(first_conv_body, plan, every),
        (mats, mats, sds((rows, width), F32)),
        vmem(3),
        [pltpu.VMEM((factors, (REACH + 2) * width), F32)],
    )(auto, auto_far, bits_x)

    def conv(offsets, bits_now, before):
        return call(functools.partial(conv_body, plan, offsets), field, vmem(4))(
            bits_now, high, low, before
        )

    def conv_tail(offsets, bits_now):
        return call(
            functools.partial(conv_tail_body, plan, shards, offsets),
            (field, rest),
            vmem(5),
            tail_room,
        )(bits_now, high, low, stk, far_stk)

    scale = PENALTY / (steps * shards)
    numers_now = (numer, numer_far)
    for sweep in range(ITERS):
        if sweep:
            part, tail = conv_tail(every[:REACH], bits_x)
            tails = (tail, swap(tail, "chan", 1))
            den = conv(every[REACH:], bits_x, part)
            grams = gram_rounds(gram, odd, (part,), (den, tails[1]))
        else:
            tails = (tail, swap(tail, "chan", 1))
        operands = (x, bits_x, low_x, den, *numers_now, *tails, *grams)
        counts = (len(numers_now), len(grams))
        if sweep == ITERS - 1:
            return call(
                functools.partial(last_body, plan, scale, shards, counts),
                sds((factors, steps), F32),
                vmem(len(operands)),
                [pltpu.VMEM((rows, width), F32), pltpu.VMEM((steps + 2 * LANES, LANES), F32)],
            )(*operands)
        outs = (field, window, low_field, sds((factors, factors), F32))
        if counts[0] > 1:
            outs = (field,) + outs
        got = call(
            functools.partial(update_body, plan, scale, shards, counts),
            outs,
            vmem(len(operands)),
            [pltpu.VMEM((rows, width), F32), pltpu.VMEM((rows, 2 * width), BF16)],
        )(*operands)
        if counts[0] > 1:
            numers_now, got = got[:1], got[1:]
        x, bits_x, low_x, gram = got


def solution(mesh):
    in_specs = (P("chan", "tm"), P("chan", "tm"), P(None, "tm"))
    out_specs = P(None, "tm")
    return jax.shard_map(
        on_device, mesh=mesh, in_specs=in_specs, out_specs=out_specs, check_vma=False
    )
```

```python
import functools

import jax
import jax.numpy as jnp
from jax import lax
from jax.experimental import pallas as pl
from jax.experimental.pallas import tpu as pltpu
from jax.sharding import PartitionSpec as P

LAGS = 32
ITERS = 3
PENALTY = 0.2

PHASES = 4
CHUNKS = 16
REACH = LAGS // PHASES
LANES = 128
GROUP = 8

NT = (((1,), (1,)), ((), ()))
NN = (((1,), (0,)), ((), ()))
TN = (((0,), (0,)), ((), ()))
F32 = jnp.float32
BF16 = jnp.bfloat16


def dot(a, b, dims=NN):
    return lax.dot_general(a, b, dims, preferred_element_type=F32)


def split(a):
    high = a.astype(BF16)
    return high, (a - high.astype(F32)).astype(BF16)


def vmem(n=1):
    return [pl.BlockSpec(memory_space=pltpu.VMEM)] * n


def smem(n=1):
    return [pl.BlockSpec(memory_space=pltpu.SMEM)] * n


def call(body, out_shape, in_specs, scratch=(), flops=0, moved=0, limit=16):
    return pl.pallas_call(
        body,
        out_shape=out_shape,
        in_specs=in_specs,
        out_specs=jax.tree.map(lambda _: pl.BlockSpec(memory_space=pltpu.VMEM), out_shape),
        scratch_shapes=list(scratch),
        compiler_params=pltpu.CompilerParams(vmem_limit_bytes=limit * 2**20),
        cost_estimate=pl.CostEstimate(flops=flops, bytes_accessed=moved, transcendentals=0),
    )


class Plan:
    def __init__(self, steps, factors):
        self.steps = steps
        self.factors = factors
        self.width = PHASES * factors
        self.edge = 2 * REACH
        self.rows = steps // PHASES + 2 * self.edge
        self.per = self.rows // CHUNKS
        self.ext = self.per + 2 * REACH
        self.stride = PHASES * self.per
        self.halo = PHASES * (self.edge + REACH)
        self.front = PHASES * self.edge
        self.back = PHASES * (self.edge + REACH)
        wide = steps + 2 * self.halo
        self.wide = -(-wide // LANES) * LANES
        self.tiles = LAGS + PHASES


def lane_tiles(count):
    return [slice(i * LANES, (i + 1) * LANES) for i in range(count)]


def row_tile(m):
    return slice(m * CHUNKS, (m + 1) * CHUNKS)


def turned(buf, left, fields, right):
    middle = [field[:, at] for field in fields for at in lane_tiles(field.shape[1] // LANES)]
    parts = [left] + middle + [right]
    for i, part in enumerate(parts):
        part = part.astype(F32)
        spare = LANES - part.shape[0]
        low = part if spare == part.shape[0] else jnp.zeros((spare, LANES), F32)
        buf[i * LANES : (i + 1) * LANES, :] = jnp.concatenate([part, low], 0).T


def spread(plan, tile, m, bits_ref):
    j = lax.broadcasted_iota(jnp.int32, tile.shape, 0)
    bits_ref[row_tile(m + REACH), :] = tile.astype(BF16)
    if m >= plan.per - REACH:
        low = jnp.where(j == 0, 0.0, pltpu.roll(tile, 1, 0))
        bits_ref[row_tile(m - plan.per + REACH), :] = low.astype(BF16)
    if m < REACH:
        high = jnp.where(j == CHUNKS - 1, 0.0, pltpu.roll(tile, CHUNKS - 1, 0))
        bits_ref[row_tile(m + plan.per + REACH), :] = high.astype(BF16)


def lay_loadings(plan, load_ref, left_ref, right_ref, x_ref, bits_ref, low_ref, buf):
    factors = plan.factors
    left, right = (
        ref[:factors, :].astype(F32) + ref[factors : 2 * factors, :].astype(F32)
        for ref in (left_ref, right_ref)
    )
    turned(buf, left, (load_ref,), right)
    lane = lax.broadcasted_iota(jnp.int32, (CHUNKS, LANES), 1)
    skip = LANES - plan.halo
    for m in range(plan.ext):
        halves = []
        for h in range(PHASES // 2):
            at = skip + PHASES * m + 2 * h
            even = buf[pl.ds(at, CHUNKS, stride=plan.stride), :]
            odd = buf[pl.ds(at + 1, CHUNKS, stride=plan.stride), :]
            halves.append(jnp.where(lane < factors, even, odd))
        tile = jnp.concatenate(halves, 1)
        bits = tile.astype(BF16)
        bits_ref[row_tile(m), :] = bits
        if REACH <= m < REACH + plan.per:
            x_ref[row_tile(m - REACH), :] = tile
            low_ref[row_tile(m - REACH), :] = (tile - bits.astype(F32)).astype(BF16)


def lay_data(plan, *refs):
    fields, (rims_ref, out_ref, buf) = refs[:-3], refs[-3:]
    turned(buf, rims_ref[:, :LANES], fields, rims_ref[:, LANES:])
    skip = LANES - plan.front
    for m in range(plan.per + REACH):
        for p, at in enumerate(lane_tiles(PHASES)):
            rows = pl.ds(skip + PHASES * m + p, CHUNKS, stride=plan.stride)
            out_ref[row_tile(m), at] = buf[rows, :].astype(BF16)


def first_body(plan, load_any, data_any, motif_any, *refs):
    data_ref, motif_ref, gram_ref, near_ref, wide_ref, load_ref, sems = refs
    factors = plan.factors
    moves = [
        pltpu.make_async_copy(source, target, sems.at[i])
        for i, (source, target) in enumerate(
            ((load_any, load_ref), (data_any, data_ref), (motif_any, motif_ref.at[0]))
        )
    ]
    for move in moves:
        move.start()
    for move in moves:
        move.wait()
    odd = lax.axis_index("tm") % 2 == 1
    head, tail = slice(0, LANES), slice(plan.steps - LANES, plan.steps)
    for rim_ref, even_at, odd_at in ((near_ref, tail, head), (wide_ref, head, tail)):
        high, low = split(jnp.where(odd, load_ref[:, odd_at], load_ref[:, even_at]))
        rim_ref[:factors, :] = high
        rim_ref[factors : 2 * factors, :] = low
        rim_ref[2 * factors :, :] = jnp.where(
            odd, data_ref[:, odd_at].astype(F32), data_ref[:, even_at].astype(F32)
        ).astype(BF16)
    high, low = split(load_ref[...])
    cross = dot(high, low, NT)
    gram_ref[...] = dot(high, high, NT) + cross + cross.T


def lay_motifs(plan, me, crossed, first_ref, second_ref, stk_ref, padded):
    factors = plan.factors
    channels = first_ref.shape[1]
    span = GROUP * LAGS
    padded[channels:, :] = jnp.zeros((LANES - channels, padded.shape[1]), BF16)
    row = lax.broadcasted_iota(jnp.int32, (span, span), 0)
    col = lax.broadcasted_iota(jnp.int32, (span, span), 1)
    pick = jnp.where(col == (row % GROUP) * LAGS + row // GROUP, 1.0, 0.0).astype(BF16)
    for q in range(PHASES):
        rows = slice(q * factors, (q + 1) * factors)
        if q:
            stk_ref[rows, : q * LANES] = jnp.zeros((factors, q * LANES), BF16)
        stk_ref[rows, (LAGS + q) * LANES :] = jnp.zeros((factors, (PHASES - q) * LANES), BF16)
    for pair in range(factors // (2 * GROUP)):
        halves = []
        for block in (2 * pair, 2 * pair + 1):
            room = slice(block * span, (block + 1) * span)
            step = block ^ me
            index, late = step // 2, step % 2
            if crossed is not None:
                index = jnp.where(crossed, (step // 2) % 2 + 2 * (step % 2), index)
                late = jnp.where(crossed, step // 4, late)
            one, two = first_ref[index].astype(F32), second_ref[index].astype(F32)
            padded[:channels, room] = jnp.where(late == 1, two, one).astype(BF16)
            halves.append(dot(pick, padded[:, room], NT))
        for lag in range(LAGS):
            cut = slice(lag * GROUP, (lag + 1) * GROUP)
            tile = jnp.concatenate([halves[0][cut], halves[1][cut]], 0).astype(BF16)
            for q in range(PHASES):
                first = q * factors + pair * 2 * GROUP
                stk_ref[first : first + 2 * GROUP, (lag + q) * LANES : (lag + q + 1) * LANES] = tile


def auto_body(plan, moved, first_ref, second_ref, *refs):
    before, (stk_ref, auto_ref, padded) = refs[:-3], refs[-3:]
    factors = plan.factors
    me = lax.axis_index("tm") if moved else 0
    crossed = None
    lay_motifs(plan, me, crossed, first_ref, second_ref, stk_ref, padded)
    last = (PHASES - 1) * factors
    deep = PHASES * LANES
    auto_ref[...] = before[0][...] if before else jnp.zeros_like(auto_ref)
    for u in range(REACH + 1):
        taps = min(u + 1, REACH)
        cuts = [slice((u - a) * deep, (u - a + 1) * deep) for a in range(taps)]
        left = jnp.concatenate([stk_ref[last : last + factors, cut] for cut in cuts], 0)
        auto_ref[: taps * factors, :] += dot(left, stk_ref[:, u * deep : (u + 1) * deep], NT)


def numer_body(plan, stk_ref, data_ref, numer_ref, before=None):
    deep = PHASES * LANES
    for s in range(REACH + 1):
        rows = slice(s * CHUNKS, s * CHUNKS + plan.rows)
        part = dot(data_ref[rows, :], stk_ref[:, s * deep : (s + 1) * deep], NT)
        if s:
            numer_ref[...] += part
        else:
            numer_ref[...] = part if before is None else part + before[...]


def numer_tail_body(plan, shards, stk_a, stk_b, data_ref, before, bits_ref, *refs):
    numer_ref, tail_ref, past, ahead, ahead2 = refs
    tail_body(plan, shards, bits_ref, (stk_a, stk_b), tail_ref, past, ahead, ahead2)
    numer_body(plan, stk_b, data_ref, numer_ref, before)


def tail_start(plan, stk_ref, past, ahead):
    factors = plan.factors
    group = 2 * LANES // factors
    known = past[...]
    total = jnp.zeros((LAGS, LANES), F32)
    for first in range(0, LAGS, group):
        lags = range(first, first + group)
        rows = jnp.concatenate([known[LAGS - l : 2 * LAGS - l, :factors] for l in lags], 1)
        mat = jnp.concatenate([stk_ref[:factors, l * LANES : (l + 1) * LANES] for l in lags], 0)
        total += dot(rows.astype(BF16), mat)
    ahead[:LAGS, :] = jnp.zeros((LAGS, LANES), F32)
    ahead[LAGS:, :] = total


def tail_part(plan, stk_ref, ahead):
    factors = plan.factors
    beyond = ahead[...]
    high = beyond.astype(BF16).astype(F32)
    low = beyond - high
    out = jnp.zeros((2 * LAGS, factors), F32)
    for first in range(0, LAGS, 2):
        lags = range(first, first + 2)
        rows = jnp.concatenate(
            [jnp.concatenate([part[l : l + LAGS] for l in lags], 1) for part in (high, low)], 0
        )
        mat = stk_ref[:factors, first * LANES : (first + 2) * LANES]
        out += dot(rows.astype(BF16), mat, NT)
    return out[:LAGS] + out[LAGS:]


def tail_body(plan, shards, bits_ref, stks, out_ref, past, *aheads):
    out_ref[...] = jnp.zeros_like(out_ref)

    factors = plan.factors
    start = (plan.steps // PHASES + plan.edge) - (CHUNKS - 1) * plan.per
    ends = [
        bits_ref[row_tile(start + i), :].astype(F32)[CHUNKS - 1 :] for i in range(REACH)
    ]
    known = jnp.concatenate(ends, 0)
    past[...] = jnp.zeros_like(past)
    for p in range(PHASES):
        part = known[:, p * factors : (p + 1) * factors]
        part = jnp.concatenate([part, jnp.zeros((REACH, LANES - factors), F32)], 1)
        past[pl.ds(p, REACH, stride=PHASES), :] = part
    for stk_ref, ahead in zip(stks, aheads):
        tail_start(plan, stk_ref, past, ahead)
    over = sum(tail_part(plan, stk_ref, ahead) for stk_ref, ahead in zip(stks, aheads))
    past[:LAGS, :] = jnp.concatenate([over, jnp.zeros((LAGS, LANES - factors), F32)], 1)
    value = jnp.concatenate(
        [past[pl.ds(p, REACH, stride=PHASES), :][:, :factors] for p in range(PHASES)], 1
    )
    out_ref[...] = jnp.where(lax.axis_index("tm") == shards - 1, value, 0.0)


def taps_body(plan, auto_a, auto_b, high_ref, low_ref, line):
    factors, width = plan.factors, plan.width
    line[:, :width] = jnp.zeros((factors, width), F32)
    for a in range(REACH):
        rows = slice(a * factors, (a + 1) * factors)
        line[:, (REACH - a) * width : (REACH - a + 1) * width] = auto_a[rows, :] + auto_b[rows, :]
    zero = (REACH * PHASES + PHASES - 1) * factors
    back = [
        line[:, zero - d * factors : zero - (d - 1) * factors].T for d in range(1, PHASES)
    ]
    back.append(jnp.zeros((factors, factors), F32))
    line[:, (REACH + 1) * width :] = jnp.concatenate(back, 1)
    for s in range(REACH + 1):
        for p in range(PHASES):
            first = zero - (PHASES * s + p) * factors
            high, low = split(line[:, first : first + width])
            rows = slice(s * width + p * factors, s * width + (p + 1) * factors)
            high_ref[rows, :] = high
            low_ref[rows, :] = low


def conv_body(plan, offsets, bits_ref, high_ref, low_ref, *refs):
    before, out_ref = refs[:-1], refs[-1]
    width, rows = plan.width, plan.rows
    for i, s in enumerate(offsets):
        at = (REACH + s) * CHUNKS
        mat = slice(abs(s) * width, (abs(s) + 1) * width)
        dims = NN if s >= 0 else NT
        part = dot(bits_ref[at : at + rows, :], high_ref[mat, :], dims)
        part += dot(bits_ref[at : at + rows, :], low_ref[mat, :], dims)
        if i:
            out_ref[...] += part
        else:
            out_ref[...] = part + before[0][...] if before else part


def conv_tail_body(plan, shards, offsets, bits_ref, high_ref, low_ref, stk_a, stk_b, *refs):
    out_ref, tail_ref, past, ahead, ahead2 = refs
    tail_body(plan, shards, bits_ref, (stk_a, stk_b), tail_ref, past, ahead, ahead2)
    conv_body(plan, offsets, bits_ref, high_ref, low_ref, out_ref)


def first_conv_body(plan, offsets, auto_a, auto_b, bits_ref, high_ref, low_ref, out_ref, line):
    taps_body(plan, auto_a, auto_b, high_ref, low_ref, line)
    conv_body(plan, offsets, bits_ref, high_ref, low_ref, out_ref)


def penalties(plan, scale, grams, bits_ref, low_ref):
    factors, rows = plan.factors, plan.rows
    total = grams[0][...]
    if len(grams) > 1:
        here, far, both = (g[...] for g in grams[1:])
        odd = lax.axis_index("chan") % 2 == 1
        near = jnp.where(odd, far, here)
        next_one = jnp.where(odd, here, far)
        total = (total + near) + (next_one + both)
    r = lax.broadcasted_iota(jnp.int32, (factors, factors), 0)
    c = lax.broadcasted_iota(jnp.int32, (factors, factors), 1)
    off = jnp.where(r == c, 0.0, total) * scale
    blank = jnp.zeros((factors, factors), F32)
    high, low = split(
        jnp.concatenate(
            [
                jnp.concatenate([off if p == q else blank for q in range(PHASES)], 1)
                for p in range(PHASES)
            ],
            0,
        )
    )
    bits = bits_ref[REACH * CHUNKS : REACH * CHUNKS + rows, :]
    return dot(bits, high) + dot(bits, low) + dot(low_ref[...], high)


def new_tile(plan, shards, me, m, x_ref, den_ref, numer, pen, tails):
    at = row_tile(m)
    den = den_ref[at, :] + pen[at, :]
    j = lax.broadcasted_iota(jnp.int32, den.shape, 0)
    end = (plan.steps // PHASES + plan.edge) - (CHUNKS - 1) * plan.per
    if end - REACH <= m < end:
        i = m - end + REACH
        over = tails[0][i : i + 1, :] + tails[1][i : i + 1, :]
        den -= jnp.where((j == CHUNKS - 1) & (me == shards - 1), over, 0.0)
    new = x_ref[at, :] * numer / den
    if m < plan.edge:
        new = jnp.where((j == 0) & (me == 0), 0.0, new)
    if m >= end:
        new = jnp.where((j == CHUNKS - 1) & (me == shards - 1), 0.0, new)
    return new


def update_body(plan, scale, shards, counts, x_ref, bits_ref, low_ref, den_ref, *refs):
    numers, tails, grams = refs[: counts[0]], refs[counts[0] :][:2], refs[counts[0] + 2 :][: counts[1]]
    refs = refs[counts[0] + 2 + counts[1] :]
    if counts[0] > 1:
        numer_ref, refs = refs[0], refs[1:]
    out_ref, out_bits, out_low, gram_ref, pen, both = refs
    factors, width = plan.factors, plan.width
    me = lax.axis_index("tm")
    pen[...] = penalties(plan, scale, grams, bits_ref, low_ref)
    end = (plan.steps // PHASES + plan.edge) - (CHUNKS - 1) * plan.per
    for m in range(plan.per):
        at = row_tile(m)
        numer = numers[0][at, :]
        if counts[0] > 1:
            numer = numer + numers[1][at, :]
            numer_ref[at, :] = numer
        new = new_tile(plan, shards, me, m, x_ref, den_ref, numer, pen, tails)
        out_ref[at, :] = new
        spread(plan, new, m, out_bits)
        high, low = split(new)
        out_low[at, :] = low
        j = lax.broadcasted_iota(jnp.int32, new.shape, 0)
        kept = new
        if m < plan.edge:
            kept = jnp.where(j == 0, 0.0, kept)
        if m >= end:
            kept = jnp.where(j == CHUNKS - 1, 0.0, kept)
        high, low = split(kept)
        both[at, :width] = high
        both[at, width:] = low
    same, cross = 0.0, 0.0
    for lanes in lane_tiles(width // LANES):
        ahead = slice(width + lanes.start, width + lanes.stop)
        full = dot(both[:, lanes], jnp.concatenate([both[:, lanes], both[:, ahead]], 1), TN)
        for p in range(LANES // factors):
            at = slice(p * factors, (p + 1) * factors)
            same += full[at, at]
            cross += full[at, LANES + at.start : LANES + at.stop]
    gram_ref[...] = same + cross + cross.T


def last_body(plan, scale, shards, counts, x_ref, bits_ref, low_ref, den_ref, *refs):
    numers, tails, grams = refs[: counts[0]], refs[counts[0] :][:2], refs[counts[0] + 2 :][: counts[1]]
    out_ref, pen, buf = refs[counts[0] + 2 + counts[1] :]
    me = lax.axis_index("tm")
    pen[...] = penalties(plan, scale, grams, bits_ref, low_ref)
    for m in range(plan.per):
        numer = sum(n[row_tile(m), :] for n in numers)
        new = new_tile(plan, shards, me, m, x_ref, den_ref, numer, pen, tails)
        for h, lanes in enumerate(lane_tiles(PHASES // 2)):
            at = PHASES * m + 2 * h
            buf[pl.ds(at, CHUNKS, stride=plan.stride), :] = new[:, lanes]
            turn = pltpu.roll(new[:, lanes], LANES // 2, 1)
            buf[pl.ds(at + 1, CHUNKS, stride=plan.stride), :] = turn
    for i, lanes in enumerate(lane_tiles(plan.steps // LANES)):
        at = plan.front + i * LANES
        out_ref[:, lanes] = buf[at : at + LANES, :].T[: plan.factors, :]


def swap(x, axis, bit):
    count = lax.axis_size(axis)
    return lax.ppermute(x, axis, [(i, i ^ bit) for i in range(count)])


def mixed(x, bit_even, bit_odd):
    wide = lax.axis_size("chan")
    pairs = []
    for t in range(lax.axis_size("tm")):
        for c in range(wide):
            far = t ^ (bit_odd if c % 2 else bit_even)
            pairs.append((t * wide + c, far * wide + c))
    return lax.ppermute(x, ("tm", "chan"), pairs)


def shifted(x, axis, by):
    count = lax.axis_size(axis)
    return lax.ppermute(x, axis, [(i, i + by) for i in range(count) if 0 <= i + by < count])


def between(x):
    count, wide = lax.axis_size("tm"), lax.axis_size("chan")
    pairs = []
    for t in range(count):
        far = t + (1 if t % 2 else -1)
        for c in range(wide):
            target = (far, c) if 0 <= far < count else (t, c ^ (wide // 2))
            pairs.append((t * wide + c, target[0] * wide + target[1]))
    return lax.ppermute(x, ("tm", "chan"), pairs)


def doubling(axis):
    count = lax.axis_size(axis)
    bits = [1 << b for b in range(count.bit_length() - 1)]
    return bits[1:] + bits[:1]


def after(x, *others):
    return lax.optimization_barrier((x, *others))[0]


def gram_rounds(x, odd, *meanwhile):
    bits = doubling("tm")
    singles, pairs = bits[-1:], bits[:-1]
    if len(pairs) % 2:
        singles, pairs = singles + pairs[-1:], pairs[:-1]
    gaps = list(meanwhile)

    def gap(*values):
        others = gaps.pop(0) if gaps else ()
        return lax.optimization_barrier(values + others)[: len(values)]

    for bit in singles:
        x = x + gap(swap(x, "tm", bit))[0]
    terms = [x]
    while pairs:
        one, two, pairs = pairs[0], pairs[1], pairs[2:]
        here, both = gap(mixed(x, one, two), swap(x, "tm", one ^ two))
        far = swap(here, "chan", 1)
        terms = [x, here, far, both]
        if pairs:
            near, other = jnp.where(odd, far, here), jnp.where(odd, here, far)
            x = (x + near) + (other + both)
    return terms


def on_device(data, motifs, loadings):
    channels, steps = data.shape
    factors = loadings.shape[0]
    plan = Plan(steps, factors)
    shards = lax.axis_size("tm")
    width, rows = plan.width, plan.rows
    ext_rows = plan.ext * CHUNKS
    sds = jax.ShapeDtypeStruct
    me = lax.axis_index("tm")
    odd = lax.axis_index("chan") % 2 == 1

    rim = sds((2 * factors + channels, LANES), BF16)
    data_in, even, gram, near_rim, wide_rim = call(
        functools.partial(first_body, plan),
        (
            sds(data.shape, BF16),
            sds((1,) + motifs.shape, BF16),
            sds((factors, factors), F32),
            rim,
            rim,
        ),
        [pl.BlockSpec(memory_space=pltpu.HBM)] * 3,
        [
            pltpu.VMEM(loadings.shape, F32),
            pltpu.SemaphoreType.DMA((3,)),
        ],
        limit=53,
    )(loadings, data, motifs)

    moved = motifs.shape[1] == GROUP * LAGS
    bits = doubling("tm")
    tracks = (bits, bits)

    front = slice(0, steps // (2 * LANES) * LANES)

    def gather_round(x, i):
        return mixed(x, tracks[0][i], tracks[1][i])

    for i, bit in enumerate(bits[:-1]):
        near = gather_round(even if i else motifs[None], i)
        if i:
            gram_near = swap(gram, "tm", bits[i - 1])
            if i == 1:
                wide_rim = between(wide_rim)
                ready = after(data_in, even)
                far_data = [swap(ready[:, at], "chan", 2) for at in (front, slice(front.stop, steps))]
                near_rim = swap(after(near_rim, even), "tm", bits[-1])
                near, gram_near, near_rim, far_front = lax.optimization_barrier(
                    (near, gram_near, near_rim, far_data[0])
                )
            else:
                near, gram_near = lax.optimization_barrier((near, gram_near))
            gram = gram + gram_near
        even = jnp.concatenate([even, near], 0)
    odds = gather_round(even, len(bits) - 1)
    far_even = swap(even, "chan", 2)
    gram_near = swap(gram, "tm", bits[-1])
    right_side = me % 2 == 1
    nothing = jnp.zeros_like(wide_rim)
    left = jnp.where(me == 0, nothing, jnp.where(right_side, near_rim, wide_rim))
    right = jnp.where(me == shards - 1, nothing, jnp.where(right_side, wide_rim, near_rim))
    if not moved:
        order = [0]
        for bit in bits:
            order = order + [o ^ bit for o in order]
        slots = jnp.concatenate([even, odds], 0)
        index = jnp.array([order.index(b) for b in range(shards)], jnp.int32)
        slots = jnp.take(slots, jnp.take(index, jnp.arange(shards) ^ me), axis=0)
        slots = jnp.moveaxis(slots, 0, 1).reshape(channels, -1, GROUP * LAGS)
        slots = jnp.moveaxis(slots, 1, 0)
        even, odds = slots[0::2], slots[1::2]
        far_even = swap(even, "chan", 2)

    def lay(*fields):
        return call(
            functools.partial(lay_data, plan),
            sds(((plan.per + REACH) * CHUNKS, PHASES * LANES), BF16),
            vmem(len(fields)),
            [pltpu.VMEM((steps + 2 * LANES, LANES), F32)],
        )(*fields)

    field, window = sds((rows, width), F32), sds((ext_rows, width), BF16)
    low_field, rest = sds((rows, width), BF16), sds((REACH, width), F32)
    tail_room = [pltpu.VMEM((2 * LAGS, LANES), F32)] * 3
    rims = jnp.concatenate([left[2 * factors :], right[2 * factors :]], 1)
    own_laid = lay(data_in, rims)
    x, bits_x, low_x = call(
        functools.partial(lay_loadings, plan),
        (field, window, low_field),
        vmem(3),
        [pltpu.VMEM((steps + 2 * LANES, LANES), F32)],
    )(loadings, left, right)
    odds, far_even, gram_near, far_back, own_laid, x, bits_x = lax.optimization_barrier(
        (odds, far_even, gram_near, far_data[1], own_laid, x, bits_x)
    )
    gram = gram + gram_near
    gram_near = swap(gram, "tm", bits[-2])
    far_odds = swap(jnp.concatenate([odds, rims[None]], 0), "chan", 2)
    far_odds, gram_near = lax.optimization_barrier((far_odds, gram_near))
    gram = gram + gram_near
    far_rims = far_odds[-1]

    def autos(evens, odd_ones, *before):
        return call(
            functools.partial(auto_body, plan, moved),
            (sds((width, plan.tiles * LANES), BF16), sds((REACH * factors, width), F32)),
            vmem(2 + len(before)),
            [pltpu.VMEM((LANES, factors * LAGS), BF16)],
        )(evens, odd_ones, *before)

    stk, auto = autos(even, odds)
    numer = call(functools.partial(numer_body, plan), field, vmem(2))(stk, own_laid)
    far_odds, numer = lax.optimization_barrier((far_odds, numer))
    far_stk, auto = autos(far_even, far_odds, auto)
    far_front, far_back, far_rims, auto = lax.optimization_barrier(
        (far_front, far_back, far_rims, auto)
    )
    auto_far = swap(auto, "chan", 1)
    numer, tail = call(
        functools.partial(numer_tail_body, plan, shards),
        (field, rest),
        vmem(5),
        tail_room,
    )(stk, far_stk, lay(far_front, far_back, far_rims), numer, bits_x)
    numer, tail, auto_far = lax.optimization_barrier((numer, tail, auto_far))
    numer_far = swap(numer, "chan", 1)
    grams = [gram]

    mats = sds(((REACH + 1) * width, width), BF16)
    every = list(range(-REACH, REACH + 1))
    high, low, den = call(
        functools.partial(first_conv_body, plan, every),
        (mats, mats, sds((rows, width), F32)),
        vmem(3),
        [pltpu.VMEM((factors, (REACH + 2) * width), F32)],
    )(auto, auto_far, bits_x)

    def conv(offsets, bits_now, before):
        return call(functools.partial(conv_body, plan, offsets), field, vmem(4))(
            bits_now, high, low, before
        )

    def conv_tail(offsets, bits_now):
        return call(
            functools.partial(conv_tail_body, plan, shards, offsets),
            (field, rest),
            vmem(5),
            tail_room,
        )(bits_now, high, low, stk, far_stk)

    scale = PENALTY / (steps * shards)
    numers_now = (numer, numer_far)
    for sweep in range(ITERS):
        if sweep:
            part, tail = conv_tail(every[:REACH + 3], bits_x)
            tails = (tail, swap(tail, "chan", 1))
            den = conv(every[REACH + 3:], bits_x, part)
            grams = gram_rounds(gram, odd, (part,), (den, tails[1]))
        else:
            tails = (tail, swap(tail, "chan", 1))
        operands = (x, bits_x, low_x, den, *numers_now, *tails, *grams)
        counts = (len(numers_now), len(grams))
        if sweep == ITERS - 1:
            return call(
                functools.partial(last_body, plan, scale, shards, counts),
                sds((factors, steps), F32),
                vmem(len(operands)),
                [pltpu.VMEM((rows, width), F32), pltpu.VMEM((steps + 2 * LANES, LANES), F32)],
            )(*operands)
        outs = (field, window, low_field, sds((factors, factors), F32))
        if counts[0] > 1:
            outs = (field,) + outs
        got = call(
            functools.partial(update_body, plan, scale, shards, counts),
            outs,
            vmem(len(operands)),
            [pltpu.VMEM((rows, width), F32), pltpu.VMEM((rows, 2 * width), BF16)],
        )(*operands)
        if counts[0] > 1:
            numers_now, got = got[:1], got[1:]
        x, bits_x, low_x, gram = got


def solution(mesh):
    in_specs = (P("chan", "tm"), P("chan", "tm"), P(None, "tm"))
    out_specs = P(None, "tm")
    return jax.shard_map(
        on_device, mesh=mesh, in_specs=in_specs, out_specs=out_specs, check_vma=False
    )
```

```python
import functools

import jax
import jax.numpy as jnp
from jax import lax
from jax.experimental import pallas as pl
from jax.experimental.pallas import tpu as pltpu
from jax.sharding import PartitionSpec as P

LAGS = 32
ITERS = 3
PENALTY = 0.2

PHASES = 4
CHUNKS = 16
REACH = LAGS // PHASES
LANES = 128
GROUP = 8

NT = (((1,), (1,)), ((), ()))
NN = (((1,), (0,)), ((), ()))
TN = (((0,), (0,)), ((), ()))
F32 = jnp.float32
BF16 = jnp.bfloat16


def dot(a, b, dims=NN):
    return lax.dot_general(a, b, dims, preferred_element_type=F32)


def split(a):
    high = a.astype(BF16)
    return high, (a - high.astype(F32)).astype(BF16)


def vmem(n=1):
    return [pl.BlockSpec(memory_space=pltpu.VMEM)] * n


def smem(n=1):
    return [pl.BlockSpec(memory_space=pltpu.SMEM)] * n


def call(body, out_shape, in_specs, scratch=(), flops=0, moved=0, limit=16):
    return pl.pallas_call(
        body,
        out_shape=out_shape,
        in_specs=in_specs,
        out_specs=jax.tree.map(lambda _: pl.BlockSpec(memory_space=pltpu.VMEM), out_shape),
        scratch_shapes=list(scratch),
        compiler_params=pltpu.CompilerParams(vmem_limit_bytes=limit * 2**20),
        cost_estimate=pl.CostEstimate(flops=flops, bytes_accessed=moved, transcendentals=0),
    )


class Plan:
    def __init__(self, steps, factors):
        self.steps = steps
        self.factors = factors
        self.width = PHASES * factors
        self.edge = 2 * REACH
        self.rows = steps // PHASES + 2 * self.edge
        self.per = self.rows // CHUNKS
        self.ext = self.per + 2 * REACH
        self.stride = PHASES * self.per
        self.halo = PHASES * (self.edge + REACH)
        self.front = PHASES * self.edge
        self.back = PHASES * (self.edge + REACH)
        wide = steps + 2 * self.halo
        self.wide = -(-wide // LANES) * LANES
        self.tiles = LAGS + PHASES


def lane_tiles(count):
    return [slice(i * LANES, (i + 1) * LANES) for i in range(count)]


def row_tile(m):
    return slice(m * CHUNKS, (m + 1) * CHUNKS)


def turned(buf, left, fields, right):
    middle = [field[:, at] for field in fields for at in lane_tiles(field.shape[1] // LANES)]
    parts = [left] + middle + [right]
    for i, part in enumerate(parts):
        part = part.astype(F32)
        spare = LANES - part.shape[0]
        low = part if spare == part.shape[0] else jnp.zeros((spare, LANES), F32)
        buf[i * LANES : (i + 1) * LANES, :] = jnp.concatenate([part, low], 0).T


def spread(plan, tile, m, bits_ref):
    j = lax.broadcasted_iota(jnp.int32, tile.shape, 0)
    bits_ref[row_tile(m + REACH), :] = tile.astype(BF16)
    if m >= plan.per - REACH:
        low = jnp.where(j == 0, 0.0, pltpu.roll(tile, 1, 0))
        bits_ref[row_tile(m - plan.per + REACH), :] = low.astype(BF16)
    if m < REACH:
        high = jnp.where(j == CHUNKS - 1, 0.0, pltpu.roll(tile, CHUNKS - 1, 0))
        bits_ref[row_tile(m + plan.per + REACH), :] = high.astype(BF16)


def lay_loadings(plan, load_ref, left_ref, right_ref, x_ref, bits_ref, low_ref, buf):
    factors = plan.factors
    left, right = (
        ref[:factors, :].astype(F32) + ref[factors : 2 * factors, :].astype(F32)
        for ref in (left_ref, right_ref)
    )
    turned(buf, left, (load_ref,), right)
    lane = lax.broadcasted_iota(jnp.int32, (CHUNKS, LANES), 1)
    skip = LANES - plan.halo
    for m in range(plan.ext):
        halves = []
        for h in range(PHASES // 2):
            at = skip + PHASES * m + 2 * h
            even = buf[pl.ds(at, CHUNKS, stride=plan.stride), :]
            odd = buf[pl.ds(at + 1, CHUNKS, stride=plan.stride), :]
            halves.append(jnp.where(lane < factors, even, odd))
        tile = jnp.concatenate(halves, 1)
        bits = tile.astype(BF16)
        bits_ref[row_tile(m), :] = bits
        if REACH <= m < REACH + plan.per:
            x_ref[row_tile(m - REACH), :] = tile
            low_ref[row_tile(m - REACH), :] = (tile - bits.astype(F32)).astype(BF16)


def lay_data(plan, *refs):
    fields, (rims_ref, out_ref, buf) = refs[:-3], refs[-3:]
    turned(buf, rims_ref[:, :LANES], fields, rims_ref[:, LANES:])
    skip = LANES - plan.front
    for m in range(plan.per + REACH):
        for p, at in enumerate(lane_tiles(PHASES)):
            rows = pl.ds(skip + PHASES * m + p, CHUNKS, stride=plan.stride)
            out_ref[row_tile(m), at] = buf[rows, :].astype(BF16)


def first_body(plan, load_any, data_any, motif_any, *refs):
    data_ref, motif_ref, gram_ref, near_ref, wide_ref, load_ref, sems = refs
    factors = plan.factors
    moves = [
        pltpu.make_async_copy(source, target, sems.at[i])
        for i, (source, target) in enumerate(
            ((load_any, load_ref), (data_any, data_ref), (motif_any, motif_ref.at[0]))
        )
    ]
    for move in moves:
        move.start()
    for move in moves:
        move.wait()
    odd = lax.axis_index("tm") % 2 == 1
    head, tail = slice(0, LANES), slice(plan.steps - LANES, plan.steps)
    for rim_ref, even_at, odd_at in ((near_ref, tail, head), (wide_ref, head, tail)):
        high, low = split(jnp.where(odd, load_ref[:, odd_at], load_ref[:, even_at]))
        rim_ref[:factors, :] = high
        rim_ref[factors : 2 * factors, :] = low
        rim_ref[2 * factors :, :] = jnp.where(
            odd, data_ref[:, odd_at].astype(F32), data_ref[:, even_at].astype(F32)
        ).astype(BF16)
    high, low = split(load_ref[...])
    cross = dot(high, low, NT)
    gram_ref[...] = dot(high, high, NT) + cross + cross.T


def lay_motifs(plan, me, crossed, first_ref, second_ref, stk_ref, padded):
    factors = plan.factors
    channels = first_ref.shape[1]
    span = GROUP * LAGS
    padded[channels:, :] = jnp.zeros((LANES - channels, padded.shape[1]), BF16)
    row = lax.broadcasted_iota(jnp.int32, (span, span), 0)
    col = lax.broadcasted_iota(jnp.int32, (span, span), 1)
    pick = jnp.where(col == (row % GROUP) * LAGS + row // GROUP, 1.0, 0.0).astype(BF16)
    for q in range(PHASES):
        rows = slice(q * factors, (q + 1) * factors)
        if q:
            stk_ref[rows, : q * LANES] = jnp.zeros((factors, q * LANES), BF16)
        stk_ref[rows, (LAGS + q) * LANES :] = jnp.zeros((factors, (PHASES - q) * LANES), BF16)
    for pair in range(factors // (2 * GROUP)):
        halves = []
        for block in (2 * pair, 2 * pair + 1):
            room = slice(block * span, (block + 1) * span)
            step = block ^ me
            index, late = step // 2, step % 2
            if crossed is not None:
                index = jnp.where(crossed, (step // 2) % 2 + 2 * (step % 2), index)
                late = jnp.where(crossed, step // 4, late)
            one, two = first_ref[index].astype(F32), second_ref[index].astype(F32)
            padded[:channels, room] = jnp.where(late == 1, two, one).astype(BF16)
            halves.append(dot(pick, padded[:, room], NT))
        for lag in range(LAGS):
            cut = slice(lag * GROUP, (lag + 1) * GROUP)
            tile = jnp.concatenate([halves[0][cut], halves[1][cut]], 0).astype(BF16)
            for q in range(PHASES):
                first = q * factors + pair * 2 * GROUP
                stk_ref[first : first + 2 * GROUP, (lag + q) * LANES : (lag + q + 1) * LANES] = tile


def auto_body(plan, moved, first_ref, second_ref, *refs):
    before, (stk_ref, auto_ref, padded) = refs[:-3], refs[-3:]
    factors = plan.factors
    me = lax.axis_index("tm") if moved else 0
    crossed = None
    lay_motifs(plan, me, crossed, first_ref, second_ref, stk_ref, padded)
    last = (PHASES - 1) * factors
    deep = PHASES * LANES
    auto_ref[...] = before[0][...] if before else jnp.zeros_like(auto_ref)
    for u in range(REACH + 1):
        taps = min(u + 1, REACH)
        cuts = [slice((u - a) * deep, (u - a + 1) * deep) for a in range(taps)]
        left = jnp.concatenate([stk_ref[last : last + factors, cut] for cut in cuts], 0)
        auto_ref[: taps * factors, :] += dot(left, stk_ref[:, u * deep : (u + 1) * deep], NT)


def numer_body(plan, stk_ref, data_ref, numer_ref, before=None):
    deep = PHASES * LANES
    for s in range(REACH + 1):
        rows = slice(s * CHUNKS, s * CHUNKS + plan.rows)
        part = dot(data_ref[rows, :], stk_ref[:, s * deep : (s + 1) * deep], NT)
        if s:
            numer_ref[: plan.rows, :] += part
        else:
            numer_ref[: plan.rows, :] = part if before is None else part + before[...]


def numer_tail_body(plan, shards, stk_a, stk_b, data_ref, before, bits_ref, *refs):
    numer_ref, past, ahead, ahead2 = refs
    tail_ref = numer_ref.at[plan.rows :, :]
    tail_body(plan, shards, bits_ref, (stk_a, stk_b), tail_ref, past, ahead, ahead2)
    numer_body(plan, stk_b, data_ref, numer_ref, before)


def tail_start(plan, stk_ref, past, ahead):
    factors = plan.factors
    group = 2 * LANES // factors
    known = past[...]
    total = jnp.zeros((LAGS, LANES), F32)
    for first in range(0, LAGS, group):
        lags = range(first, first + group)
        rows = jnp.concatenate([known[LAGS - l : 2 * LAGS - l, :factors] for l in lags], 1)
        mat = jnp.concatenate([stk_ref[:factors, l * LANES : (l + 1) * LANES] for l in lags], 0)
        total += dot(rows.astype(BF16), mat)
    ahead[:LAGS, :] = jnp.zeros((LAGS, LANES), F32)
    ahead[LAGS:, :] = total


def tail_part(plan, stk_ref, ahead):
    factors = plan.factors
    beyond = ahead[...]
    high = beyond.astype(BF16).astype(F32)
    low = beyond - high
    out = jnp.zeros((2 * LAGS, factors), F32)
    for first in range(0, LAGS, 2):
        lags = range(first, first + 2)
        rows = jnp.concatenate(
            [jnp.concatenate([part[l : l + LAGS] for l in lags], 1) for part in (high, low)], 0
        )
        mat = stk_ref[:factors, first * LANES : (first + 2) * LANES]
        out += dot(rows.astype(BF16), mat, NT)
    return out[:LAGS] + out[LAGS:]


def tail_body(plan, shards, bits_ref, stks, out_ref, past, *aheads):
    out_ref[...] = jnp.zeros_like(out_ref)

    factors = plan.factors
    start = (plan.steps // PHASES + plan.edge) - (CHUNKS - 1) * plan.per
    ends = [
        bits_ref[row_tile(start + i), :].astype(F32)[CHUNKS - 1 :] for i in range(REACH)
    ]
    known = jnp.concatenate(ends, 0)
    past[...] = jnp.zeros_like(past)
    for p in range(PHASES):
        part = known[:, p * factors : (p + 1) * factors]
        part = jnp.concatenate([part, jnp.zeros((REACH, LANES - factors), F32)], 1)
        past[pl.ds(p, REACH, stride=PHASES), :] = part
    for stk_ref, ahead in zip(stks, aheads):
        tail_start(plan, stk_ref, past, ahead)
    over = sum(tail_part(plan, stk_ref, ahead) for stk_ref, ahead in zip(stks, aheads))
    past[:LAGS, :] = jnp.concatenate([over, jnp.zeros((LAGS, LANES - factors), F32)], 1)
    value = jnp.concatenate(
        [past[pl.ds(p, REACH, stride=PHASES), :][:, :factors] for p in range(PHASES)], 1
    )
    out_ref[...] = jnp.where(lax.axis_index("tm") == shards - 1, value, 0.0)


def taps_body(plan, auto_a, auto_b, high_ref, low_ref, line):
    factors, width = plan.factors, plan.width
    line[:, :width] = jnp.zeros((factors, width), F32)
    for a in range(REACH):
        rows = slice(a * factors, (a + 1) * factors)
        line[:, (REACH - a) * width : (REACH - a + 1) * width] = auto_a[rows, :] + auto_b[rows, :]
    zero = (REACH * PHASES + PHASES - 1) * factors
    back = [
        line[:, zero - d * factors : zero - (d - 1) * factors].T for d in range(1, PHASES)
    ]
    back.append(jnp.zeros((factors, factors), F32))
    line[:, (REACH + 1) * width :] = jnp.concatenate(back, 1)
    for s in range(REACH + 1):
        for p in range(PHASES):
            first = zero - (PHASES * s + p) * factors
            high, low = split(line[:, first : first + width])
            rows = slice(s * width + p * factors, s * width + (p + 1) * factors)
            high_ref[rows, :] = high
            low_ref[rows, :] = low


def conv_body(plan, offsets, bits_ref, high_ref, low_ref, *refs):
    before, out_ref = refs[:-1], refs[-1]
    width, rows = plan.width, plan.rows
    for i, s in enumerate(offsets):
        at = (REACH + s) * CHUNKS
        mat = slice(abs(s) * width, (abs(s) + 1) * width)
        dims = NN if s >= 0 else NT
        part = dot(bits_ref[at : at + rows, :], high_ref[mat, :], dims)
        part += dot(bits_ref[at : at + rows, :], low_ref[mat, :], dims)
        if i:
            out_ref[...] += part
        else:
            out_ref[...] = part + before[0][...] if before else part


def conv_tail_body(plan, shards, offsets, bits_ref, high_ref, low_ref, stk_a, stk_b, *refs):
    out_ref, tail_ref, past, ahead, ahead2 = refs
    tail_body(plan, shards, bits_ref, (stk_a, stk_b), tail_ref, past, ahead, ahead2)
    conv_body(plan, offsets, bits_ref, high_ref, low_ref, out_ref)


def first_conv_body(plan, offsets, auto_a, auto_b, bits_ref, high_ref, low_ref, out_ref, line):
    taps_body(plan, auto_a, auto_b, high_ref, low_ref, line)
    conv_body(plan, offsets, bits_ref, high_ref, low_ref, out_ref)


def penalties(plan, scale, grams, bits_ref, low_ref):
    factors, rows = plan.factors, plan.rows
    total = grams[0][...]
    if len(grams) > 1:
        here, far, both = (g[...] for g in grams[1:])
        odd = lax.axis_index("chan") % 2 == 1
        near = jnp.where(odd, far, here)
        next_one = jnp.where(odd, here, far)
        total = (total + near) + (next_one + both)
    r = lax.broadcasted_iota(jnp.int32, (factors, factors), 0)
    c = lax.broadcasted_iota(jnp.int32, (factors, factors), 1)
    off = jnp.where(r == c, 0.0, total) * scale
    blank = jnp.zeros((factors, factors), F32)
    high, low = split(
        jnp.concatenate(
            [
                jnp.concatenate([off if p == q else blank for q in range(PHASES)], 1)
                for p in range(PHASES)
            ],
            0,
        )
    )
    bits = bits_ref[REACH * CHUNKS : REACH * CHUNKS + rows, :]
    return dot(bits, high) + dot(bits, low) + dot(low_ref[...], high)


def new_tile(plan, shards, me, m, x_ref, den_ref, numer, pen, tails):
    at = row_tile(m)
    den = den_ref[at, :] + pen[at, :]
    j = lax.broadcasted_iota(jnp.int32, den.shape, 0)
    end = (plan.steps // PHASES + plan.edge) - (CHUNKS - 1) * plan.per
    if end - REACH <= m < end:
        i = m - end + REACH
        over = tails[0][i : i + 1, :] + tails[1][i : i + 1, :]
        den -= jnp.where((j == CHUNKS - 1) & (me == shards - 1), over, 0.0)
    new = x_ref[at, :] * numer / den
    if m < plan.edge:
        new = jnp.where((j == 0) & (me == 0), 0.0, new)
    if m >= end:
        new = jnp.where((j == CHUNKS - 1) & (me == shards - 1), 0.0, new)
    return new


def update_body(plan, scale, shards, counts, x_ref, bits_ref, low_ref, den_ref, *refs):
    numers, refs = refs[: counts[0]], refs[counts[0] :]
    if counts[0] > 1:
        tails = [numer[plan.rows :, :] for numer in numers]
    else:
        tails, refs = refs[:2], refs[2:]
    grams, refs = refs[: counts[1]], refs[counts[1] :]
    if counts[0] > 1:
        numer_ref, refs = refs[0], refs[1:]
    out_ref, out_bits, out_low, gram_ref, pen, both = refs
    factors, width = plan.factors, plan.width
    me = lax.axis_index("tm")
    pen[...] = penalties(plan, scale, grams, bits_ref, low_ref)
    end = (plan.steps // PHASES + plan.edge) - (CHUNKS - 1) * plan.per
    for m in range(plan.per):
        at = row_tile(m)
        numer = numers[0][at, :]
        if counts[0] > 1:
            numer = numer + numers[1][at, :]
            numer_ref[at, :] = numer
        new = new_tile(plan, shards, me, m, x_ref, den_ref, numer, pen, tails)
        out_ref[at, :] = new
        spread(plan, new, m, out_bits)
        high, low = split(new)
        out_low[at, :] = low
        j = lax.broadcasted_iota(jnp.int32, new.shape, 0)
        kept = new
        if m < plan.edge:
            kept = jnp.where(j == 0, 0.0, kept)
        if m >= end:
            kept = jnp.where(j == CHUNKS - 1, 0.0, kept)
        high, low = split(kept)
        both[at, :width] = high
        both[at, width:] = low
    same, cross = 0.0, 0.0
    for lanes in lane_tiles(width // LANES):
        ahead = slice(width + lanes.start, width + lanes.stop)
        full = dot(both[:, lanes], jnp.concatenate([both[:, lanes], both[:, ahead]], 1), TN)
        for p in range(LANES // factors):
            at = slice(p * factors, (p + 1) * factors)
            same += full[at, at]
            cross += full[at, LANES + at.start : LANES + at.stop]
    gram_ref[...] = same + cross + cross.T


def last_body(plan, scale, shards, counts, x_ref, bits_ref, low_ref, den_ref, *refs):
    numers, tails, grams = refs[: counts[0]], refs[counts[0] :][:2], refs[counts[0] + 2 :][: counts[1]]
    out_ref, pen, buf = refs[counts[0] + 2 + counts[1] :]
    me = lax.axis_index("tm")
    pen[...] = penalties(plan, scale, grams, bits_ref, low_ref)
    for m in range(plan.per):
        numer = sum(n[row_tile(m), :] for n in numers)
        new = new_tile(plan, shards, me, m, x_ref, den_ref, numer, pen, tails)
        for h, lanes in enumerate(lane_tiles(PHASES // 2)):
            at = PHASES * m + 2 * h
            buf[pl.ds(at, CHUNKS, stride=plan.stride), :] = new[:, lanes]
            turn = pltpu.roll(new[:, lanes], LANES // 2, 1)
            buf[pl.ds(at + 1, CHUNKS, stride=plan.stride), :] = turn
    for i, lanes in enumerate(lane_tiles(plan.steps // LANES)):
        at = plan.front + i * LANES
        out_ref[:, lanes] = buf[at : at + LANES, :].T[: plan.factors, :]


def swap(x, axis, bit):
    count = lax.axis_size(axis)
    return lax.ppermute(x, axis, [(i, i ^ bit) for i in range(count)])


def mixed(x, bit_even, bit_odd):
    wide = lax.axis_size("chan")
    pairs = []
    for t in range(lax.axis_size("tm")):
        for c in range(wide):
            far = t ^ (bit_odd if c % 2 else bit_even)
            pairs.append((t * wide + c, far * wide + c))
    return lax.ppermute(x, ("tm", "chan"), pairs)


def shifted(x, axis, by):
    count = lax.axis_size(axis)
    return lax.ppermute(x, axis, [(i, i + by) for i in range(count) if 0 <= i + by < count])


def between(x):
    count, wide = lax.axis_size("tm"), lax.axis_size("chan")
    pairs = []
    for t in range(count):
        far = t + (1 if t % 2 else -1)
        for c in range(wide):
            target = (far, c) if 0 <= far < count else (t, c ^ (wide // 2))
            pairs.append((t * wide + c, target[0] * wide + target[1]))
    return lax.ppermute(x, ("tm", "chan"), pairs)


def doubling(axis):
    count = lax.axis_size(axis)
    bits = [1 << b for b in range(count.bit_length() - 1)]
    return bits[1:] + bits[:1]


def after(x, *others):
    return lax.optimization_barrier((x, *others))[0]


def gram_rounds(x, odd, *meanwhile):
    bits = doubling("tm")
    singles, pairs = bits[-1:], bits[:-1]
    if len(pairs) % 2:
        singles, pairs = singles + pairs[-1:], pairs[:-1]
    gaps = list(meanwhile)

    def gap(*values):
        others = gaps.pop(0) if gaps else ()
        return lax.optimization_barrier(values + others)[: len(values)]

    for bit in singles:
        x = x + gap(swap(x, "tm", bit))[0]
    terms = [x]
    while pairs:
        one, two, pairs = pairs[0], pairs[1], pairs[2:]
        here, both = gap(mixed(x, one, two), swap(x, "tm", one ^ two))
        far = swap(here, "chan", 1)
        terms = [x, here, far, both]
        if pairs:
            near, other = jnp.where(odd, far, here), jnp.where(odd, here, far)
            x = (x + near) + (other + both)
    return terms


def on_device(data, motifs, loadings):
    channels, steps = data.shape
    factors = loadings.shape[0]
    plan = Plan(steps, factors)
    shards = lax.axis_size("tm")
    width, rows = plan.width, plan.rows
    ext_rows = plan.ext * CHUNKS
    sds = jax.ShapeDtypeStruct
    me = lax.axis_index("tm")
    odd = lax.axis_index("chan") % 2 == 1

    rim = sds((2 * factors + channels, LANES), BF16)
    data_in, even, gram, near_rim, wide_rim = call(
        functools.partial(first_body, plan),
        (
            sds(data.shape, BF16),
            sds((1,) + motifs.shape, BF16),
            sds((factors, factors), F32),
            rim,
            rim,
        ),
        [pl.BlockSpec(memory_space=pltpu.HBM)] * 3,
        [
            pltpu.VMEM(loadings.shape, F32),
            pltpu.SemaphoreType.DMA((3,)),
        ],
        limit=53,
    )(loadings, data, motifs)

    moved = motifs.shape[1] == GROUP * LAGS
    bits = doubling("tm")
    tracks = (bits, bits)

    front = slice(0, 5 * steps // (8 * LANES) * LANES)

    def gather_round(x, i):
        return mixed(x, tracks[0][i], tracks[1][i])

    for i, bit in enumerate(bits[:-1]):
        near = gather_round(even if i else motifs[None], i)
        if i:
            gram_near = swap(gram, "tm", bits[i - 1])
            if i == 1:
                wide_rim = between(wide_rim)
                ready = after(data_in, even)
                far_data = [swap(ready[:, at], "chan", 2) for at in (front, slice(front.stop, steps))]
                near_rim = swap(after(near_rim, even), "tm", bits[-1])
                near, gram_near, near_rim, far_front = lax.optimization_barrier(
                    (near, gram_near, near_rim, far_data[0])
                )
            else:
                near, gram_near = lax.optimization_barrier((near, gram_near))
            gram = gram + gram_near
        even = jnp.concatenate([even, near], 0)
    odds = gather_round(even, len(bits) - 1)
    far_even = swap(even, "chan", 2)
    gram_near = swap(gram, "tm", bits[-1])
    right_side = me % 2 == 1
    nothing = jnp.zeros_like(wide_rim)
    left = jnp.where(me == 0, nothing, jnp.where(right_side, near_rim, wide_rim))
    right = jnp.where(me == shards - 1, nothing, jnp.where(right_side, wide_rim, near_rim))
    if not moved:
        order = [0]
        for bit in bits:
            order = order + [o ^ bit for o in order]
        slots = jnp.concatenate([even, odds], 0)
        index = jnp.array([order.index(b) for b in range(shards)], jnp.int32)
        slots = jnp.take(slots, jnp.take(index, jnp.arange(shards) ^ me), axis=0)
        slots = jnp.moveaxis(slots, 0, 1).reshape(channels, -1, GROUP * LAGS)
        slots = jnp.moveaxis(slots, 1, 0)
        even, odds = slots[0::2], slots[1::2]
        far_even = swap(even, "chan", 2)

    def lay(*fields):
        return call(
            functools.partial(lay_data, plan),
            sds(((plan.per + REACH) * CHUNKS, PHASES * LANES), BF16),
            vmem(len(fields)),
            [pltpu.VMEM((steps + 2 * LANES, LANES), F32)],
        )(*fields)

    field, window = sds((rows, width), F32), sds((ext_rows, width), BF16)
    low_field, rest = sds((rows, width), BF16), sds((REACH, width), F32)
    tail_room = [pltpu.VMEM((2 * LAGS, LANES), F32)] * 3
    rims = jnp.concatenate([left[2 * factors :], right[2 * factors :]], 1)
    own_laid = lay(data_in, rims)
    x, bits_x, low_x = call(
        functools.partial(lay_loadings, plan),
        (field, window, low_field),
        vmem(3),
        [pltpu.VMEM((steps + 2 * LANES, LANES), F32)],
    )(loadings, left, right)
    odds, far_even, gram_near, far_back, own_laid, x, bits_x = lax.optimization_barrier(
        (odds, far_even, gram_near, far_data[1], own_laid, x, bits_x)
    )
    gram = gram + gram_near
    gram_near = swap(gram, "tm", bits[-2])
    far_odds = swap(jnp.concatenate([odds, rims[None]], 0), "chan", 2)
    far_odds, gram_near = lax.optimization_barrier((far_odds, gram_near))
    gram = gram + gram_near
    far_rims = far_odds[-1]

    def autos(evens, odd_ones, *before):
        return call(
            functools.partial(auto_body, plan, moved),
            (sds((width, plan.tiles * LANES), BF16), sds((REACH * factors, width), F32)),
            vmem(2 + len(before)),
            [pltpu.VMEM((LANES, factors * LAGS), BF16)],
        )(evens, odd_ones, *before)

    stk, auto = autos(even, odds)
    numer = call(functools.partial(numer_body, plan), field, vmem(2))(stk, own_laid)
    far_odds, numer = lax.optimization_barrier((far_odds, numer))
    far_stk, auto = autos(far_even, far_odds, auto)
    far_front, far_back, far_rims, auto = lax.optimization_barrier(
        (far_front, far_back, far_rims, auto)
    )
    auto_far = swap(auto, "chan", 1)
    numer = call(
        functools.partial(numer_tail_body, plan, shards),
        sds((rows + REACH, width), F32),
        vmem(5),
        tail_room,
    )(stk, far_stk, lay(far_front, far_back, far_rims), numer, bits_x)
    numer, auto_far = lax.optimization_barrier((numer, auto_far))
    numer_far = swap(numer, "chan", 1)
    grams = [gram]

    mats = sds(((REACH + 1) * width, width), BF16)
    every = list(range(-REACH, REACH + 1))
    high, low, den = call(
        functools.partial(first_conv_body, plan, every),
        (mats, mats, sds((rows, width), F32)),
        vmem(3),
        [pltpu.VMEM((factors, (REACH + 2) * width), F32)],
    )(auto, auto_far, bits_x)

    def conv(offsets, bits_now, before):
        return call(functools.partial(conv_body, plan, offsets), field, vmem(4))(
            bits_now, high, low, before
        )

    def conv_tail(offsets, bits_now):
        return call(
            functools.partial(conv_tail_body, plan, shards, offsets),
            (field, rest),
            vmem(5),
            tail_room,
        )(bits_now, high, low, stk, far_stk)

    scale = PENALTY / (steps * shards)
    numers_now = (numer, numer_far)
    for sweep in range(ITERS):
        if sweep:
            part, tail = conv_tail(every[:REACH + 3], bits_x)
            tails = (tail, swap(tail, "chan", 1))
            den = conv(every[REACH + 3:], bits_x, part)
            grams = gram_rounds(gram, odd, (part,), (den, tails[1]))
        else:
            tails = ()
        operands = (x, bits_x, low_x, den, *numers_now, *tails, *grams)
        counts = (len(numers_now), len(grams))
        if sweep == ITERS - 1:
            return call(
                functools.partial(last_body, plan, scale, shards, counts),
                sds((factors, steps), F32),
                vmem(len(operands)),
                [pltpu.VMEM((rows, width), F32), pltpu.VMEM((steps + 2 * LANES, LANES), F32)],
            )(*operands)
        outs = (field, window, low_field, sds((factors, factors), F32))
        if counts[0] > 1:
            outs = (field,) + outs
        got = call(
            functools.partial(update_body, plan, scale, shards, counts),
            outs,
            vmem(len(operands)),
            [pltpu.VMEM((rows, width), F32), pltpu.VMEM((rows, 2 * width), BF16)],
        )(*operands)
        if counts[0] > 1:
            numers_now, got = got[:1], got[1:]
        x, bits_x, low_x, gram = got


def solution(mesh):
    in_specs = (P("chan", "tm"), P("chan", "tm"), P(None, "tm"))
    out_specs = P(None, "tm")
    return jax.shard_map(
        on_device, mesh=mesh, in_specs=in_specs, out_specs=out_specs, check_vma=False
    )
```

```python
import functools

import jax
import jax.numpy as jnp
from jax import lax
from jax.experimental import pallas as pl
from jax.experimental.pallas import tpu as pltpu
from jax.sharding import PartitionSpec as P

LAGS = 32
ITERS = 3
PENALTY = 0.2

PHASES = 4
CHUNKS = 16
REACH = LAGS // PHASES
LANES = 128
GROUP = 8

NT = (((1,), (1,)), ((), ()))
NN = (((1,), (0,)), ((), ()))
TN = (((0,), (0,)), ((), ()))
F32 = jnp.float32
BF16 = jnp.bfloat16


def dot(a, b, dims=NN):
    return lax.dot_general(a, b, dims, preferred_element_type=F32)


def split(a):
    high = a.astype(BF16)
    return high, (a - high.astype(F32)).astype(BF16)


def vmem(n=1):
    return [pl.BlockSpec(memory_space=pltpu.VMEM)] * n


def smem(n=1):
    return [pl.BlockSpec(memory_space=pltpu.SMEM)] * n


def call(body, out_shape, in_specs, scratch=(), flops=0, moved=0, limit=16):
    return pl.pallas_call(
        body,
        out_shape=out_shape,
        in_specs=in_specs,
        out_specs=jax.tree.map(lambda _: pl.BlockSpec(memory_space=pltpu.VMEM), out_shape),
        scratch_shapes=list(scratch),
        compiler_params=pltpu.CompilerParams(vmem_limit_bytes=limit * 2**20),
        cost_estimate=pl.CostEstimate(flops=flops, bytes_accessed=moved, transcendentals=0),
    )


class Plan:
    def __init__(self, steps, factors):
        self.steps = steps
        self.factors = factors
        self.width = PHASES * factors
        self.edge = 2 * REACH
        self.rows = steps // PHASES + 2 * self.edge
        self.per = self.rows // CHUNKS
        self.ext = self.per + 2 * REACH
        self.stride = PHASES * self.per
        self.halo = PHASES * (self.edge + REACH)
        self.front = PHASES * self.edge
        self.back = PHASES * (self.edge + REACH)
        wide = steps + 2 * self.halo
        self.wide = -(-wide // LANES) * LANES
        self.tiles = LAGS + PHASES


def lane_tiles(count):
    return [slice(i * LANES, (i + 1) * LANES) for i in range(count)]


def row_tile(m):
    return slice(m * CHUNKS, (m + 1) * CHUNKS)


def turned(buf, left, fields, right):
    middle = [field[:, at] for field in fields for at in lane_tiles(field.shape[1] // LANES)]
    parts = [left] + middle + [right]
    for i, part in enumerate(parts):
        part = part.astype(F32)
        spare = LANES - part.shape[0]
        low = part if spare == part.shape[0] else jnp.zeros((spare, LANES), F32)
        buf[i * LANES : (i + 1) * LANES, :] = jnp.concatenate([part, low], 0).T


def spread(plan, tile, m, bits_ref):
    j = lax.broadcasted_iota(jnp.int32, tile.shape, 0)
    bits_ref[row_tile(m + REACH), :] = tile.astype(BF16)
    if m >= plan.per - REACH:
        low = jnp.where(j == 0, 0.0, pltpu.roll(tile, 1, 0))
        bits_ref[row_tile(m - plan.per + REACH), :] = low.astype(BF16)
    if m < REACH:
        high = jnp.where(j == CHUNKS - 1, 0.0, pltpu.roll(tile, CHUNKS - 1, 0))
        bits_ref[row_tile(m + plan.per + REACH), :] = high.astype(BF16)


def lay_loadings(plan, load_ref, left_ref, right_ref, x_ref, bits_ref, low_ref, buf):
    factors = plan.factors
    left, right = (
        ref[:factors, :].astype(F32) + ref[factors : 2 * factors, :].astype(F32)
        for ref in (left_ref, right_ref)
    )
    turned(buf, left, (load_ref,), right)
    lane = lax.broadcasted_iota(jnp.int32, (CHUNKS, LANES), 1)
    skip = LANES - plan.halo
    for m in range(plan.ext):
        halves = []
        for h in range(PHASES // 2):
            at = skip + PHASES * m + 2 * h
            even = buf[pl.ds(at, CHUNKS, stride=plan.stride), :]
            odd = buf[pl.ds(at + 1, CHUNKS, stride=plan.stride), :]
            halves.append(jnp.where(lane < factors, even, odd))
        tile = jnp.concatenate(halves, 1)
        bits = tile.astype(BF16)
        bits_ref[row_tile(m), :] = bits
        if REACH <= m < REACH + plan.per:
            x_ref[row_tile(m - REACH), :] = tile
            low_ref[row_tile(m - REACH), :] = (tile - bits.astype(F32)).astype(BF16)


def lay_data(plan, *refs):
    fields, (rims_ref, out_ref, buf) = refs[:-3], refs[-3:]
    turned(buf, rims_ref[:, :LANES], fields, rims_ref[:, LANES:])
    skip = LANES - plan.front
    for m in range(plan.per + REACH):
        for p, at in enumerate(lane_tiles(PHASES)):
            rows = pl.ds(skip + PHASES * m + p, CHUNKS, stride=plan.stride)
            out_ref[row_tile(m), at] = buf[rows, :].astype(BF16)


def first_body(plan, load_any, data_any, motif_any, *refs):
    data_ref, motif_ref, gram_ref, near_ref, wide_ref, load_ref, sems = refs
    factors = plan.factors
    moves = [
        pltpu.make_async_copy(source, target, sems.at[i])
        for i, (source, target) in enumerate(
            ((load_any, load_ref), (data_any, data_ref), (motif_any, motif_ref.at[0]))
        )
    ]
    for move in moves:
        move.start()
    for move in moves:
        move.wait()
    odd = lax.axis_index("tm") % 2 == 1
    head, tail = slice(0, LANES), slice(plan.steps - LANES, plan.steps)
    for rim_ref, even_at, odd_at in ((near_ref, tail, head), (wide_ref, head, tail)):
        high, low = split(jnp.where(odd, load_ref[:, odd_at], load_ref[:, even_at]))
        rim_ref[:factors, :] = high
        rim_ref[factors : 2 * factors, :] = low
        rim_ref[2 * factors :, :] = jnp.where(
            odd, data_ref[:, odd_at].astype(F32), data_ref[:, even_at].astype(F32)
        ).astype(BF16)
    high, low = split(load_ref[...])
    cross = dot(high, low, NT)
    gram_ref[...] = dot(high, high, NT) + cross + cross.T


def lay_motifs(plan, me, crossed, first_ref, second_ref, stk_ref, padded):
    factors = plan.factors
    channels = first_ref.shape[1]
    span = GROUP * LAGS
    padded[channels:, :] = jnp.zeros((LANES - channels, padded.shape[1]), BF16)
    row = lax.broadcasted_iota(jnp.int32, (span, span), 0)
    col = lax.broadcasted_iota(jnp.int32, (span, span), 1)
    pick = jnp.where(col == (row % GROUP) * LAGS + row // GROUP, 1.0, 0.0).astype(BF16)
    for q in range(PHASES):
        rows = slice(q * factors, (q + 1) * factors)
        if q:
            stk_ref[rows, : q * LANES] = jnp.zeros((factors, q * LANES), BF16)
        stk_ref[rows, (LAGS + q) * LANES :] = jnp.zeros((factors, (PHASES - q) * LANES), BF16)
    for pair in range(factors // (2 * GROUP)):
        halves = []
        for block in (2 * pair, 2 * pair + 1):
            room = slice(block * span, (block + 1) * span)
            step = block ^ me
            index, late = step // 2, step % 2
            if crossed is not None:
                index = jnp.where(crossed, (step // 2) % 2 + 2 * (step % 2), index)
                late = jnp.where(crossed, step // 4, late)
            one, two = first_ref[index].astype(F32), second_ref[index].astype(F32)
            padded[:channels, room] = jnp.where(late == 1, two, one).astype(BF16)
            halves.append(dot(pick, padded[:, room], NT))
        for lag in range(LAGS):
            cut = slice(lag * GROUP, (lag + 1) * GROUP)
            tile = jnp.concatenate([halves[0][cut], halves[1][cut]], 0).astype(BF16)
            for q in range(PHASES):
                first = q * factors + pair * 2 * GROUP
                stk_ref[first : first + 2 * GROUP, (lag + q) * LANES : (lag + q + 1) * LANES] = tile


def auto_body(plan, moved, first_ref, second_ref, *refs):
    before, (stk_ref, auto_ref, padded) = refs[:-3], refs[-3:]
    factors = plan.factors
    me = lax.axis_index("tm") if moved else 0
    crossed = None
    lay_motifs(plan, me, crossed, first_ref, second_ref, stk_ref, padded)
    last = (PHASES - 1) * factors
    deep = PHASES * LANES
    auto_ref[...] = before[0][...] if before else jnp.zeros_like(auto_ref)
    for u in range(REACH + 1):
        taps = min(u + 1, REACH)
        cuts = [slice((u - a) * deep, (u - a + 1) * deep) for a in range(taps)]
        left = jnp.concatenate([stk_ref[last : last + factors, cut] for cut in cuts], 0)
        auto_ref[: taps * factors, :] += dot(left, stk_ref[:, u * deep : (u + 1) * deep], NT)


def numer_body(plan, stk_ref, data_ref, numer_ref, before=None):
    deep = PHASES * LANES
    for s in range(REACH + 1):
        rows = slice(s * CHUNKS, s * CHUNKS + plan.rows)
        part = dot(data_ref[rows, :], stk_ref[:, s * deep : (s + 1) * deep], NT)
        if s:
            numer_ref[: plan.rows, :] += part
        else:
            numer_ref[: plan.rows, :] = part if before is None else part + before[...]


def numer_tail_body(plan, shards, stk_a, stk_b, data_ref, before, bits_ref, *refs):
    numer_ref, past, ahead, ahead2 = refs
    tail_ref = numer_ref.at[plan.rows :, :]
    tail_body(plan, shards, bits_ref, (stk_a, stk_b), tail_ref, past, ahead, ahead2)
    numer_body(plan, stk_b, data_ref, numer_ref, before)


def tail_start(plan, stk_ref, past, ahead):
    factors = plan.factors
    group = 2 * LANES // factors
    known = past[...]
    total = jnp.zeros((LAGS, LANES), F32)
    for first in range(0, LAGS, group):
        lags = range(first, first + group)
        rows = jnp.concatenate([known[LAGS - l : 2 * LAGS - l, :factors] for l in lags], 1)
        mat = jnp.concatenate([stk_ref[:factors, l * LANES : (l + 1) * LANES] for l in lags], 0)
        total += dot(rows.astype(BF16), mat)
    ahead[:LAGS, :] = jnp.zeros((LAGS, LANES), F32)
    ahead[LAGS:, :] = total


def tail_part(plan, stk_ref, ahead):
    factors = plan.factors
    beyond = ahead[...]
    high = beyond.astype(BF16).astype(F32)
    low = beyond - high
    out = jnp.zeros((2 * LAGS, factors), F32)
    for first in range(0, LAGS, 2):
        lags = range(first, first + 2)
        rows = jnp.concatenate(
            [jnp.concatenate([part[l : l + LAGS] for l in lags], 1) for part in (high, low)], 0
        )
        mat = stk_ref[:factors, first * LANES : (first + 2) * LANES]
        out += dot(rows.astype(BF16), mat, NT)
    return out[:LAGS] + out[LAGS:]


def tail_body(plan, shards, bits_ref, stks, out_ref, past, *aheads):
    out_ref[...] = jnp.zeros_like(out_ref)

    factors = plan.factors
    start = (plan.steps // PHASES + plan.edge) - (CHUNKS - 1) * plan.per
    ends = [
        bits_ref[row_tile(start + i), :].astype(F32)[CHUNKS - 1 :] for i in range(REACH)
    ]
    known = jnp.concatenate(ends, 0)
    past[...] = jnp.zeros_like(past)
    for p in range(PHASES):
        part = known[:, p * factors : (p + 1) * factors]
        part = jnp.concatenate([part, jnp.zeros((REACH, LANES - factors), F32)], 1)
        past[pl.ds(p, REACH, stride=PHASES), :] = part
    for stk_ref, ahead in zip(stks, aheads):
        tail_start(plan, stk_ref, past, ahead)
    over = sum(tail_part(plan, stk_ref, ahead) for stk_ref, ahead in zip(stks, aheads))
    past[:LAGS, :] = jnp.concatenate([over, jnp.zeros((LAGS, LANES - factors), F32)], 1)
    value = jnp.concatenate(
        [past[pl.ds(p, REACH, stride=PHASES), :][:, :factors] for p in range(PHASES)], 1
    )
    out_ref[...] = jnp.where(lax.axis_index("tm") == shards - 1, value, 0.0)


def taps_body(plan, auto_a, auto_b, high_ref, low_ref, line):
    factors, width = plan.factors, plan.width
    line[:, :width] = jnp.zeros((factors, width), F32)
    for a in range(REACH):
        rows = slice(a * factors, (a + 1) * factors)
        line[:, (REACH - a) * width : (REACH - a + 1) * width] = auto_a[rows, :] + auto_b[rows, :]
    zero = (REACH * PHASES + PHASES - 1) * factors
    back = [
        line[:, zero - d * factors : zero - (d - 1) * factors].T for d in range(1, PHASES)
    ]
    back.append(jnp.zeros((factors, factors), F32))
    line[:, (REACH + 1) * width :] = jnp.concatenate(back, 1)
    for s in range(REACH + 1):
        for p in range(PHASES):
            first = zero - (PHASES * s + p) * factors
            high, low = split(line[:, first : first + width])
            rows = slice(s * width + p * factors, s * width + (p + 1) * factors)
            high_ref[rows, :] = high
            low_ref[rows, :] = low


def conv_body(plan, offsets, bits_ref, high_ref, low_ref, *refs):
    before, out_ref = refs[:-1], refs[-1]
    width, rows = plan.width, plan.rows
    for i, s in enumerate(offsets):
        at = (REACH + s) * CHUNKS
        mat = slice(abs(s) * width, (abs(s) + 1) * width)
        dims = NN if s >= 0 else NT
        part = dot(bits_ref[at : at + rows, :], high_ref[mat, :], dims)
        part += dot(bits_ref[at : at + rows, :], low_ref[mat, :], dims)
        if i:
            out_ref[...] += part
        else:
            out_ref[...] = part + before[0][...] if before else part


def conv_tail_body(plan, shards, offsets, bits_ref, high_ref, low_ref, stk_a, stk_b, *refs):
    out_ref, tail_ref, past, ahead, ahead2 = refs
    tail_body(plan, shards, bits_ref, (stk_a, stk_b), tail_ref, past, ahead, ahead2)
    conv_body(plan, offsets, bits_ref, high_ref, low_ref, out_ref)


def first_conv_body(plan, offsets, auto_a, auto_b, bits_ref, high_ref, low_ref, out_ref, line):
    taps_body(plan, auto_a, auto_b, high_ref, low_ref, line)
    conv_body(plan, offsets, bits_ref, high_ref, low_ref, out_ref)


def penalties(plan, scale, grams, bits_ref, low_ref):
    factors, rows = plan.factors, plan.rows
    total = grams[0][...]
    if len(grams) > 1:
        here, far, both = (g[...] for g in grams[1:])
        odd = lax.axis_index("chan") % 2 == 1
        near = jnp.where(odd, far, here)
        next_one = jnp.where(odd, here, far)
        total = (total + near) + (next_one + both)
    r = lax.broadcasted_iota(jnp.int32, (factors, factors), 0)
    c = lax.broadcasted_iota(jnp.int32, (factors, factors), 1)
    off = jnp.where(r == c, 0.0, total) * scale
    blank = jnp.zeros((factors, factors), F32)
    high, low = split(
        jnp.concatenate(
            [
                jnp.concatenate([off if p == q else blank for q in range(PHASES)], 1)
                for p in range(PHASES)
            ],
            0,
        )
    )
    bits = bits_ref[REACH * CHUNKS : REACH * CHUNKS + rows, :]
    return dot(bits, high) + dot(bits, low) + dot(low_ref[...], high)


def new_tile(plan, shards, me, m, x_ref, den_ref, numer, pen, tails):
    at = row_tile(m)
    den = den_ref[at, :] + pen[at, :]
    j = lax.broadcasted_iota(jnp.int32, den.shape, 0)
    end = (plan.steps // PHASES + plan.edge) - (CHUNKS - 1) * plan.per
    if end - REACH <= m < end:
        i = m - end + REACH
        over = tails[0][i : i + 1, :] + tails[1][i : i + 1, :]
        den -= jnp.where((j == CHUNKS - 1) & (me == shards - 1), over, 0.0)
    new = x_ref[at, :] * numer / den
    if m < plan.edge:
        new = jnp.where((j == 0) & (me == 0), 0.0, new)
    if m >= end:
        new = jnp.where((j == CHUNKS - 1) & (me == shards - 1), 0.0, new)
    return new


def update_body(plan, scale, shards, counts, x_ref, bits_ref, low_ref, den_ref, *refs):
    numers, refs = refs[: counts[0]], refs[counts[0] :]
    if counts[0] > 1:
        tails = [numer[plan.rows :, :] for numer in numers]
    else:
        tails, refs = refs[:2], refs[2:]
    grams, refs = refs[: counts[1]], refs[counts[1] :]
    if counts[0] > 1:
        numer_ref, refs = refs[0], refs[1:]
    out_ref, out_bits, out_low, gram_ref, pen, both = refs
    factors, width = plan.factors, plan.width
    me = lax.axis_index("tm")
    pen[...] = penalties(plan, scale, grams, bits_ref, low_ref)
    end = (plan.steps // PHASES + plan.edge) - (CHUNKS - 1) * plan.per
    for m in range(plan.per):
        at = row_tile(m)
        numer = numers[0][at, :]
        if counts[0] > 1:
            numer = numer + numers[1][at, :]
            numer_ref[at, :] = numer
        new = new_tile(plan, shards, me, m, x_ref, den_ref, numer, pen, tails)
        out_ref[at, :] = new
        spread(plan, new, m, out_bits)
        high, low = split(new)
        out_low[at, :] = low
        j = lax.broadcasted_iota(jnp.int32, new.shape, 0)
        kept = new
        if m < plan.edge:
            kept = jnp.where(j == 0, 0.0, kept)
        if m >= end:
            kept = jnp.where(j == CHUNKS - 1, 0.0, kept)
        high, low = split(kept)
        both[at, :width] = high
        both[at, width:] = low
    same, cross = 0.0, 0.0
    for lanes in lane_tiles(width // LANES):
        ahead = slice(width + lanes.start, width + lanes.stop)
        full = dot(both[:, lanes], jnp.concatenate([both[:, lanes], both[:, ahead]], 1), TN)
        for p in range(LANES // factors):
            at = slice(p * factors, (p + 1) * factors)
            same += full[at, at]
            cross += full[at, LANES + at.start : LANES + at.stop]
    gram_ref[...] = same + cross + cross.T


def last_body(plan, scale, shards, counts, x_ref, bits_ref, low_ref, den_ref, *refs):
    numers, tails, grams = refs[: counts[0]], refs[counts[0] :][:2], refs[counts[0] + 2 :][: counts[1]]
    out_ref, pen, buf = refs[counts[0] + 2 + counts[1] :]
    me = lax.axis_index("tm")
    pen[...] = penalties(plan, scale, grams, bits_ref, low_ref)
    for m in range(plan.per):
        numer = sum(n[row_tile(m), :] for n in numers)
        new = new_tile(plan, shards, me, m, x_ref, den_ref, numer, pen, tails)
        for h, lanes in enumerate(lane_tiles(PHASES // 2)):
            at = PHASES * m + 2 * h
            buf[pl.ds(at, CHUNKS, stride=plan.stride), :] = new[:, lanes]
            turn = pltpu.roll(new[:, lanes], LANES // 2, 1)
            buf[pl.ds(at + 1, CHUNKS, stride=plan.stride), :] = turn
    for i, lanes in enumerate(lane_tiles(plan.steps // LANES)):
        at = plan.front + i * LANES
        out_ref[:, lanes] = buf[at : at + LANES, :].T[: plan.factors, :]


def swap(x, axis, bit):
    count = lax.axis_size(axis)
    return lax.ppermute(x, axis, [(i, i ^ bit) for i in range(count)])


def mixed(x, bit_even, bit_odd):
    wide = lax.axis_size("chan")
    pairs = []
    for t in range(lax.axis_size("tm")):
        for c in range(wide):
            far = t ^ (bit_odd if c % 2 else bit_even)
            pairs.append((t * wide + c, far * wide + c))
    return lax.ppermute(x, ("tm", "chan"), pairs)


def shifted(x, axis, by):
    count = lax.axis_size(axis)
    return lax.ppermute(x, axis, [(i, i + by) for i in range(count) if 0 <= i + by < count])


def between(x):
    count, wide = lax.axis_size("tm"), lax.axis_size("chan")
    pairs = []
    for t in range(count):
        far = t + (1 if t % 2 else -1)
        for c in range(wide):
            target = (far, c) if 0 <= far < count else (t, c ^ (wide // 2))
            pairs.append((t * wide + c, target[0] * wide + target[1]))
    return lax.ppermute(x, ("tm", "chan"), pairs)


def doubling(axis):
    count = lax.axis_size(axis)
    bits = [1 << b for b in range(count.bit_length() - 1)]
    return bits[1:] + bits[:1]


def after(x, *others):
    return lax.optimization_barrier((x, *others))[0]


def gram_rounds(x, odd, *meanwhile):
    bits = doubling("tm")
    singles, pairs = bits[-1:], bits[:-1]
    if len(pairs) % 2:
        singles, pairs = singles + pairs[-1:], pairs[:-1]
    gaps = list(meanwhile)

    def gap(*values):
        others = gaps.pop(0) if gaps else ()
        return lax.optimization_barrier(values + others)[: len(values)]

    for bit in singles:
        x = x + gap(swap(x, "tm", bit))[0]
    terms = [x]
    while pairs:
        one, two, pairs = pairs[0], pairs[1], pairs[2:]
        here, both = gap(mixed(x, one, two), swap(x, "tm", one ^ two))
        far = swap(here, "chan", 1)
        terms = [x, here, far, both]
        if pairs:
            near, other = jnp.where(odd, far, here), jnp.where(odd, here, far)
            x = (x + near) + (other + both)
    return terms


def on_device(data, motifs, loadings):
    channels, steps = data.shape
    factors = loadings.shape[0]
    plan = Plan(steps, factors)
    shards = lax.axis_size("tm")
    width, rows = plan.width, plan.rows
    ext_rows = plan.ext * CHUNKS
    sds = jax.ShapeDtypeStruct
    me = lax.axis_index("tm")
    odd = lax.axis_index("chan") % 2 == 1

    rim = sds((2 * factors + channels, LANES), BF16)
    data_in, even, gram, near_rim, wide_rim = call(
        functools.partial(first_body, plan),
        (
            sds(data.shape, BF16),
            sds((1,) + motifs.shape, BF16),
            sds((factors, factors), F32),
            rim,
            rim,
        ),
        [pl.BlockSpec(memory_space=pltpu.HBM)] * 3,
        [
            pltpu.VMEM(loadings.shape, F32),
            pltpu.SemaphoreType.DMA((3,)),
        ],
        limit=53,
    )(loadings, data, motifs)

    moved = motifs.shape[1] == GROUP * LAGS
    bits = doubling("tm")
    tracks = (bits, bits)

    def gather_round(x, i):
        return mixed(x, tracks[0][i], tracks[1][i])

    for i, bit in enumerate(bits[:-1]):
        near = gather_round(even if i else motifs[None], i)
        if i:
            gram_near = swap(gram, "tm", bits[i - 1])
            if i == 1:
                wide_rim = between(wide_rim)
                far_data = swap(data, "chan", 2)
                near_rim = swap(after(near_rim, even), "tm", bits[-1])
                near, gram_near, near_rim, far_data = lax.optimization_barrier(
                    (near, gram_near, near_rim, far_data)
                )
            else:
                near, gram_near = lax.optimization_barrier((near, gram_near))
            gram = gram + gram_near
        even = jnp.concatenate([even, near], 0)
    odds = gather_round(even, len(bits) - 1)
    far_even = swap(even, "chan", 2)
    gram_near = swap(gram, "tm", bits[-1])
    right_side = me % 2 == 1
    nothing = jnp.zeros_like(wide_rim)
    left = jnp.where(me == 0, nothing, jnp.where(right_side, near_rim, wide_rim))
    right = jnp.where(me == shards - 1, nothing, jnp.where(right_side, wide_rim, near_rim))
    if not moved:
        order = [0]
        for bit in bits:
            order = order + [o ^ bit for o in order]
        slots = jnp.concatenate([even, odds], 0)
        index = jnp.array([order.index(b) for b in range(shards)], jnp.int32)
        slots = jnp.take(slots, jnp.take(index, jnp.arange(shards) ^ me), axis=0)
        slots = jnp.moveaxis(slots, 0, 1).reshape(channels, -1, GROUP * LAGS)
        slots = jnp.moveaxis(slots, 1, 0)
        even, odds = slots[0::2], slots[1::2]
        far_even = swap(even, "chan", 2)

    def lay(*fields):
        return call(
            functools.partial(lay_data, plan),
            sds(((plan.per + REACH) * CHUNKS, PHASES * LANES), BF16),
            vmem(len(fields)),
            [pltpu.VMEM((steps + 2 * LANES, LANES), F32)],
        )(*fields)

    field, window = sds((rows, width), F32), sds((ext_rows, width), BF16)
    low_field, rest = sds((rows, width), BF16), sds((REACH, width), F32)
    tail_room = [pltpu.VMEM((2 * LAGS, LANES), F32)] * 3
    rims = jnp.concatenate([left[2 * factors :], right[2 * factors :]], 1)
    own_laid = lay(data_in, rims)
    x, bits_x, low_x = call(
        functools.partial(lay_loadings, plan),
        (field, window, low_field),
        vmem(3),
        [pltpu.VMEM((steps + 2 * LANES, LANES), F32)],
    )(loadings, left, right)
    odds, far_even, gram_near, own_laid, x, bits_x = lax.optimization_barrier(
        (odds, far_even, gram_near, own_laid, x, bits_x)
    )
    gram = gram + gram_near
    gram_near = swap(gram, "tm", bits[-2])
    far_odds = swap(jnp.concatenate([odds, rims[None]], 0), "chan", 2)
    far_odds, gram_near = lax.optimization_barrier((far_odds, gram_near))
    gram = gram + gram_near
    far_rims = far_odds[-1]

    def autos(evens, odd_ones, *before):
        return call(
            functools.partial(auto_body, plan, moved),
            (sds((width, plan.tiles * LANES), BF16), sds((REACH * factors, width), F32)),
            vmem(2 + len(before)),
            [pltpu.VMEM((LANES, factors * LAGS), BF16)],
        )(evens, odd_ones, *before)

    stk, auto = autos(even, odds)
    numer = call(functools.partial(numer_body, plan), field, vmem(2))(stk, own_laid)
    far_odds, numer = lax.optimization_barrier((far_odds, numer))
    far_stk, auto = autos(far_even, far_odds, auto)
    far_data, far_rims, auto = lax.optimization_barrier((far_data, far_rims, auto))
    auto_far = swap(auto, "chan", 1)
    numer = call(
        functools.partial(numer_tail_body, plan, shards),
        sds((rows + REACH, width), F32),
        vmem(5),
        tail_room,
    )(stk, far_stk, lay(far_data, far_rims), numer, bits_x)
    numer, auto_far = lax.optimization_barrier((numer, auto_far))
    numer_far = swap(numer, "chan", 1)
    grams = [gram]

    mats = sds(((REACH + 1) * width, width), BF16)
    every = list(range(-REACH, REACH + 1))
    high, low, den = call(
        functools.partial(first_conv_body, plan, every),
        (mats, mats, sds((rows, width), F32)),
        vmem(3),
        [pltpu.VMEM((factors, (REACH + 2) * width), F32)],
    )(auto, auto_far, bits_x)

    def conv(offsets, bits_now, before):
        return call(functools.partial(conv_body, plan, offsets), field, vmem(4))(
            bits_now, high, low, before
        )

    def conv_tail(offsets, bits_now):
        return call(
            functools.partial(conv_tail_body, plan, shards, offsets),
            (field, rest),
            vmem(5),
            tail_room,
        )(bits_now, high, low, stk, far_stk)

    scale = PENALTY / (steps * shards)
    numers_now = (numer, numer_far)
    for sweep in range(ITERS):
        if sweep:
            part, tail = conv_tail(every[:REACH + 3], bits_x)
            tails = (tail, swap(tail, "chan", 1))
            den = conv(every[REACH + 3:], bits_x, part)
            grams = gram_rounds(gram, odd, (part,), (den, tails[1]))
        else:
            tails = ()
        operands = (x, bits_x, low_x, den, *numers_now, *tails, *grams)
        counts = (len(numers_now), len(grams))
        if sweep == ITERS - 1:
            return call(
                functools.partial(last_body, plan, scale, shards, counts),
                sds((factors, steps), F32),
                vmem(len(operands)),
                [pltpu.VMEM((rows, width), F32), pltpu.VMEM((steps + 2 * LANES, LANES), F32)],
            )(*operands)
        outs = (field, window, low_field, sds((factors, factors), F32))
        if counts[0] > 1:
            outs = (field,) + outs
        got = call(
            functools.partial(update_body, plan, scale, shards, counts),
            outs,
            vmem(len(operands)),
            [pltpu.VMEM((rows, width), F32), pltpu.VMEM((rows, 2 * width), BF16)],
        )(*operands)
        if counts[0] > 1:
            numers_now, got = got[:1], got[1:]
        x, bits_x, low_x, gram = got


def solution(mesh):
    in_specs = (P("chan", "tm"), P("chan", "tm"), P(None, "tm"))
    out_specs = P(None, "tm")
    return jax.shard_map(
        on_device, mesh=mesh, in_specs=in_specs, out_specs=out_specs, check_vma=False
    )
```

```python
import functools

import jax
import jax.numpy as jnp
from jax import lax
from jax.experimental import pallas as pl
from jax.experimental.pallas import tpu as pltpu
from jax.sharding import PartitionSpec as P

LAGS = 32
ITERS = 3
PENALTY = 0.2

PHASES = 4
CHUNKS = 16
REACH = LAGS // PHASES
LANES = 128
GROUP = 8

NT = (((1,), (1,)), ((), ()))
NN = (((1,), (0,)), ((), ()))
TN = (((0,), (0,)), ((), ()))
F32 = jnp.float32
BF16 = jnp.bfloat16


def dot(a, b, dims=NN):
    return lax.dot_general(a, b, dims, preferred_element_type=F32)


def split(a):
    high = a.astype(BF16)
    return high, (a - high.astype(F32)).astype(BF16)


def vmem(n=1):
    return [pl.BlockSpec(memory_space=pltpu.VMEM)] * n


def smem(n=1):
    return [pl.BlockSpec(memory_space=pltpu.SMEM)] * n


def call(body, out_shape, in_specs, scratch=(), flops=0, moved=0, limit=16):
    return pl.pallas_call(
        body,
        out_shape=out_shape,
        in_specs=in_specs,
        out_specs=jax.tree.map(lambda _: pl.BlockSpec(memory_space=pltpu.VMEM), out_shape),
        scratch_shapes=list(scratch),
        compiler_params=pltpu.CompilerParams(vmem_limit_bytes=limit * 2**20),
        cost_estimate=pl.CostEstimate(flops=flops, bytes_accessed=moved, transcendentals=0),
    )


class Plan:
    def __init__(self, steps, factors):
        self.steps = steps
        self.factors = factors
        self.width = PHASES * factors
        self.edge = 2 * REACH
        self.rows = steps // PHASES + 2 * self.edge
        self.per = self.rows // CHUNKS
        self.ext = self.per + 2 * REACH
        self.stride = PHASES * self.per
        self.halo = PHASES * (self.edge + REACH)
        self.front = PHASES * self.edge
        self.back = PHASES * (self.edge + REACH)
        wide = steps + 2 * self.halo
        self.wide = -(-wide // LANES) * LANES
        self.tiles = LAGS + PHASES


def lane_tiles(count):
    return [slice(i * LANES, (i + 1) * LANES) for i in range(count)]


def row_tile(m):
    return slice(m * CHUNKS, (m + 1) * CHUNKS)


def turned(buf, left, fields, right):
    middle = [field[:, at] for field in fields for at in lane_tiles(field.shape[1] // LANES)]
    parts = [left] + middle + [right]
    for i, part in enumerate(parts):
        part = part.astype(F32)
        spare = LANES - part.shape[0]
        low = part if spare == part.shape[0] else jnp.zeros((spare, LANES), F32)
        buf[i * LANES : (i + 1) * LANES, :] = jnp.concatenate([part, low], 0).T


def spread(plan, tile, m, bits_ref):
    j = lax.broadcasted_iota(jnp.int32, tile.shape, 0)
    bits_ref[row_tile(m + REACH), :] = tile.astype(BF16)
    if m >= plan.per - REACH:
        low = jnp.where(j == 0, 0.0, pltpu.roll(tile, 1, 0))
        bits_ref[row_tile(m - plan.per + REACH), :] = low.astype(BF16)
    if m < REACH:
        high = jnp.where(j == CHUNKS - 1, 0.0, pltpu.roll(tile, CHUNKS - 1, 0))
        bits_ref[row_tile(m + plan.per + REACH), :] = high.astype(BF16)


def lay_loadings(plan, load_ref, left_ref, right_ref, x_ref, bits_ref, low_ref, buf):
    factors = plan.factors
    left, right = (
        ref[:factors, :].astype(F32) + ref[factors : 2 * factors, :].astype(F32)
        for ref in (left_ref, right_ref)
    )
    turned(buf, left, (load_ref,), right)
    lane = lax.broadcasted_iota(jnp.int32, (CHUNKS, LANES), 1)
    skip = LANES - plan.halo
    for m in range(plan.ext):
        halves = []
        for h in range(PHASES // 2):
            at = skip + PHASES * m + 2 * h
            even = buf[pl.ds(at, CHUNKS, stride=plan.stride), :]
            odd = buf[pl.ds(at + 1, CHUNKS, stride=plan.stride), :]
            halves.append(jnp.where(lane < factors, even, odd))
        tile = jnp.concatenate(halves, 1)
        bits = tile.astype(BF16)
        bits_ref[row_tile(m), :] = bits
        if REACH <= m < REACH + plan.per:
            x_ref[row_tile(m - REACH), :] = tile
            low_ref[row_tile(m - REACH), :] = (tile - bits.astype(F32)).astype(BF16)


def lay_data(plan, *refs):
    fields, (rims_ref, out_ref, buf) = refs[:-3], refs[-3:]
    turned(buf, rims_ref[:, :LANES], fields, rims_ref[:, LANES:])
    skip = LANES - plan.front
    for m in range(plan.per + REACH):
        for p, at in enumerate(lane_tiles(PHASES)):
            rows = pl.ds(skip + PHASES * m + p, CHUNKS, stride=plan.stride)
            out_ref[row_tile(m), at] = buf[rows, :].astype(BF16)


def first_body(plan, load_any, data_any, motif_any, *refs):
    data_ref, motif_ref, gram_ref, near_ref, wide_ref, load_ref, sems = refs
    factors = plan.factors
    moves = [
        pltpu.make_async_copy(source, target, sems.at[i])
        for i, (source, target) in enumerate(
            ((load_any, load_ref), (data_any, data_ref), (motif_any, motif_ref.at[0]))
        )
    ]
    for move in moves:
        move.start()
    for move in moves:
        move.wait()
    odd = lax.axis_index("tm") % 2 == 1
    head, tail = slice(0, LANES), slice(plan.steps - LANES, plan.steps)
    for rim_ref, even_at, odd_at in ((near_ref, tail, head), (wide_ref, head, tail)):
        high, low = split(jnp.where(odd, load_ref[:, odd_at], load_ref[:, even_at]))
        rim_ref[:factors, :] = high
        rim_ref[factors : 2 * factors, :] = low
        rim_ref[2 * factors :, :] = jnp.where(
            odd, data_ref[:, odd_at].astype(F32), data_ref[:, even_at].astype(F32)
        ).astype(BF16)
    high, low = split(load_ref[...])
    cross = dot(high, low, NT)
    gram_ref[...] = dot(high, high, NT) + cross + cross.T


def lay_motifs(plan, me, crossed, first_ref, second_ref, stk_ref, padded):
    factors = plan.factors
    channels = first_ref.shape[1]
    span = GROUP * LAGS
    padded[channels:, :] = jnp.zeros((LANES - channels, padded.shape[1]), BF16)
    row = lax.broadcasted_iota(jnp.int32, (span, span), 0)
    col = lax.broadcasted_iota(jnp.int32, (span, span), 1)
    pick = jnp.where(col == (row % GROUP) * LAGS + row // GROUP, 1.0, 0.0).astype(BF16)
    for q in range(PHASES):
        rows = slice(q * factors, (q + 1) * factors)
        if q:
            stk_ref[rows, : q * LANES] = jnp.zeros((factors, q * LANES), BF16)
        stk_ref[rows, (LAGS + q) * LANES :] = jnp.zeros((factors, (PHASES - q) * LANES), BF16)
    for pair in range(factors // (2 * GROUP)):
        halves = []
        for block in (2 * pair, 2 * pair + 1):
            room = slice(block * span, (block + 1) * span)
            step = block ^ me
            index, late = step // 2, step % 2
            if crossed is not None:
                index = jnp.where(crossed, (step // 2) % 2 + 2 * (step % 2), index)
                late = jnp.where(crossed, step // 4, late)
            one, two = first_ref[index].astype(F32), second_ref[index].astype(F32)
            padded[:channels, room] = jnp.where(late == 1, two, one).astype(BF16)
            halves.append(dot(pick, padded[:, room], NT))
        for lag in range(LAGS):
            cut = slice(lag * GROUP, (lag + 1) * GROUP)
            tile = jnp.concatenate([halves[0][cut], halves[1][cut]], 0).astype(BF16)
            for q in range(PHASES):
                first = q * factors + pair * 2 * GROUP
                stk_ref[first : first + 2 * GROUP, (lag + q) * LANES : (lag + q + 1) * LANES] = tile


def auto_body(plan, moved, first_ref, second_ref, *refs):
    before, (stk_ref, auto_ref, padded) = refs[:-3], refs[-3:]
    factors = plan.factors
    me = lax.axis_index("tm") if moved else 0
    crossed = None
    lay_motifs(plan, me, crossed, first_ref, second_ref, stk_ref, padded)
    last = (PHASES - 1) * factors
    deep = PHASES * LANES
    auto_ref[...] = before[0][...] if before else jnp.zeros_like(auto_ref)
    for u in range(REACH + 1):
        taps = min(u + 1, REACH)
        cuts = [slice((u - a) * deep, (u - a + 1) * deep) for a in range(taps)]
        left = jnp.concatenate([stk_ref[last : last + factors, cut] for cut in cuts], 0)
        auto_ref[: taps * factors, :] += dot(left, stk_ref[:, u * deep : (u + 1) * deep], NT)


def numer_body(plan, stk_ref, data_ref, numer_ref, before=None):
    deep = PHASES * LANES
    for s in range(REACH + 1):
        rows = slice(s * CHUNKS, s * CHUNKS + plan.rows)
        part = dot(data_ref[rows, :], stk_ref[:, s * deep : (s + 1) * deep], NT)
        if s:
            numer_ref[: plan.rows, :] += part
        else:
            numer_ref[: plan.rows, :] = part if before is None else part + before[...]


def numer_tail_body(plan, shards, stk_a, stk_b, data_ref, before, bits_ref, *refs):
    numer_ref, past, ahead, ahead2 = refs
    tail_ref = numer_ref.at[plan.rows :, :]
    tail_body(plan, shards, bits_ref, (stk_a, stk_b), tail_ref, past, ahead, ahead2)
    numer_body(plan, stk_b, data_ref, numer_ref, before)


def tail_start(plan, stk_ref, past, ahead):
    factors = plan.factors
    group = 2 * LANES // factors
    known = past[...]
    total = jnp.zeros((LAGS, LANES), F32)
    for first in range(0, LAGS, group):
        lags = range(first, first + group)
        rows = jnp.concatenate([known[LAGS - l : 2 * LAGS - l, :factors] for l in lags], 1)
        mat = jnp.concatenate([stk_ref[:factors, l * LANES : (l + 1) * LANES] for l in lags], 0)
        total += dot(rows.astype(BF16), mat)
    ahead[:LAGS, :] = jnp.zeros((LAGS, LANES), F32)
    ahead[LAGS:, :] = total


def tail_part(plan, stk_ref, ahead):
    factors = plan.factors
    beyond = ahead[...]
    high = beyond.astype(BF16).astype(F32)
    low = beyond - high
    out = jnp.zeros((2 * LAGS, factors), F32)
    for first in range(0, LAGS, 2):
        lags = range(first, first + 2)
        rows = jnp.concatenate(
            [jnp.concatenate([part[l : l + LAGS] for l in lags], 1) for part in (high, low)], 0
        )
        mat = stk_ref[:factors, first * LANES : (first + 2) * LANES]
        out += dot(rows.astype(BF16), mat, NT)
    return out[:LAGS] + out[LAGS:]


def tail_body(plan, shards, bits_ref, stks, out_ref, past, *aheads):
    out_ref[...] = jnp.zeros_like(out_ref)

    factors = plan.factors
    start = (plan.steps // PHASES + plan.edge) - (CHUNKS - 1) * plan.per
    ends = [
        bits_ref[row_tile(start + i), :].astype(F32)[CHUNKS - 1 :] for i in range(REACH)
    ]
    known = jnp.concatenate(ends, 0)
    past[...] = jnp.zeros_like(past)
    for p in range(PHASES):
        part = known[:, p * factors : (p + 1) * factors]
        part = jnp.concatenate([part, jnp.zeros((REACH, LANES - factors), F32)], 1)
        past[pl.ds(p, REACH, stride=PHASES), :] = part
    for stk_ref, ahead in zip(stks, aheads):
        tail_start(plan, stk_ref, past, ahead)
    over = sum(tail_part(plan, stk_ref, ahead) for stk_ref, ahead in zip(stks, aheads))
    past[:LAGS, :] = jnp.concatenate([over, jnp.zeros((LAGS, LANES - factors), F32)], 1)
    value = jnp.concatenate(
        [past[pl.ds(p, REACH, stride=PHASES), :][:, :factors] for p in range(PHASES)], 1
    )
    out_ref[...] = jnp.where(lax.axis_index("tm") == shards - 1, value, 0.0)


def taps_body(plan, auto_a, auto_b, high_ref, low_ref, line):
    factors, width = plan.factors, plan.width
    line[:, :width] = jnp.zeros((factors, width), F32)
    for a in range(REACH):
        rows = slice(a * factors, (a + 1) * factors)
        line[:, (REACH - a) * width : (REACH - a + 1) * width] = auto_a[rows, :] + auto_b[rows, :]
    zero = (REACH * PHASES + PHASES - 1) * factors
    back = [
        line[:, zero - d * factors : zero - (d - 1) * factors].T for d in range(1, PHASES)
    ]
    back.append(jnp.zeros((factors, factors), F32))
    line[:, (REACH + 1) * width :] = jnp.concatenate(back, 1)
    for s in range(REACH + 1):
        for p in range(PHASES):
            first = zero - (PHASES * s + p) * factors
            high, low = split(line[:, first : first + width])
            rows = slice(s * width + p * factors, s * width + (p + 1) * factors)
            high_ref[rows, :] = high
            low_ref[rows, :] = low


def conv_body(plan, offsets, bits_ref, high_ref, low_ref, *refs):
    before, out_ref = refs[:-1], refs[-1]
    width, rows = plan.width, plan.rows
    for i, s in enumerate(offsets):
        at = (REACH + s) * CHUNKS
        mat = slice(abs(s) * width, (abs(s) + 1) * width)
        dims = NN if s >= 0 else NT
        part = dot(bits_ref[at : at + rows, :], high_ref[mat, :], dims)
        part += dot(bits_ref[at : at + rows, :], low_ref[mat, :], dims)
        if i:
            out_ref[...] += part
        else:
            out_ref[...] = part + before[0][...] if before else part


def conv_tail_body(plan, shards, offsets, bits_ref, high_ref, low_ref, stk_a, stk_b, *refs):
    out_ref, tail_ref, past, ahead, ahead2 = refs
    tail_body(plan, shards, bits_ref, (stk_a, stk_b), tail_ref, past, ahead, ahead2)
    conv_body(plan, offsets, bits_ref, high_ref, low_ref, out_ref)


def first_conv_body(plan, offsets, auto_a, auto_b, bits_ref, high_ref, low_ref, out_ref, line):
    taps_body(plan, auto_a, auto_b, high_ref, low_ref, line)
    conv_body(plan, offsets, bits_ref, high_ref, low_ref, out_ref)


def penalties(plan, scale, grams, bits_ref, low_ref):
    factors, rows = plan.factors, plan.rows
    total = grams[0][...]
    if len(grams) > 1:
        here, far, both = (g[...] for g in grams[1:])
        odd = lax.axis_index("chan") % 2 == 1
        near = jnp.where(odd, far, here)
        next_one = jnp.where(odd, here, far)
        total = (total + near) + (next_one + both)
    r = lax.broadcasted_iota(jnp.int32, (factors, factors), 0)
    c = lax.broadcasted_iota(jnp.int32, (factors, factors), 1)
    off = jnp.where(r == c, 0.0, total) * scale
    blank = jnp.zeros((factors, factors), F32)
    high, low = split(
        jnp.concatenate(
            [
                jnp.concatenate([off if p == q else blank for q in range(PHASES)], 1)
                for p in range(PHASES)
            ],
            0,
        )
    )
    bits = bits_ref[REACH * CHUNKS : REACH * CHUNKS + rows, :]
    return dot(bits, high) + dot(bits, low) + dot(low_ref[...], high)


def new_tile(plan, shards, me, m, x_ref, den_ref, numer, pen, tails):
    at = row_tile(m)
    den = den_ref[at, :] + pen[at, :]
    j = lax.broadcasted_iota(jnp.int32, den.shape, 0)
    end = (plan.steps // PHASES + plan.edge) - (CHUNKS - 1) * plan.per
    if end - REACH <= m < end:
        i = m - end + REACH
        over = tails[0][i : i + 1, :] + tails[1][i : i + 1, :]
        den -= jnp.where((j == CHUNKS - 1) & (me == shards - 1), over, 0.0)
    new = x_ref[at, :] * numer / den
    if m < plan.edge:
        new = jnp.where((j == 0) & (me == 0), 0.0, new)
    if m >= end:
        new = jnp.where((j == CHUNKS - 1) & (me == shards - 1), 0.0, new)
    return new


def update_body(plan, scale, shards, counts, x_ref, bits_ref, low_ref, den_ref, *refs):
    numers, refs = refs[: counts[0]], refs[counts[0] :]
    if counts[0] > 1:
        tails = [numer[plan.rows :, :] for numer in numers]
    else:
        tails, refs = refs[:2], refs[2:]
    grams, refs = refs[: counts[1]], refs[counts[1] :]
    if counts[0] > 1:
        numer_ref, refs = refs[0], refs[1:]
    out_ref, out_bits, out_low, gram_ref, pen, both = refs
    factors, width = plan.factors, plan.width
    me = lax.axis_index("tm")
    pen[...] = penalties(plan, scale, grams, bits_ref, low_ref)
    end = (plan.steps // PHASES + plan.edge) - (CHUNKS - 1) * plan.per
    for m in range(plan.per):
        at = row_tile(m)
        numer = numers[0][at, :]
        if counts[0] > 1:
            numer = numer + numers[1][at, :]
            numer_ref[at, :] = numer
        new = new_tile(plan, shards, me, m, x_ref, den_ref, numer, pen, tails)
        out_ref[at, :] = new
        spread(plan, new, m, out_bits)
        high, low = split(new)
        out_low[at, :] = low
        j = lax.broadcasted_iota(jnp.int32, new.shape, 0)
        kept = new
        if m < plan.edge:
            kept = jnp.where(j == 0, 0.0, kept)
        if m >= end:
            kept = jnp.where(j == CHUNKS - 1, 0.0, kept)
        high, low = split(kept)
        both[at, :width] = high
        both[at, width:] = low
    same, cross = 0.0, 0.0
    for lanes in lane_tiles(width // LANES):
        ahead = slice(width + lanes.start, width + lanes.stop)
        full = dot(both[:, lanes], jnp.concatenate([both[:, lanes], both[:, ahead]], 1), TN)
        for p in range(LANES // factors):
            at = slice(p * factors, (p + 1) * factors)
            same += full[at, at]
            cross += full[at, LANES + at.start : LANES + at.stop]
    gram_ref[...] = same + cross + cross.T


def last_body(plan, scale, shards, counts, x_ref, bits_ref, low_ref, den_ref, *refs):
    numers, tails, grams = refs[: counts[0]], refs[counts[0] :][:2], refs[counts[0] + 2 :][: counts[1]]
    out_ref, pen, buf = refs[counts[0] + 2 + counts[1] :]
    me = lax.axis_index("tm")
    pen[...] = penalties(plan, scale, grams, bits_ref, low_ref)
    for m in range(plan.per):
        numer = sum(n[row_tile(m), :] for n in numers)
        new = new_tile(plan, shards, me, m, x_ref, den_ref, numer, pen, tails)
        for h, lanes in enumerate(lane_tiles(PHASES // 2)):
            at = PHASES * m + 2 * h
            buf[pl.ds(at, CHUNKS, stride=plan.stride), :] = new[:, lanes]
            turn = pltpu.roll(new[:, lanes], LANES // 2, 1)
            buf[pl.ds(at + 1, CHUNKS, stride=plan.stride), :] = turn
    for i, lanes in enumerate(lane_tiles(plan.steps // LANES)):
        at = plan.front + i * LANES
        out_ref[:, lanes] = buf[at : at + LANES, :].T[: plan.factors, :]


def swap(x, axis, bit):
    count = lax.axis_size(axis)
    return lax.ppermute(x, axis, [(i, i ^ bit) for i in range(count)])


def mixed(x, bit_even, bit_odd):
    wide = lax.axis_size("chan")
    pairs = []
    for t in range(lax.axis_size("tm")):
        for c in range(wide):
            far = t ^ (bit_odd if c % 2 else bit_even)
            pairs.append((t * wide + c, far * wide + c))
    return lax.ppermute(x, ("tm", "chan"), pairs)


def shifted(x, axis, by):
    count = lax.axis_size(axis)
    return lax.ppermute(x, axis, [(i, i + by) for i in range(count) if 0 <= i + by < count])


def between(x):
    count, wide = lax.axis_size("tm"), lax.axis_size("chan")
    pairs = []
    for t in range(count):
        far = t + (1 if t % 2 else -1)
        for c in range(wide):
            target = (far, c) if 0 <= far < count else (t, c ^ (wide // 2))
            pairs.append((t * wide + c, target[0] * wide + target[1]))
    return lax.ppermute(x, ("tm", "chan"), pairs)


def doubling(axis):
    count = lax.axis_size(axis)
    bits = [1 << b for b in range(count.bit_length() - 1)]
    return bits[1:] + bits[:1]


def after(x, *others):
    return lax.optimization_barrier((x, *others))[0]


def gram_rounds(x, odd, *meanwhile):
    bits = doubling("tm")
    singles, pairs = bits[-1:], bits[:-1]
    if len(pairs) % 2:
        singles, pairs = singles + pairs[-1:], pairs[:-1]
    gaps = list(meanwhile)

    def gap(*values):
        others = gaps.pop(0) if gaps else ()
        return lax.optimization_barrier(values + others)[: len(values)]

    for bit in singles:
        x = x + gap(swap(x, "tm", bit))[0]
    terms = [x]
    while pairs:
        one, two, pairs = pairs[0], pairs[1], pairs[2:]
        here, both = gap(mixed(x, one, two), swap(x, "tm", one ^ two))
        far = swap(here, "chan", 1)
        terms = [x, here, far, both]
        if pairs:
            near, other = jnp.where(odd, far, here), jnp.where(odd, here, far)
            x = (x + near) + (other + both)
    return terms


def on_device(data, motifs, loadings):
    channels, steps = data.shape
    factors = loadings.shape[0]
    plan = Plan(steps, factors)
    shards = lax.axis_size("tm")
    width, rows = plan.width, plan.rows
    ext_rows = plan.ext * CHUNKS
    sds = jax.ShapeDtypeStruct
    me = lax.axis_index("tm")
    odd = lax.axis_index("chan") % 2 == 1

    rim = sds((2 * factors + channels, LANES), BF16)
    data_in, even, gram, near_rim, wide_rim = call(
        functools.partial(first_body, plan),
        (
            sds(data.shape, BF16),
            sds((1,) + motifs.shape, BF16),
            sds((factors, factors), F32),
            rim,
            rim,
        ),
        [pl.BlockSpec(memory_space=pltpu.HBM)] * 3,
        [
            pltpu.VMEM(loadings.shape, F32),
            pltpu.SemaphoreType.DMA((3,)),
        ],
        limit=53,
    )(loadings, data, motifs)

    moved = motifs.shape[1] == GROUP * LAGS
    bits = doubling("tm")
    tracks = (bits, bits)

    def gather_round(x, i):
        return mixed(x, tracks[0][i], tracks[1][i])

    for i, bit in enumerate(bits[:-1]):
        near = gather_round(even if i else motifs[None], i)
        if i:
            gram_near = swap(gram, "tm", bits[i - 1])
            if i == 1:
                wide_rim = between(wide_rim)
                far_data = swap(data, "chan", 2)
                near_rim = swap(after(near_rim, even), "tm", bits[-1])
                near, gram_near, near_rim, far_data = lax.optimization_barrier(
                    (near, gram_near, near_rim, far_data)
                )
            else:
                near, gram_near = lax.optimization_barrier((near, gram_near))
            gram = gram + gram_near
        even = jnp.concatenate([even, near], 0)
    odds = gather_round(even, len(bits) - 1)
    far_even = swap(even, "chan", 2)
    gram_near = swap(gram, "tm", bits[-1])
    right_side = me % 2 == 1
    nothing = jnp.zeros_like(wide_rim)
    left = jnp.where(me == 0, nothing, jnp.where(right_side, near_rim, wide_rim))
    right = jnp.where(me == shards - 1, nothing, jnp.where(right_side, wide_rim, near_rim))
    if not moved:
        order = [0]
        for bit in bits:
            order = order + [o ^ bit for o in order]
        slots = jnp.concatenate([even, odds], 0)
        index = jnp.array([order.index(b) for b in range(shards)], jnp.int32)
        slots = jnp.take(slots, jnp.take(index, jnp.arange(shards) ^ me), axis=0)
        slots = jnp.moveaxis(slots, 0, 1).reshape(channels, -1, GROUP * LAGS)
        slots = jnp.moveaxis(slots, 1, 0)
        even, odds = slots[0::2], slots[1::2]
        far_even = swap(even, "chan", 2)

    def lay(*fields):
        return call(
            functools.partial(lay_data, plan),
            sds(((plan.per + REACH) * CHUNKS, PHASES * LANES), BF16),
            vmem(len(fields)),
            [pltpu.VMEM((steps + 2 * LANES, LANES), F32)],
        )(*fields)

    field, window = sds((rows, width), F32), sds((ext_rows, width), BF16)
    low_field, rest = sds((rows, width), BF16), sds((REACH, width), F32)
    tail_room = [pltpu.VMEM((2 * LAGS, LANES), F32)] * 3
    rims = jnp.concatenate([left[2 * factors :], right[2 * factors :]], 1)
    own_laid = lay(data_in, rims)
    x, bits_x, low_x = call(
        functools.partial(lay_loadings, plan),
        (field, window, low_field),
        vmem(3),
        [pltpu.VMEM((steps + 2 * LANES, LANES), F32)],
    )(loadings, left, right)
    odds, far_even, gram_near, own_laid, x, bits_x = lax.optimization_barrier(
        (odds, far_even, gram_near, own_laid, x, bits_x)
    )
    gram = gram + gram_near
    gram_near = swap(gram, "tm", bits[-2])
    far_odds = swap(jnp.concatenate([odds, rims[None]], 0), "chan", 2)
    far_odds, gram_near = lax.optimization_barrier((far_odds, gram_near))
    gram = gram + gram_near
    far_rims = far_odds[-1]

    def autos(evens, odd_ones, *before):
        return call(
            functools.partial(auto_body, plan, moved),
            (sds((width, plan.tiles * LANES), BF16), sds((REACH * factors, width), F32)),
            vmem(2 + len(before)),
            [pltpu.VMEM((LANES, factors * LAGS), BF16)],
        )(evens, odd_ones, *before)

    stk, auto = autos(even, odds)
    numer = call(functools.partial(numer_body, plan), field, vmem(2))(stk, own_laid)
    far_odds, numer = lax.optimization_barrier((far_odds, numer))
    far_stk, auto = autos(far_even, far_odds, auto)
    far_data, far_rims, auto = lax.optimization_barrier((far_data, far_rims, auto))
    auto_far = swap(auto, "chan", 1)
    numer = call(
        functools.partial(numer_tail_body, plan, shards),
        sds((rows + REACH, width), F32),
        vmem(5),
        tail_room,
    )(stk, far_stk, lay(far_data, far_rims), numer, bits_x)
    numer, auto_far = lax.optimization_barrier((numer, auto_far))
    numer_far = swap(numer, "chan", 1)
    grams = [gram]

    mats = sds(((REACH + 1) * width, width), BF16)
    every = list(range(-REACH, REACH + 1))
    high, low, den = call(
        functools.partial(first_conv_body, plan, every),
        (mats, mats, sds((rows, width), F32)),
        vmem(3),
        [pltpu.VMEM((factors, (REACH + 2) * width), F32)],
    )(auto, auto_far, bits_x)

    def conv(offsets, bits_now, before):
        return call(functools.partial(conv_body, plan, offsets), field, vmem(4))(
            bits_now, high, low, before
        )

    def conv_tail(offsets, bits_now):
        return call(
            functools.partial(conv_tail_body, plan, shards, offsets),
            (field, rest),
            vmem(5),
            tail_room,
        )(bits_now, high, low, stk, far_stk)

    scale = PENALTY / (steps * shards)
    numers_now = (numer, numer_far)
    for sweep in range(ITERS):
        if sweep:
            part, tail = conv_tail(every[:REACH], bits_x)
            tails = (tail, swap(tail, "chan", 1))
            den = conv(every[REACH:], bits_x, part)
            grams = gram_rounds(gram, odd, (part,), (den, tails[1]))
        else:
            tails = ()
        operands = (x, bits_x, low_x, den, *numers_now, *tails, *grams)
        counts = (len(numers_now), len(grams))
        if sweep == ITERS - 1:
            return call(
                functools.partial(last_body, plan, scale, shards, counts),
                sds((factors, steps), F32),
                vmem(len(operands)),
                [pltpu.VMEM((rows, width), F32), pltpu.VMEM((steps + 2 * LANES, LANES), F32)],
            )(*operands)
        outs = (field, window, low_field, sds((factors, factors), F32))
        if counts[0] > 1:
            outs = (field,) + outs
        got = call(
            functools.partial(update_body, plan, scale, shards, counts),
            outs,
            vmem(len(operands)),
            [pltpu.VMEM((rows, width), F32), pltpu.VMEM((rows, 2 * width), BF16)],
        )(*operands)
        if counts[0] > 1:
            numers_now, got = got[:1], got[1:]
        x, bits_x, low_x, gram = got


def solution(mesh):
    in_specs = (P("chan", "tm"), P("chan", "tm"), P(None, "tm"))
    out_specs = P(None, "tm")
    return jax.shard_map(
        on_device, mesh=mesh, in_specs=in_specs, out_specs=out_specs, check_vma=False
    )
```

```python
import functools

import jax
import jax.numpy as jnp
from jax import lax
from jax.experimental import pallas as pl
from jax.experimental.pallas import tpu as pltpu
from jax.sharding import PartitionSpec as P

LAGS = 32
ITERS = 3
PENALTY = 0.2

PHASES = 4
CHUNKS = 16
REACH = LAGS // PHASES
LANES = 128
GROUP = 8

NT = (((1,), (1,)), ((), ()))
NN = (((1,), (0,)), ((), ()))
TN = (((0,), (0,)), ((), ()))
F32 = jnp.float32
BF16 = jnp.bfloat16


def dot(a, b, dims=NN):
    return lax.dot_general(a, b, dims, preferred_element_type=F32)


def split(a):
    high = a.astype(BF16)
    return high, (a - high.astype(F32)).astype(BF16)


def vmem(n=1):
    return [pl.BlockSpec(memory_space=pltpu.VMEM)] * n


def smem(n=1):
    return [pl.BlockSpec(memory_space=pltpu.SMEM)] * n


def call(body, out_shape, in_specs, scratch=(), flops=0, moved=0, limit=16):
    return pl.pallas_call(
        body,
        out_shape=out_shape,
        in_specs=in_specs,
        out_specs=jax.tree.map(lambda _: pl.BlockSpec(memory_space=pltpu.VMEM), out_shape),
        scratch_shapes=list(scratch),
        compiler_params=pltpu.CompilerParams(vmem_limit_bytes=limit * 2**20),
        cost_estimate=pl.CostEstimate(flops=flops, bytes_accessed=moved, transcendentals=0),
    )


class Plan:
    def __init__(self, steps, factors):
        self.steps = steps
        self.factors = factors
        self.width = PHASES * factors
        self.edge = 2 * REACH
        self.rows = steps // PHASES + 2 * self.edge
        self.per = self.rows // CHUNKS
        self.ext = self.per + 2 * REACH
        self.stride = PHASES * self.per
        self.halo = PHASES * (self.edge + REACH)
        self.front = PHASES * self.edge
        self.back = PHASES * (self.edge + REACH)
        wide = steps + 2 * self.halo
        self.wide = -(-wide // LANES) * LANES
        self.tiles = LAGS + PHASES


def lane_tiles(count):
    return [slice(i * LANES, (i + 1) * LANES) for i in range(count)]


def row_tile(m):
    return slice(m * CHUNKS, (m + 1) * CHUNKS)


def turned(buf, left, fields, right):
    middle = [field[:, at] for field in fields for at in lane_tiles(field.shape[1] // LANES)]
    parts = [left] + middle + [right]
    for i, part in enumerate(parts):
        part = part.astype(F32)
        spare = LANES - part.shape[0]
        low = part if spare == part.shape[0] else jnp.zeros((spare, LANES), F32)
        buf[i * LANES : (i + 1) * LANES, :] = jnp.concatenate([part, low], 0).T


def spread(plan, tile, m, bits_ref):
    j = lax.broadcasted_iota(jnp.int32, tile.shape, 0)
    bits_ref[row_tile(m + REACH), :] = tile.astype(BF16)
    if m >= plan.per - REACH:
        low = jnp.where(j == 0, 0.0, pltpu.roll(tile, 1, 0))
        bits_ref[row_tile(m - plan.per + REACH), :] = low.astype(BF16)
    if m < REACH:
        high = jnp.where(j == CHUNKS - 1, 0.0, pltpu.roll(tile, CHUNKS - 1, 0))
        bits_ref[row_tile(m + plan.per + REACH), :] = high.astype(BF16)


def lay_loadings(plan, load_ref, left_ref, right_ref, x_ref, bits_ref, low_ref, buf):
    factors = plan.factors
    left, right = (
        ref[:factors, :].astype(F32) + ref[factors : 2 * factors, :].astype(F32)
        for ref in (left_ref, right_ref)
    )
    turned(buf, left, (load_ref,), right)
    lane = lax.broadcasted_iota(jnp.int32, (CHUNKS, LANES), 1)
    skip = LANES - plan.halo
    for m in range(plan.ext):
        halves = []
        for h in range(PHASES // 2):
            at = skip + PHASES * m + 2 * h
            even = buf[pl.ds(at, CHUNKS, stride=plan.stride), :]
            odd = buf[pl.ds(at + 1, CHUNKS, stride=plan.stride), :]
            halves.append(jnp.where(lane < factors, even, odd))
        tile = jnp.concatenate(halves, 1)
        bits = tile.astype(BF16)
        bits_ref[row_tile(m), :] = bits
        if REACH <= m < REACH + plan.per:
            x_ref[row_tile(m - REACH), :] = tile
            low_ref[row_tile(m - REACH), :] = (tile - bits.astype(F32)).astype(BF16)


def lay_data(plan, *refs):
    fields, (rims_ref, out_ref, buf) = refs[:-3], refs[-3:]
    turned(buf, rims_ref[:, :LANES], fields, rims_ref[:, LANES:])
    skip = LANES - plan.front
    for m in range(plan.per + REACH):
        for p, at in enumerate(lane_tiles(PHASES)):
            rows = pl.ds(skip + PHASES * m + p, CHUNKS, stride=plan.stride)
            out_ref[row_tile(m), at] = buf[rows, :].astype(BF16)


def first_body(plan, load_any, data_any, motif_any, *refs):
    data_ref, motif_ref, gram_ref, near_ref, wide_ref, load_ref, sems = refs
    factors = plan.factors
    moves = [
        pltpu.make_async_copy(source, target, sems.at[i])
        for i, (source, target) in enumerate(
            ((load_any, load_ref), (data_any, data_ref), (motif_any, motif_ref.at[0]))
        )
    ]
    for move in moves:
        move.start()
    for move in moves:
        move.wait()
    odd = lax.axis_index("tm") % 2 == 1
    head, tail = slice(0, LANES), slice(plan.steps - LANES, plan.steps)
    for rim_ref, even_at, odd_at in ((near_ref, tail, head), (wide_ref, head, tail)):
        high, low = split(jnp.where(odd, load_ref[:, odd_at], load_ref[:, even_at]))
        rim_ref[:factors, :] = high
        rim_ref[factors : 2 * factors, :] = low
        rim_ref[2 * factors :, :] = jnp.where(
            odd, data_ref[:, odd_at].astype(F32), data_ref[:, even_at].astype(F32)
        ).astype(BF16)
    high, low = split(load_ref[...])
    cross = dot(high, low, NT)
    gram_ref[...] = dot(high, high, NT) + cross + cross.T


def lay_motifs(plan, me, crossed, first_ref, second_ref, stk_ref, padded):
    factors = plan.factors
    channels = first_ref.shape[1]
    span = GROUP * LAGS
    padded[channels:, :] = jnp.zeros((LANES - channels, padded.shape[1]), BF16)
    row = lax.broadcasted_iota(jnp.int32, (span, span), 0)
    col = lax.broadcasted_iota(jnp.int32, (span, span), 1)
    pick = jnp.where(col == (row % GROUP) * LAGS + row // GROUP, 1.0, 0.0).astype(BF16)
    for q in range(PHASES):
        rows = slice(q * factors, (q + 1) * factors)
        if q:
            stk_ref[rows, : q * LANES] = jnp.zeros((factors, q * LANES), BF16)
        stk_ref[rows, (LAGS + q) * LANES :] = jnp.zeros((factors, (PHASES - q) * LANES), BF16)
    for pair in range(factors // (2 * GROUP)):
        halves = []
        for block in (2 * pair, 2 * pair + 1):
            room = slice(block * span, (block + 1) * span)
            step = block ^ me
            index, late = step // 2, step % 2
            if crossed is not None:
                index = jnp.where(crossed, (step // 2) % 2 + 2 * (step % 2), index)
                late = jnp.where(crossed, step // 4, late)
            one, two = first_ref[index].astype(F32), second_ref[index].astype(F32)
            padded[:channels, room] = jnp.where(late == 1, two, one).astype(BF16)
            halves.append(dot(pick, padded[:, room], NT))
        for lag in range(LAGS):
            cut = slice(lag * GROUP, (lag + 1) * GROUP)
            tile = jnp.concatenate([halves[0][cut], halves[1][cut]], 0).astype(BF16)
            for q in range(PHASES):
                first = q * factors + pair * 2 * GROUP
                stk_ref[first : first + 2 * GROUP, (lag + q) * LANES : (lag + q + 1) * LANES] = tile


def auto_body(plan, moved, first_ref, second_ref, *refs):
    before, (stk_ref, auto_ref, padded) = refs[:-3], refs[-3:]
    factors = plan.factors
    me = lax.axis_index("tm") if moved else 0
    crossed = None
    lay_motifs(plan, me, crossed, first_ref, second_ref, stk_ref, padded)
    last = (PHASES - 1) * factors
    deep = PHASES * LANES
    auto_ref[...] = before[0][...] if before else jnp.zeros_like(auto_ref)
    for u in range(REACH + 1):
        taps = min(u + 1, REACH)
        cuts = [slice((u - a) * deep, (u - a + 1) * deep) for a in range(taps)]
        left = jnp.concatenate([stk_ref[last : last + factors, cut] for cut in cuts], 0)
        auto_ref[: taps * factors, :] += dot(left, stk_ref[:, u * deep : (u + 1) * deep], NT)


def numer_body(plan, stk_ref, data_ref, numer_ref, before=None):
    deep = PHASES * LANES
    for s in range(REACH + 1):
        rows = slice(s * CHUNKS, s * CHUNKS + plan.rows)
        part = dot(data_ref[rows, :], stk_ref[:, s * deep : (s + 1) * deep], NT)
        if s:
            numer_ref[: plan.rows, :] += part
        else:
            numer_ref[: plan.rows, :] = part if before is None else part + before[...]


def numer_tail_body(plan, shards, stk_a, stk_b, data_ref, before, bits_ref, *refs):
    numer_ref, past, ahead, ahead2 = refs
    tail_ref = numer_ref.at[plan.rows :, :]
    tail_body(plan, shards, bits_ref, (stk_a, stk_b), tail_ref, past, ahead, ahead2)
    numer_body(plan, stk_b, data_ref, numer_ref, before)


def tail_start(plan, stk_ref, past, ahead):
    factors = plan.factors
    group = 2 * LANES // factors
    known = past[...]
    total = jnp.zeros((LAGS, LANES), F32)
    for first in range(0, LAGS, group):
        lags = range(first, first + group)
        rows = jnp.concatenate([known[LAGS - l : 2 * LAGS - l, :factors] for l in lags], 1)
        mat = jnp.concatenate([stk_ref[:factors, l * LANES : (l + 1) * LANES] for l in lags], 0)
        total += dot(rows.astype(BF16), mat)
    ahead[:LAGS, :] = jnp.zeros((LAGS, LANES), F32)
    ahead[LAGS:, :] = total


def tail_part(plan, stk_ref, ahead):
    factors = plan.factors
    beyond = ahead[...]
    high = beyond.astype(BF16).astype(F32)
    low = beyond - high
    out = jnp.zeros((2 * LAGS, factors), F32)
    for first in range(0, LAGS, 2):
        lags = range(first, first + 2)
        rows = jnp.concatenate(
            [jnp.concatenate([part[l : l + LAGS] for l in lags], 1) for part in (high, low)], 0
        )
        mat = stk_ref[:factors, first * LANES : (first + 2) * LANES]
        out += dot(rows.astype(BF16), mat, NT)
    return out[:LAGS] + out[LAGS:]


def tail_body(plan, shards, bits_ref, stks, out_ref, past, *aheads):
    out_ref[...] = jnp.zeros_like(out_ref)

    factors = plan.factors
    start = (plan.steps // PHASES + plan.edge) - (CHUNKS - 1) * plan.per
    ends = [
        bits_ref[row_tile(start + i), :].astype(F32)[CHUNKS - 1 :] for i in range(REACH)
    ]
    known = jnp.concatenate(ends, 0)
    past[...] = jnp.zeros_like(past)
    for p in range(PHASES):
        part = known[:, p * factors : (p + 1) * factors]
        part = jnp.concatenate([part, jnp.zeros((REACH, LANES - factors), F32)], 1)
        past[pl.ds(p, REACH, stride=PHASES), :] = part
    for stk_ref, ahead in zip(stks, aheads):
        tail_start(plan, stk_ref, past, ahead)
    over = sum(tail_part(plan, stk_ref, ahead) for stk_ref, ahead in zip(stks, aheads))
    past[:LAGS, :] = jnp.concatenate([over, jnp.zeros((LAGS, LANES - factors), F32)], 1)
    value = jnp.concatenate(
        [past[pl.ds(p, REACH, stride=PHASES), :][:, :factors] for p in range(PHASES)], 1
    )
    out_ref[...] = jnp.where(lax.axis_index("tm") == shards - 1, value, 0.0)


def taps_body(plan, auto_a, auto_b, high_ref, low_ref, line):
    factors, width = plan.factors, plan.width
    line[:, :width] = jnp.zeros((factors, width), F32)
    for a in range(REACH):
        rows = slice(a * factors, (a + 1) * factors)
        line[:, (REACH - a) * width : (REACH - a + 1) * width] = auto_a[rows, :] + auto_b[rows, :]
    zero = (REACH * PHASES + PHASES - 1) * factors
    back = [
        line[:, zero - d * factors : zero - (d - 1) * factors].T for d in range(1, PHASES)
    ]
    back.append(jnp.zeros((factors, factors), F32))
    line[:, (REACH + 1) * width :] = jnp.concatenate(back, 1)
    for s in range(REACH + 1):
        for p in range(PHASES):
            first = zero - (PHASES * s + p) * factors
            high, low = split(line[:, first : first + width])
            rows = slice(s * width + p * factors, s * width + (p + 1) * factors)
            high_ref[rows, :] = high
            low_ref[rows, :] = low


def conv_body(plan, offsets, bits_ref, high_ref, low_ref, *refs):
    before, out_ref = refs[:-1], refs[-1]
    width, rows = plan.width, plan.rows
    for i, s in enumerate(offsets):
        at = (REACH + s) * CHUNKS
        mat = slice(abs(s) * width, (abs(s) + 1) * width)
        dims = NN if s >= 0 else NT
        part = dot(bits_ref[at : at + rows, :], high_ref[mat, :], dims)
        part += dot(bits_ref[at : at + rows, :], low_ref[mat, :], dims)
        if i:
            out_ref[...] += part
        else:
            out_ref[...] = part + before[0][...] if before else part


def conv_tail_body(plan, shards, offsets, bits_ref, high_ref, low_ref, stk_a, stk_b, *refs):
    out_ref, tail_ref, past, ahead, ahead2 = refs
    tail_body(plan, shards, bits_ref, (stk_a, stk_b), tail_ref, past, ahead, ahead2)
    conv_body(plan, offsets, bits_ref, high_ref, low_ref, out_ref)


def first_conv_body(plan, offsets, auto_a, auto_b, bits_ref, high_ref, low_ref, out_ref, line):
    taps_body(plan, auto_a, auto_b, high_ref, low_ref, line)
    conv_body(plan, offsets, bits_ref, high_ref, low_ref, out_ref)


def penalties(plan, scale, grams, bits_ref, low_ref):
    factors, rows = plan.factors, plan.rows
    total = grams[0][...]
    if len(grams) > 1:
        here, far, both = (g[...] for g in grams[1:])
        odd = lax.axis_index("chan") % 2 == 1
        near = jnp.where(odd, far, here)
        next_one = jnp.where(odd, here, far)
        total = (total + near) + (next_one + both)
    r = lax.broadcasted_iota(jnp.int32, (factors, factors), 0)
    c = lax.broadcasted_iota(jnp.int32, (factors, factors), 1)
    off = jnp.where(r == c, 0.0, total) * scale
    blank = jnp.zeros((factors, factors), F32)
    high, low = split(
        jnp.concatenate(
            [
                jnp.concatenate([off if p == q else blank for q in range(PHASES)], 1)
                for p in range(PHASES)
            ],
            0,
        )
    )
    bits = bits_ref[REACH * CHUNKS : REACH * CHUNKS + rows, :]
    return dot(bits, high) + dot(bits, low) + dot(low_ref[...], high)


def new_tile(plan, shards, me, m, x_ref, den_ref, numer, pen, tails):
    at = row_tile(m)
    den = den_ref[at, :] + pen[at, :]
    j = lax.broadcasted_iota(jnp.int32, den.shape, 0)
    end = (plan.steps // PHASES + plan.edge) - (CHUNKS - 1) * plan.per
    if end - REACH <= m < end:
        i = m - end + REACH
        over = tails[0][i : i + 1, :] + tails[1][i : i + 1, :]
        den -= jnp.where((j == CHUNKS - 1) & (me == shards - 1), over, 0.0)
    new = x_ref[at, :] * numer / den
    if m < plan.edge:
        new = jnp.where((j == 0) & (me == 0), 0.0, new)
    if m >= end:
        new = jnp.where((j == CHUNKS - 1) & (me == shards - 1), 0.0, new)
    return new


def update_body(plan, scale, shards, counts, x_ref, bits_ref, low_ref, den_ref, *refs):
    numers, refs = refs[: counts[0]], refs[counts[0] :]
    if counts[0] > 1:
        tails = [numer[plan.rows :, :] for numer in numers]
    else:
        tails, refs = refs[:2], refs[2:]
    grams, refs = refs[: counts[1]], refs[counts[1] :]
    if counts[0] > 1:
        numer_ref, refs = refs[0], refs[1:]
    out_ref, out_bits, out_low, gram_ref, pen, both = refs
    factors, width = plan.factors, plan.width
    me = lax.axis_index("tm")
    pen[...] = penalties(plan, scale, grams, bits_ref, low_ref)
    end = (plan.steps // PHASES + plan.edge) - (CHUNKS - 1) * plan.per
    for m in range(plan.per):
        at = row_tile(m)
        numer = numers[0][at, :]
        if counts[0] > 1:
            numer = numer + numers[1][at, :]
            numer_ref[at, :] = numer
        new = new_tile(plan, shards, me, m, x_ref, den_ref, numer, pen, tails)
        out_ref[at, :] = new
        spread(plan, new, m, out_bits)
        high, low = split(new)
        out_low[at, :] = low
        j = lax.broadcasted_iota(jnp.int32, new.shape, 0)
        kept = new
        if m < plan.edge:
            kept = jnp.where(j == 0, 0.0, kept)
        if m >= end:
            kept = jnp.where(j == CHUNKS - 1, 0.0, kept)
        high, low = split(kept)
        both[at, :width] = high
        both[at, width:] = low
    same, cross = 0.0, 0.0
    for lanes in lane_tiles(width // LANES):
        ahead = slice(width + lanes.start, width + lanes.stop)
        full = dot(both[:, lanes], jnp.concatenate([both[:, lanes], both[:, ahead]], 1), TN)
        for p in range(LANES // factors):
            at = slice(p * factors, (p + 1) * factors)
            same += full[at, at]
            cross += full[at, LANES + at.start : LANES + at.stop]
    gram_ref[...] = same + cross + cross.T


def last_body(plan, scale, shards, counts, x_ref, bits_ref, low_ref, den_ref, *refs):
    numers, tails, grams = refs[: counts[0]], refs[counts[0] :][:2], refs[counts[0] + 2 :][: counts[1]]
    out_ref, pen, buf = refs[counts[0] + 2 + counts[1] :]
    me = lax.axis_index("tm")
    pen[...] = penalties(plan, scale, grams, bits_ref, low_ref)
    for m in range(plan.per):
        numer = sum(n[row_tile(m), :] for n in numers)
        new = new_tile(plan, shards, me, m, x_ref, den_ref, numer, pen, tails)
        for h, lanes in enumerate(lane_tiles(PHASES // 2)):
            at = PHASES * m + 2 * h
            buf[pl.ds(at, CHUNKS, stride=plan.stride), :] = new[:, lanes]
            turn = pltpu.roll(new[:, lanes], LANES // 2, 1)
            buf[pl.ds(at + 1, CHUNKS, stride=plan.stride), :] = turn
    for i, lanes in enumerate(lane_tiles(plan.steps // LANES)):
        at = plan.front + i * LANES
        out_ref[:, lanes] = buf[at : at + LANES, :].T[: plan.factors, :]


def swap(x, axis, bit):
    count = lax.axis_size(axis)
    return lax.ppermute(x, axis, [(i, i ^ bit) for i in range(count)])


def mixed(x, bit_even, bit_odd):
    wide = lax.axis_size("chan")
    pairs = []
    for t in range(lax.axis_size("tm")):
        for c in range(wide):
            far = t ^ (bit_odd if c % 2 else bit_even)
            pairs.append((t * wide + c, far * wide + c))
    return lax.ppermute(x, ("tm", "chan"), pairs)


def shifted(x, axis, by):
    count = lax.axis_size(axis)
    return lax.ppermute(x, axis, [(i, i + by) for i in range(count) if 0 <= i + by < count])


def between(x):
    count, wide = lax.axis_size("tm"), lax.axis_size("chan")
    pairs = []
    for t in range(count):
        far = t + (1 if t % 2 else -1)
        for c in range(wide):
            target = (far, c) if 0 <= far < count else (t, c ^ (wide // 2))
            pairs.append((t * wide + c, target[0] * wide + target[1]))
    return lax.ppermute(x, ("tm", "chan"), pairs)


def doubling(axis):
    count = lax.axis_size(axis)
    bits = [1 << b for b in range(count.bit_length() - 1)]
    return bits[1:] + bits[:1]


def after(x, *others):
    return lax.optimization_barrier((x, *others))[0]


def gram_rounds(x, odd, *meanwhile):
    bits = doubling("tm")
    singles, pairs = bits[-1:], bits[:-1]
    if len(pairs) % 2:
        singles, pairs = singles + pairs[-1:], pairs[:-1]
    gaps = list(meanwhile)

    def gap(*values):
        others = gaps.pop(0) if gaps else ()
        return lax.optimization_barrier(values + others)[: len(values)]

    for bit in singles:
        x = x + gap(swap(x, "tm", bit))[0]
    terms = [x]
    while pairs:
        one, two, pairs = pairs[0], pairs[1], pairs[2:]
        here, both = gap(mixed(x, one, two), swap(x, "tm", one ^ two))
        far = swap(here, "chan", 1)
        terms = [x, here, far, both]
        if pairs:
            near, other = jnp.where(odd, far, here), jnp.where(odd, here, far)
            x = (x + near) + (other + both)
    return terms


def on_device(data, motifs, loadings):
    channels, steps = data.shape
    factors = loadings.shape[0]
    plan = Plan(steps, factors)
    shards = lax.axis_size("tm")
    width, rows = plan.width, plan.rows
    ext_rows = plan.ext * CHUNKS
    sds = jax.ShapeDtypeStruct
    me = lax.axis_index("tm")
    odd = lax.axis_index("chan") % 2 == 1

    rim = sds((2 * factors + channels, LANES), BF16)
    data_in, even, gram, near_rim, wide_rim = call(
        functools.partial(first_body, plan),
        (
            sds(data.shape, BF16),
            sds((1,) + motifs.shape, BF16),
            sds((factors, factors), F32),
            rim,
            rim,
        ),
        [pl.BlockSpec(memory_space=pltpu.HBM)] * 3,
        [
            pltpu.VMEM(loadings.shape, F32),
            pltpu.SemaphoreType.DMA((3,)),
        ],
        limit=53,
    )(loadings, data, motifs)

    moved = motifs.shape[1] == GROUP * LAGS
    bits = doubling("tm")
    tracks = (bits, bits)

    def gather_round(x, i):
        return mixed(x, tracks[0][i], tracks[1][i])

    for i, bit in enumerate(bits[:-1]):
        near = gather_round(even if i else motifs[None], i)
        if i:
            gram_near = swap(gram, "tm", bits[i - 1])
            if i == 1:
                wide_rim = between(wide_rim)
                far_data = swap(data, "chan", 2)
                near_rim = swap(after(near_rim, even), "tm", bits[-1])
                near, gram_near, near_rim, far_data = lax.optimization_barrier(
                    (near, gram_near, near_rim, far_data)
                )
            else:
                near, gram_near = lax.optimization_barrier((near, gram_near))
            gram = gram + gram_near
        even = jnp.concatenate([even, near], 0)
    odds = gather_round(even, len(bits) - 1)
    far_even = swap(even, "chan", 2)
    gram_near = swap(gram, "tm", bits[-1])
    right_side = me % 2 == 1
    nothing = jnp.zeros_like(wide_rim)
    left = jnp.where(me == 0, nothing, jnp.where(right_side, near_rim, wide_rim))
    right = jnp.where(me == shards - 1, nothing, jnp.where(right_side, wide_rim, near_rim))
    if not moved:
        order = [0]
        for bit in bits:
            order = order + [o ^ bit for o in order]
        slots = jnp.concatenate([even, odds], 0)
        index = jnp.array([order.index(b) for b in range(shards)], jnp.int32)
        slots = jnp.take(slots, jnp.take(index, jnp.arange(shards) ^ me), axis=0)
        slots = jnp.moveaxis(slots, 0, 1).reshape(channels, -1, GROUP * LAGS)
        slots = jnp.moveaxis(slots, 1, 0)
        even, odds = slots[0::2], slots[1::2]
        far_even = swap(even, "chan", 2)

    def lay(*fields):
        return call(
            functools.partial(lay_data, plan),
            sds(((plan.per + REACH) * CHUNKS, PHASES * LANES), BF16),
            vmem(len(fields)),
            [pltpu.VMEM((steps + 2 * LANES, LANES), F32)],
        )(*fields)

    field, window = sds((rows, width), F32), sds((ext_rows, width), BF16)
    low_field, rest = sds((rows, width), BF16), sds((REACH, width), F32)
    tail_room = [pltpu.VMEM((2 * LAGS, LANES), F32)] * 3
    rims = jnp.concatenate([left[2 * factors :], right[2 * factors :]], 1)
    own_laid = lay(data_in, rims)
    x, bits_x, low_x = call(
        functools.partial(lay_loadings, plan),
        (field, window, low_field),
        vmem(3),
        [pltpu.VMEM((steps + 2 * LANES, LANES), F32)],
    )(loadings, left, right)
    odds, far_even, gram_near, own_laid, x, bits_x = lax.optimization_barrier(
        (odds, far_even, gram_near, own_laid, x, bits_x)
    )
    gram = gram + gram_near
    gram_near = swap(gram, "tm", bits[-2])
    far_odds = swap(jnp.concatenate([odds, rims[None]], 0), "chan", 2)
    far_odds, gram_near = lax.optimization_barrier((far_odds, gram_near))
    gram = gram + gram_near
    far_rims = far_odds[-1]

    def autos(evens, odd_ones, *before):
        return call(
            functools.partial(auto_body, plan, moved),
            (sds((width, plan.tiles * LANES), BF16), sds((REACH * factors, width), F32)),
            vmem(2 + len(before)),
            [pltpu.VMEM((LANES, factors * LAGS), BF16)],
        )(evens, odd_ones, *before)

    stk, auto = autos(even, odds)
    numer = call(functools.partial(numer_body, plan), field, vmem(2))(stk, own_laid)
    far_odds, numer = lax.optimization_barrier((far_odds, numer))
    far_stk, auto = autos(far_even, far_odds, auto)
    far_data, far_rims, auto = lax.optimization_barrier((far_data, far_rims, auto))
    auto_far = swap(auto, "chan", 1)
    numer = call(
        functools.partial(numer_tail_body, plan, shards),
        sds((rows + REACH, width), F32),
        vmem(5),
        tail_room,
    )(stk, far_stk, lay(far_data, far_rims), numer, bits_x)
    numer, auto_far = lax.optimization_barrier((numer, auto_far))
    numer_far = swap(numer, "chan", 1)
    grams = [gram]

    mats = sds(((REACH + 1) * width, width), BF16)
    every = list(range(-REACH, REACH + 1))
    high, low, den = call(
        functools.partial(first_conv_body, plan, every),
        (mats, mats, sds((rows, width), F32)),
        vmem(3),
        [pltpu.VMEM((factors, (REACH + 2) * width), F32)],
    )(auto, auto_far, bits_x)

    def conv(offsets, bits_now, before):
        return call(functools.partial(conv_body, plan, offsets), field, vmem(4))(
            bits_now, high, low, before
        )

    def conv_tail(offsets, bits_now):
        return call(
            functools.partial(conv_tail_body, plan, shards, offsets),
            (field, rest),
            vmem(5),
            tail_room,
        )(bits_now, high, low, stk, far_stk)

    scale = PENALTY / (steps * shards)
    numers_now = (numer, numer_far)
    for sweep in range(ITERS):
        if sweep:
            part, tail = conv_tail(every[: REACH - 2], bits_x)
            tails = (tail, swap(tail, "chan", 1))
            den = conv(every[REACH - 2 :], bits_x, part)
            grams = gram_rounds(gram, odd, (part,), (den, tails[1]))
        else:
            tails = ()
        operands = (x, bits_x, low_x, den, *numers_now, *tails, *grams)
        counts = (len(numers_now), len(grams))
        if sweep == ITERS - 1:
            return call(
                functools.partial(last_body, plan, scale, shards, counts),
                sds((factors, steps), F32),
                vmem(len(operands)),
                [pltpu.VMEM((rows, width), F32), pltpu.VMEM((steps + 2 * LANES, LANES), F32)],
            )(*operands)
        outs = (field, window, low_field, sds((factors, factors), F32))
        if counts[0] > 1:
            outs = (field,) + outs
        got = call(
            functools.partial(update_body, plan, scale, shards, counts),
            outs,
            vmem(len(operands)),
            [pltpu.VMEM((rows, width), F32), pltpu.VMEM((rows, 2 * width), BF16)],
        )(*operands)
        if counts[0] > 1:
            numers_now, got = got[:1], got[1:]
        x, bits_x, low_x, gram = got


def solution(mesh):
    in_specs = (P("chan", "tm"), P("chan", "tm"), P(None, "tm"))
    out_specs = P(None, "tm")
    return jax.shard_map(
        on_device, mesh=mesh, in_specs=in_specs, out_specs=out_specs, check_vma=False
    )
```
